128 devices in a mesh: row: 4 (over y), col: 32 (over z, x, core).
Axes of the slice: x: 4, y: 4, z: 4, core: 2. Of those that a mesh axis runs over, the one named last changes fastest.
Arguments:
- gradient: float32 [4096, 16384], P(('row', 'col')), may hold values from -240 to 240
- weights: float32 [4096, 16384], P(('row', 'col')), may hold values from -6 to 6
- momentum: float32 [4096, 16384], P(('row', 'col')), may hold values from -3 to 3
- fresh_momentum: float32 [4096, 16384], P(('row', 'col')), may hold values from -6 to 6
- gaussian_noise: float32 [4096, 16384], P(('row', 'col')), may hold values from -6 to 6
- resample: int32 [4, 16], replicated, may hold values 0 or 1
- step_index: int32 [1], replicated, may hold values from 0 to 2999
Outputs:
- new_weights: float32 [4096, 16384], P(('row', 'col'))
- next_momentum: float32 [4096, 16384], P(('row', 'col'))
The draws below stay inside these ranges and needn't reach their ends.
All inputs are finite; a program needn't handle non-finite values.
Results may differ from the reference program's by a relative error of at most 0.00016.
Values sent between devices are 32-bit elements; how exact they have to be, the bound alone decides.
No kernel may reach another device: no remote copies, remote signals or barrier semaphores. Data moves between devices by JAX's collectives and lax.ppermute only.
A program may use at most 128 MiB of HBM per device.

```python
import math
import jax
import jax.numpy as jnp
from jax import lax

BLOCK = 1024
ITERS = 3
CYCLE = 1000
D = 4096
F = 16384
TILE_ROWS = 4
TILE_COLS = 16


def ladder_scale(key, block_count):
    key_order, key_jitter = jax.random.split(key, 2)
    order_keys = jax.random.split(key_order, block_count)
    ranks = jax.vmap(lambda one_key: jax.random.permutation(one_key, BLOCK))(order_keys)
    ladder = ((ranks.astype(jnp.float32) + 0.5) / BLOCK) ** (-0.3)
    jitter = jnp.exp(jax.random.uniform(key_jitter, (block_count, BLOCK), jnp.float32, math.log(0.8), math.log(1.25)))
    return (ladder * jitter).reshape(block_count * BLOCK)


def draw_gradient(key, part):
    key = jax.random.fold_in(key, 11)
    key_base, key_rows, key_cols = jax.random.split(key, 3)
    row_scale = ladder_scale(key_rows, D // BLOCK)
    col_scale = ladder_scale(key_cols, F // BLOCK)
    base_draw = jnp.clip(jax.random.normal(key_base, (D, F), jnp.float32), -4.0, 4.0)
    return 0.3 * base_draw * row_scale[:, None] * col_scale[None, :]


def place_ends(values, stream_key, low, top_value):
    longest = values.shape.index(max(values.shape))
    spots = []
    for shift in (0, 1):
        where = [jax.random.randint(jax.random.fold_in(stream_key, axis), (), 0, length) for axis, length in enumerate(values.shape)]
        where[longest] = (where[longest] + shift) % values.shape[longest]
        spots.append(tuple(where))
    return values.at[spots[0]].set(low).at[spots[1]].set(top_value)


def block_scale(own_key, shape, cuts, smallest, largest):
    level, own = 1.0, jax.random.fold_in(own_key, 6)
    for dim, parts in cuts:
        heights = jnp.exp(jax.random.uniform(jax.random.fold_in(own, dim), (parts,), jnp.float32, smallest / len(cuts), largest / len(cuts)))
        level = level * jnp.repeat(heights, shape[dim] // parts).reshape([-1 if axis == dim else 1 for axis in range(len(shape))])
    return level


def scatter_about(stream_key, extent, spread, limit, shards=(), held_as=jnp.bfloat16):
    values = jax.random.normal(stream_key, extent, jnp.float32) * spread
    if len(shards) > 0:
        values = block_scale(stream_key, extent, shards, -0.22, 0.18) * values
    return jnp.clip(values, min=-limit, max=limit).astype(held_as)


def setup_inputs(seed: int = 0) -> dict:
    splits = jax.random.split(jax.random.key(seed), 8)
    return {
        "gradient": draw_gradient(jax.random.fold_in(splits[7], 71), 0),
        "weights": scatter_about(splits[1], (D, F), 1.0, 6.0, ((0, 128),), jnp.float32),
        "momentum": scatter_about(splits[2], (D, F), 0.5, 3.0, ((0, 128),), jnp.float32),
        "fresh_momentum": scatter_about(splits[3], (D, F), 1.0, 6.0, ((0, 128),), jnp.float32),
        "gaussian_noise": scatter_about(splits[4], (D, F), 1.0, 6.0, ((0, 128),), jnp.float32),
        "resample": place_ends((jax.random.randint(splits[5], (TILE_ROWS, TILE_COLS), 0, 2) < 1).astype(jnp.int32), jax.random.fold_in(splits[5], 1), 0, 1),
        "step_index": jax.random.randint(splits[6], (1,), 0, 3 * CYCLE).astype(jnp.int32),
    }


full_precision = lax.Precision.HIGHEST
NORM_EPS = 1e-06
BASE_RATE = 0.5
DAMPING_COEFF = 0.1
HEAT_LEVEL = 1.0

def inverse_root(factor):
    matrix_size = factor.shape[0]
    norm_scale = jnp.sqrt(jnp.sum(factor * factor)) + NORM_EPS
    current = factor / norm_scale
    identity = jnp.eye(matrix_size, dtype=jnp.float32)
    root_part = current
    for turn_index in range(ITERS):
        step_matrix = (5.0 * identity - current) * 0.25
        if turn_index == 0:
            root_part = step_matrix
        else:
            root_part = jnp.dot(root_part, step_matrix, precision=full_precision)
        if turn_index + 1 < ITERS:
            for repeat_index in range(4):
                current = jnp.dot(current, step_matrix, precision=full_precision)
    return root_part

def reference(gradient, weights, momentum, fresh_momentum, gaussian_noise, resample, step_index):
    tile_rows = D // BLOCK
    tile_cols = F // BLOCK
    grad_grid = gradient.reshape(tile_rows, BLOCK, F)

    def left_factor(row_block):
        return jnp.dot(row_block, row_block.T, precision=full_precision)
    left_stats = lax.map(left_factor, grad_grid)
    col_blocks = gradient.reshape(D, tile_cols, BLOCK).transpose(1, 0, 2)

    def right_factor(col_block):
        return jnp.dot(col_block.T, col_block, precision=full_precision)
    right_stats = lax.map(right_factor, col_blocks)
    left_roots = lax.map(inverse_root, left_stats)
    right_roots = lax.map(inverse_root, right_stats)

    def precondition(packed_in):
        row_block, left_root = packed_in
        tile_view = row_block.reshape(BLOCK, tile_cols, BLOCK)
        mixed_part = jnp.einsum('atb,tcb->atc', tile_view, right_roots, precision=full_precision)
        return jnp.einsum('xa,atc->xtc', left_root, mixed_part, precision=full_precision).reshape(BLOCK, F)
    descent_direction = lax.map(precondition, (grad_grid, left_roots)).reshape(D, F)
    grad_sq = jnp.sum(gradient * gradient)
    dir_sq = jnp.sum(descent_direction * descent_direction)
    descent_direction = descent_direction * (jnp.sqrt(grad_sq) / (jnp.sqrt(dir_sq) + NORM_EPS))
    cycle_phase = jnp.mod(step_index[0], CYCLE).astype(jnp.float32) / CYCLE
    learning_rate = BASE_RATE * 0.5 * (1.0 + jnp.cos(jnp.pi * cycle_phase))
    flag_full = jnp.broadcast_to(resample[:, None, :, None], (tile_rows, BLOCK, tile_cols, BLOCK)).reshape(D, F)
    prior_momentum = jnp.where(flag_full == 1, jnp.sqrt(learning_rate) * fresh_momentum, momentum)
    next_momentum = (1.0 - DAMPING_COEFF) * prior_momentum - learning_rate * descent_direction + jnp.sqrt(2.0 * DAMPING_COEFF * learning_rate * HEAT_LEVEL) * gaussian_noise
    return (weights + next_momentum, next_momentum)
```

```python
import jax
import jax.numpy as jnp
from jax import lax
from jax.experimental import pallas as pl
from jax.experimental.pallas import tpu as pltpu
from jax.sharding import PartitionSpec as P

BLOCK = 1024
CYCLE = 1000
NORM_EPS = 1e-06
BASE_RATE = 0.5
DAMPING_COEFF = 0.1
HEAT_LEVEL = 1.0

SUB = 256
PARTS = BLOCK // SUB
PAIRS = [(a, b) for b in range(PARTS) for a in range(b + 1)]
PLACE = {pair: k for k, pair in enumerate(PAIRS)}
PACKED = len(PAIRS) * SUB
HALF = PACKED // 2
CORE_COLUMNS = (((0, 0, 1), (1, 0, 2), (2, 0, 2)), ((2, 2, 3), (3, 0, 4)))


def vmem():
    return pl.BlockSpec(memory_space=pltpu.VMEM)


def smem():
    return pl.BlockSpec(memory_space=pltpu.SMEM)


def params():
    return pltpu.CompilerParams(vmem_limit_bytes=50 << 20)


def span(k, size=SUB):
    return slice(k * size, (k + 1) * size)


def split(x):
    high = x.astype(jnp.bfloat16)
    return high, (x - high.astype(jnp.float32)).astype(jnp.bfloat16)


def dot(x, y, dims=((1,), (0,))):
    return lax.dot_general(x, y, (dims, ((), ())), preferred_element_type=jnp.float32)


def dot_split(x, y, dims=((1,), (0,))):
    return dot(x[0], y[0], dims) + dot(x[0], y[1], dims) + dot(x[1], y[0], dims)


def identity():
    rows = lax.broadcasted_iota(jnp.int32, (SUB, SUB), 0)
    cols = lax.broadcasted_iota(jnp.int32, (SUB, SUB), 1)
    return (rows == cols).astype(jnp.float32)


def put(dst, a, b, x):
    high, low = split(x)
    dst[0, span(a), span(b)] = high
    dst[1, span(a), span(b)] = low
    if a != b:
        dst[0, span(b), span(a)] = high.T
        dst[1, span(b), span(a)] = low.T


def get(src, a, b):
    high = src[0, span(a), span(b)].astype(jnp.float32)
    return high + src[1, span(a), span(b)].astype(jnp.float32)


def fold(x):
    total = jnp.sum(x.reshape(x.shape[0] // 8, 8, x.shape[1]), axis=0)
    return sum(total[:, span(k, 128)] for k in range(x.shape[1] // 128))


def gram_kernel(core_ref, own_ref, other_ref, left_ref, right_ref, tile_ref, sq_ref, turned):
    core = core_ref[0]
    own_at = pl.multiple_of(core * (BLOCK // 2), BLOCK // 2)
    other_at = pl.multiple_of((1 - core) * (BLOCK // 2), BLOCK // 2)
    sq_ref[...] = fold(own_ref[...] * own_ref[...])
    for part in range(PARTS):
        for ref, at in ((own_ref, own_at), (other_ref, other_at)):
            high, low = split(ref[span(part), :])
            tile_ref[0, span(part), pl.ds(at, BLOCK // 2)] = high
            tile_ref[1, span(part), pl.ds(at, BLOCK // 2)] = low
            turned[0, pl.ds(at, BLOCK // 2), span(part)] = high.T
            turned[1, pl.ds(at, BLOCK // 2), span(part)] = low.T

    def products(src, dst, columns):
        at = 0
        for col, first, end in columns:
            x = [src[k, first * SUB : end * SUB, :] for k in range(2)]
            y = [src[k, span(col), :] for k in range(2)]
            rows = (end - first) * SUB
            dst[at : at + rows, :] = dot_split(x, y, ((1,), (1,)))
            at += rows

    for which in range(2):

        @pl.when(core == which)
        def _(which=which):
            products(tile_ref, left_ref, CORE_COLUMNS[which])
            products(turned, right_ref, CORE_COLUMNS[which])


def gram(core, own, other):
    f32 = jnp.float32
    return pl.pallas_call(
        gram_kernel,
        out_shape=(
            jax.ShapeDtypeStruct((HALF, SUB), f32),
            jax.ShapeDtypeStruct((HALF, SUB), f32),
            jax.ShapeDtypeStruct((2, BLOCK, BLOCK), jnp.bfloat16),
            jax.ShapeDtypeStruct((8, 128), f32),
        ),
        in_specs=[smem(), vmem(), vmem()],
        out_specs=(vmem(), vmem(), vmem(), vmem()),
        scratch_shapes=[pltpu.VMEM((2, BLOCK, BLOCK), jnp.bfloat16)],
        compiler_params=params(),
        name="gram",
    )(core, own, other)


def multiply(x, y, emit):
    for b in range(PARTS):
        rows = (b + 1) * SUB
        left = [x[k, :rows, :] for k in range(2)]
        right = [y[k, :, span(b)] for k in range(2)]
        z = dot_split(left, right)
        for a in range(b + 1):
            emit(a, b, z[span(a)])


def root_kernel(core_ref, mine_ref, got_ref, out_ref, factor, s, q, d, u, w):
    core = core_ref[0]
    factor[pl.ds(pl.multiple_of(core * HALF, HALF), HALF), :] = mine_ref[...]
    factor[pl.ds(pl.multiple_of((1 - core) * HALF, HALF), HALF), :] = got_ref[...]
    unit = identity()
    squares = jnp.zeros((SUB, SUB), jnp.float32)
    for k, (a, b) in enumerate(PAIRS):
        x = factor[span(k), :]
        squares += x * x * (1.0 if a == b else 2.0)
    scale = 1.0 / (jnp.sqrt(jnp.sum(squares)) + NORM_EPS)

    def shifted(dst, a, b, z):
        z = z * -0.25
        put(dst, a, b, z + 1.25 * unit if a == b else z)

    for k, (a, b) in enumerate(PAIRS):
        shifted(s, a, b, factor[span(k), :] * scale)
    multiply(s, s, lambda a, b, z: put(q, a, b, z))
    multiply(s, q, lambda a, b, z: put(d, a, b, 5.0 * get(q, a, b) - 4.0 * z))
    multiply(d, q, lambda a, b, z: shifted(u, a, b, z))

    def squared(a, b, z):
        put(q, a, b, z)
        put(d, a, b, 5.0 * get(u, a, b) - 4.0 * z)

    multiply(u, u, squared)
    multiply(q, q, lambda a, b, z: put(w, a, b, z))
    multiply(d, w, lambda a, b, z: put(q, a, b, 1.25 * get(u, a, b) - 0.25 * z))

    def result(a, b, z):
        out_ref[span(PLACE[(a, b)]), :] = z

    multiply(s, q, result)


def root(core, mine, got):
    return pl.pallas_call(
        root_kernel,
        out_shape=jax.ShapeDtypeStruct((PACKED, SUB), jnp.float32),
        in_specs=[smem(), vmem(), vmem()],
        out_specs=vmem(),
        scratch_shapes=[pltpu.VMEM((PACKED, SUB), jnp.float32)]
        + [pltpu.VMEM((2, BLOCK, BLOCK), jnp.bfloat16)] * 5,
        compiler_params=params(),
        name="root",
    )(core, mine, got)


def direction_kernel(core_ref, own_ref, other_ref, tile_ref, out_ref, sq_ref, left, right, mixed):
    core = core_ref[0]
    half = BLOCK // 2

    def unpack_left(src):
        for k, (a, b) in enumerate(PAIRS):
            put(left, a, b, src[span(k), :])

    def unpack_right(src, which):
        for a in range(PARTS):
            for b in range(2):
                i, j = a, b + 2 * which
                x = src[span(PLACE[(min(i, j), max(i, j))]), :]
                high, low = split(x)
                right[0, span(a), span(b)] = high if i <= j else high.T
                right[1, span(a), span(b)] = low if i <= j else low.T

    @pl.when(core == 0)
    def _():
        unpack_left(own_ref)
        unpack_right(other_ref, 0)

    @pl.when(core == 1)
    def _():
        unpack_left(other_ref)
        unpack_right(own_ref, 1)

    for a in range(PARTS):
        z = dot_split(
            [tile_ref[k, span(a), :] for k in range(2)], [right[k] for k in range(2)]
        )
        high, low = split(z)
        mixed[0, span(a), :] = high
        mixed[1, span(a), :] = low
    total = jnp.zeros((8, 128), jnp.float32)
    pieces = SUB // out_ref.shape[1]
    for a in range(PARTS):
        z = dot_split([left[k, span(a), :] for k in range(2)], [mixed[k] for k in range(2)])
        total += fold(z * z)
        out_ref[span(a, pieces)] = z.reshape(pieces, out_ref.shape[1], half)
    sq_ref[...] = total


def direction(core, own, other, tile, rows):
    f32, bf16, half = jnp.float32, jnp.bfloat16, BLOCK // 2
    return pl.pallas_call(
        direction_kernel,
        out_shape=(
            jax.ShapeDtypeStruct((BLOCK // rows, rows, half), f32),
            jax.ShapeDtypeStruct((8, 128), f32),
        ),
        in_specs=[smem(), vmem(), vmem(), vmem()],
        out_specs=(vmem(), vmem()),
        scratch_shapes=[
            pltpu.VMEM((2, BLOCK, BLOCK), bf16),
            pltpu.VMEM((2, BLOCK, half), bf16),
            pltpu.VMEM((2, BLOCK, half), bf16),
        ],
        compiler_params=params(),
        name="direction",
    )(core, own, other, tile)


STEP_TILES = 2


def update_kernel(flag_ref, coef_ref, sums_ref, dir_ref, w_ref, m_ref, f_ref, n_ref, ow_ref, om_ref):
    half = BLOCK // 2
    gsq = jnp.sum(sums_ref[:8, :])
    dsq = jnp.sum(sums_ref[8:, :])
    rate, root_rate, heat = coef_ref[0], coef_ref[1], coef_ref[2]
    pull = rate * (jnp.sqrt(gsq) / (jnp.sqrt(dsq) + NORM_EPS))
    for t in range(STEP_TILES):
        flag = flag_ref[pl.program_id(0) * STEP_TILES + t]
        for k in range(2):
            at = span(2 * t + k, half)
            prior = jnp.where(flag == 1, root_rate * f_ref[:, at], m_ref[:, at])
            moved = (1.0 - DAMPING_COEFF) * prior - pull * dir_ref[2 * t + k] + heat * n_ref[:, at]
            om_ref[:, at] = moved
            ow_ref[:, at] = w_ref[:, at] + moved


def update(flags, coefs, sums, row_direction, weights, momentum, fresh, noise):
    rows, cols = weights.shape
    half, width = BLOCK // 2, STEP_TILES * BLOCK
    wide = pl.BlockSpec((rows, width), lambda i: (0, i))
    shape = jax.ShapeDtypeStruct((rows, cols), jnp.float32)
    return pl.pallas_call(
        update_kernel,
        grid=(cols // width,),
        out_shape=(shape, shape),
        in_specs=[
            smem(),
            smem(),
            pl.BlockSpec((16, 128), lambda i: (0, 0)),
            pl.BlockSpec((2 * STEP_TILES, rows, half), lambda i: (i, 0, 0)),
            wide,
            wide,
            wide,
            wide,
        ],
        out_specs=(wide, wide),
        compiler_params=params(),
        name="update",
    )(flags, coefs, sums, row_direction, weights, momentum, fresh, noise)


def swapped(x, axis, flip):
    return lax.ppermute(x, axis, [(i, i ^ flip) for i in range(lax.axis_size(axis))])


def take(x, at, size):
    return lax.dynamic_slice_in_dim(x, at * size, size, 0)


def ring_sum_scatter(x, first, second, keep):
    rows = x.shape[0] // 2
    sent = swapped(take(x, 1 - keep[0], rows), "row", first)
    x = take(x, keep[0], rows) + sent
    rows //= 2
    sent = swapped(take(x, 1 - keep[1], rows), "row", second)
    return take(x, keep[1], rows) + sent


def joined(mine, other, bit):
    return jnp.where(
        bit == 0, jnp.concatenate([mine, other], 0), jnp.concatenate([other, mine], 0)
    )


def ring_gather(x, first, second, keep):
    x = joined(x, swapped(x, "row", second), keep[1])
    return joined(x, swapped(x, "row", first), keep[0])


def everywhere(x):
    size = lax.axis_size("col")
    x = x + swapped(x, "col", 1)
    for axis, step, total in (("col", 2, 4), ("col", 8, 4), ("row", 1, 4)):
        got = [swapped(x, axis, step * k) for k in range(1, total)]
        x = x + got[0] + got[1] + got[2]
    return x


def shards(gradient, weights, momentum, fresh_momentum, gaussian_noise, resample, step_index):
    rows, cols = gradient.shape
    half = BLOCK // 2
    col_pos = lax.axis_index("col")
    row_pos = lax.axis_index("row")
    core = (col_pos % 2).reshape(1).astype(jnp.int32)
    devices = lax.axis_size("col")
    by_core = [[c for c in range(devices) if c % 2 == k] for k in range(2)]

    phase = jnp.mod(step_index[0], CYCLE).astype(jnp.float32) / CYCLE
    rate = BASE_RATE * 0.5 * (1.0 + jnp.cos(jnp.pi * phase))
    coefs = jnp.stack([rate, jnp.sqrt(rate), jnp.sqrt(2.0 * DAMPING_COEFF * rate * HEAT_LEVEL)])
    flags = lax.dynamic_index_in_dim(resample, row_pos, 0, keepdims=False)

    pieces = gradient.reshape(rows, devices, half).transpose(1, 0, 2)
    own = lax.all_to_all(pieces, "col", 0, 0).reshape(BLOCK, half)
    other = swapped(own, "col", 1)
    left, right, tile, grad_sq = gram(core, own, other)

    chips = devices // 2
    shares = lax.all_to_all(
        left.reshape(chips, HALF // chips, SUB), "col", 0, 0, axis_index_groups=by_core
    )
    low, high = row_pos % 2, row_pos // 2
    keeps = ((low ^ high, high), (high, low))
    upper = ring_sum_scatter(right[: HALF // 2], 1, 3, keeps[0])
    lower = ring_sum_scatter(right[HALF // 2 :], 3, 1, keeps[1])
    share = jnp.sum(shares, axis=0)
    left = lax.all_to_all(
        jnp.broadcast_to(share[None], shares.shape), "col", 0, 0, axis_index_groups=by_core
    ).reshape(HALF, SUB)
    upper = ring_gather(upper, 1, 3, keeps[0])
    lower = ring_gather(lower, 3, 1, keeps[1])
    right = jnp.concatenate([upper, lower], 0)

    first = core[0] == 0
    got = swapped(jnp.where(first, right, left), "col", 1)
    own_root = root(core, jnp.where(first, left, right), got)
    other_root = swapped(own_root, "col", 1)
    part, part_sq = direction(core, own_root, other_root, tile, rows)
    row_direction = lax.all_to_all(part, "col", 0, 0)
    sums = everywhere(jnp.concatenate([grad_sq, part_sq], 0))
    return update(
        flags, coefs, sums, row_direction, weights, momentum, fresh_momentum, gaussian_noise
    )


def solution(mesh):
    wide = P(("row", "col"), None)
    in_specs = (wide, wide, wide, wide, wide, P(), P())
    return jax.shard_map(
        shards, mesh=mesh, in_specs=in_specs, out_specs=(wide, wide), check_vma=False
    )
```

```python
import jax
import jax.numpy as jnp
from jax import lax
from jax.experimental import pallas as pl
from jax.experimental.pallas import tpu as pltpu
from jax.sharding import PartitionSpec as P

BLOCK = 1024
CYCLE = 1000
NORM_EPS = 1e-06
BASE_RATE = 0.5
DAMPING_COEFF = 0.1
HEAT_LEVEL = 1.0

SUB = 256
PARTS = BLOCK // SUB
SIDE = BLOCK // 2
FACTOR_PAIRS = (
    ((0, 0), (0, 1), (1, 1), (0, 2), (1, 2)),
    ((2, 2), (2, 3), (3, 3), (3, 0), (3, 1)),
)
ROOT_PAIRS = [(a, b) for b in range(PARTS) for a in range(b + 1)]
PLACE = {pair: k for k, pair in enumerate(ROOT_PAIRS)}
PACKED = len(ROOT_PAIRS) * SUB
HALF = PACKED // 2
LEVEL = 125.0 / 64.0
F32, BF16 = jnp.float32, jnp.bfloat16


def vmem():
    return pl.BlockSpec(memory_space=pltpu.VMEM)


def smem():
    return pl.BlockSpec(memory_space=pltpu.SMEM)


def array(*shape, dtype=F32):
    return jax.ShapeDtypeStruct(shape, dtype)


def whole(kernel, name, outs, ins, scratch=(), limit=16, products=0.0, scalars=1):
    cost = pl.CostEstimate(
        flops=int(products * 6 * BLOCK**3), bytes_accessed=8 << 20, transcendentals=0
    )
    return pl.pallas_call(
        kernel,
        out_shape=outs,
        in_specs=[smem()] * scalars + [vmem() for _ in ins[scalars:]],
        out_specs=jax.tree.map(lambda _: vmem(), outs),
        scratch_shapes=list(scratch),
        compiler_params=pltpu.CompilerParams(vmem_limit_bytes=limit << 20),
        cost_estimate=cost,
        name=name,
    )(*ins)


def span(k, size=SUB):
    return slice(k * size, (k + 1) * size)


def split(x):
    high = x.astype(BF16)
    return high, (x - high.astype(F32)).astype(BF16)


def dot(x, y, dims=((1,), (0,))):
    return lax.dot_general(x, y, (dims, ((), ())), preferred_element_type=F32)


def dot_split(x, y, dims=((1,), (0,))):
    return dot(x[0], y[0], dims) + dot(x[0], y[1], dims) + dot(x[1], y[0], dims)


def both(ref, *at):
    return [ref[(k,) + at] for k in range(2)]


def put(dst, a, b, x):
    high, low = split(x)
    dst[0, span(a), span(b)] = high
    dst[1, span(a), span(b)] = low
    if a != b:
        dst[0, span(b), span(a)] = high.T
        dst[1, span(b), span(a)] = low.T


def get(src, *at):
    return src[(0,) + at].astype(F32) + src[(1,) + at].astype(F32)


def block(src, a, b):
    return get(src, span(a), span(b))


def fold(x):
    total = jnp.sum(x.reshape(x.shape[0] // 8, 8, x.shape[1]), axis=0)
    total = sum(total[:, span(k, 128)] for k in range(x.shape[1] // 128))
    return total[:4] + total[4:]


EVERY = slice(None)


def left_blocks(core, src, emit):
    def rows(first, end, other_first, other_end):
        return dot_split(
            both(src, slice(first * SUB, end * SUB), EVERY),
            both(src, slice(other_first * SUB, other_end * SUB), EVERY),
            ((1,), (1,)),
        )

    @pl.when(core == 0)
    def _():
        emit(0, rows(0, 1, 0, 1))
        emit(1, rows(0, 2, 1, 2))
        emit(3, rows(0, 2, 2, 3))

    @pl.when(core == 1)
    def _():
        emit(0, rows(2, 3, 2, 3))
        emit(1, rows(2, 4, 3, 4))
        z = rows(3, 4, 0, 2)
        emit(3, z[:, span(0)])
        emit(4, z[:, span(1)])


def pair_up(dst, src):
    for part in range(PARTS):
        high, low = split(src[span(part), :])
        dst[0, span(part), :] = high
        dst[1, span(part), :] = low


def turn(dst, src):
    for part in range(PARTS):
        for k in range(2):
            dst[k, :, span(part)] = src[k, span(part), :].T


def own_kernel(core_ref, own_ref, left_ref, sq_ref, pair):
    pair_up(pair, own_ref)
    sq_ref[...] = fold(own_ref[...] * own_ref[...])

    def emit(k, z):
        left_ref[k * SUB : k * SUB + z.shape[0], :] = z

    left_blocks(core_ref[0], pair, emit)


def left_kernel(core_ref, other_ref, part_ref, left_ref, pair):
    pair_up(pair, other_ref)

    def emit(k, z):
        at = slice(k * SUB, k * SUB + z.shape[0])
        left_ref[at, :] = part_ref[at, :] + z

    left_blocks(core_ref[0], pair, emit)


RUN = HALF // 8


def halves(stream, flip):
    def at(pos):
        near, far = (pos ^ flip) % 2, (pos ^ flip) // 2
        return (near ^ far, far) if stream == 0 else (far, near)

    return at


def rows_at(ref, at, size):
    return ref[pl.ds(pl.multiple_of(at, RUN), size), :]


def right_kernel(
    core_ref, ring_ref, own_ref, other_ref, right_ref, first_ref, second_ref, own_pair, other_pair, turned
):
    core, ring = core_ref[0], ring_ref[0]
    pair_up(own_pair, own_ref)
    pair_up(other_pair, other_ref)
    turn(turned, own_pair)
    head = slice(0, SUB)
    right_ref[span(0), :] = dot_split(both(turned, head, EVERY), both(own_pair, EVERY, head))
    right_ref[SUB : 3 * SUB, :] = dot_split(
        both(turned, EVERY, EVERY), both(own_pair, EVERY, span(1))
    )

    @pl.when(core == 0)
    def _():
        right_ref[3 * SUB :, :] = dot_split(
            both(turned, EVERY, EVERY), both(other_pair, EVERY, span(0))
        )

    @pl.when(core == 1)
    def _():
        z = dot_split(both(turned, span(1), EVERY), both(other_pair, EVERY, EVERY))
        right_ref[span(3), :] = z[:, span(0)]
        right_ref[span(4), :] = z[:, span(1)]

    for stream, out in enumerate((first_ref, second_ref)):
        half, _ = halves(stream, 0)(ring)
        out[...] = rows_at(right_ref, (4 * stream + 2 * (1 - half)) * RUN, 2 * RUN)


def halve_kernel(
    ring_ref, right_ref, first_ref, second_ref, kept_ref, first_out_ref, second_out_ref, both_ref
):
    ring = ring_ref[0]
    for stream, (got, out) in enumerate(
        ((first_ref, first_out_ref), (second_ref, second_out_ref))
    ):
        half, quarter = halves(stream, 0)(ring)
        both_ref[...] = rows_at(right_ref, (4 * stream + 2 * half) * RUN, 2 * RUN) + got[...]
        kept_ref[span(stream, RUN), :] = rows_at(both_ref, quarter * RUN, RUN)
        out[...] = rows_at(both_ref, (1 - quarter) * RUN, RUN)


def place_kernel(ring_ref, mine_ref, near_ref, far_ref, over_first_ref, over_second_ref, out_ref):
    ring = ring_ref[0]
    size = RUN
    pieces = (
        (0, (mine_ref, mine_ref)),
        (1, (near_ref, near_ref)),
        (3, (far_ref, far_ref)),
        (2, (over_first_ref, over_second_ref)),
    )
    for flip, refs in pieces:
        for stream, ref in enumerate(refs):
            half, quarter = halves(stream, flip)(ring)
            at = pl.multiple_of((4 * stream + 2 * half + quarter) * size, size)
            out_ref[pl.ds(at, size), :] = ref[span(stream if flip != 2 else 0, size), :]


def spread_kernel(core_ref, shares_ref, out_ref):
    total = shares_ref[0]
    for k in range(1, shares_ref.shape[0]):
        total += shares_ref[k]
    out_ref[...] = jnp.broadcast_to(total[None], out_ref.shape)


def multiply(x, y, emit):
    for a in range(PARTS):
        z = dot_split(both(x, span(a), EVERY), both(y, EVERY, slice(a * SUB, BLOCK)))
        for b in range(a, PARTS):
            emit(a, b, z[:, span(b - a)])


def root_kernel(
    core_ref, left_ref, left_got_ref, right_ref, right_got_ref, out_ref, root_ref,
    factor, m, n, z, y, t,
):
    core = core_ref[0]

    @pl.when(core == 0)
    def _():
        factor[:HALF, :] = left_ref[...]
        factor[HALF:, :] = left_got_ref[...]

    @pl.when(core == 1)
    def _():
        factor[:HALF, :] = right_got_ref[...]
        factor[HALF:, :] = right_ref[...]

    squares = jnp.zeros((SUB, SUB), F32)
    pairs = FACTOR_PAIRS[0] + FACTOR_PAIRS[1]
    for k, (a, b) in enumerate(pairs):
        x = factor[span(k), :]
        squares += x * x * (1.0 if a == b else 2.0)
    scale = 1.0 / (jnp.sqrt(jnp.sum(squares)) + NORM_EPS)
    for k, (a, b) in enumerate(pairs):
        put(m, a, b, factor[span(k), :] * scale)

    multiply(m, m, lambda a, b, p: put(n, a, b, p))

    def cube(a, b, p):
        mm, nn = block(m, a, b), block(n, a, b)
        put(z, a, b, (25.0 * mm - 10.0 * nn + p) * (1.0 / 16.0))
        put(y, a, b, (nn - 10.0 * mm) * (1.0 / 16.0))

    multiply(m, n, cube)
    multiply(z, y, lambda a, b, p: put(t, a, b, (25.0 / 16.0) * block(z, a, b) + p))

    multiply(t, t, lambda a, b, p: put(n, a, b, p))

    def cube_again(a, b, p):
        tt, nn = block(t, a, b), block(n, a, b)
        put(z, a, b, (25.0 * tt - 10.0 * nn + p) * (1.0 / 16.0))
        put(y, a, b, (15.0 * nn - 75.0 * tt - p) * (1.0 / 64.0))

    multiply(t, n, cube_again)

    def last(a, b, p):
        put(n, a, b, -0.3125 * block(t, a, b) - (125.0 / 256.0) * block(z, a, b) - 0.25 * p)

    multiply(z, y, last)

    def result(a, b, p):
        p = 1.25 * block(n, a, b) - (25.0 / 64.0) * block(m, a, b) - 0.25 * p
        out_ref[span(PLACE[(a, b)]), :] = p
        put(root_ref, a, b, p)

    multiply(m, n, result)


def early_kernel(core_ref, root_ref, own_ref, other_ref, out_ref):
    core = core_ref[0]

    def keep(rows, cols, x):
        high, low = split(x)
        out_ref[0, rows, cols] = high
        out_ref[1, rows, cols] = low

    @pl.when(core == 0)
    def _():
        for part in range(PARTS):
            for k, src in enumerate((own_ref, other_ref)):
                x = dot_split(both(root_ref, span(part), EVERY), both(src, EVERY, EVERY))
                keep(span(part), span(k, SIDE), x + LEVEL * get(src, span(part), EVERY))

    @pl.when(core == 1)
    def _():
        for part in range(PARTS):
            at = span(part)
            x = dot_split(both(other_ref, at, EVERY), both(root_ref, span(0, SIDE), span(1, SIDE)))
            x += dot_split(both(own_ref, at, EVERY), both(root_ref, span(1, SIDE), span(1, SIDE)))
            keep(at, span(0, SIDE), x + LEVEL * get(own_ref, at, EVERY))


LANES = 128


def late_kernel(core_ref, early_ref, got_ref, sq_ref, out_ref, left, right):
    core = core_ref[0]
    rows = BLOCK // out_ref.shape[0]
    lanes = SIDE // LANES
    count = SUB // rows

    def finish(product):
        total = jnp.zeros((4, LANES), F32)
        for part in range(PARTS):
            x = product(span(part)) + LEVEL * get(early_ref, span(part), span(0, SIDE))
            total += fold(x * x)
            for lane in range(lanes):
                out_ref[span(part, count), span(lane, rows), :] = x[:, span(lane, LANES)].reshape(
                    count, rows, LANES
                )
        stats = jnp.concatenate([sq_ref[...], total], 0)
        out_ref[:, lanes * rows :, :] = jnp.broadcast_to(
            stats[None], (out_ref.shape[0],) + stats.shape
        )

    @pl.when(core == 0)
    def _():
        for a in range(PARTS):
            for b in range(2):
                x = got_ref[span(PLACE[(min(a, b), max(a, b))]), :]
                high, low = split(x)
                right[0, span(a), span(b)] = high if a <= b else high.T
                right[1, span(a), span(b)] = low if a <= b else low.T
        finish(lambda at: dot_split(both(early_ref, at, EVERY), both(right, EVERY, EVERY)))

    @pl.when(core == 1)
    def _():
        for k, (a, b) in enumerate(ROOT_PAIRS):
            put(left, a, b, got_ref[span(k), :])
        finish(
            lambda at: dot_split(both(left, at, EVERY), both(early_ref, EVERY, span(0, SIDE)))
        )


STEP_TILES = 2


def base_kernel(flag_ref, coef_ref, m_ref, f_ref, n_ref, out_ref):
    for t in range(STEP_TILES):
        at = span(t, BLOCK)
        flag = flag_ref[pl.program_id(0) * STEP_TILES + t]
        prior = jnp.where(flag == 1, coef_ref[1] * f_ref[:, at], m_ref[:, at])
        out_ref[:, at] = (1.0 - DAMPING_COEFF) * prior + coef_ref[2] * n_ref[:, at]


def update_kernel(coef_ref, sums_ref, dir_ref, w_ref, b_ref, ow_ref, om_ref):
    gsq = jnp.sum(sums_ref[:4, :])
    dsq = jnp.sum(sums_ref[4:, :])
    pull = coef_ref[0] * (jnp.sqrt(gsq) / (jnp.sqrt(dsq) + NORM_EPS))
    rows = w_ref.shape[0]
    lanes = SIDE // LANES
    for k in range(dir_ref.shape[0]):
        for lane in range(lanes):
            at = span(k * lanes + lane, LANES)
            moved = b_ref[:, at] - pull * dir_ref[k, span(lane, rows), :]
            om_ref[:, at] = moved
            ow_ref[:, at] = w_ref[:, at] + moved


def stream(kernel, name, shape, ins, specs, outs):
    rows, cols = shape
    width = STEP_TILES * BLOCK
    wide = pl.BlockSpec((rows, width), lambda i: (0, i))
    cost = pl.CostEstimate(
        flops=4 * rows * cols, bytes_accessed=(len(ins) + outs) * 4 * rows * cols, transcendentals=0
    )
    return pl.pallas_call(
        kernel,
        grid=(cols // width,),
        out_shape=tuple(array(*shape) for _ in range(outs)),
        in_specs=specs + [wide] * (len(ins) - len(specs)),
        out_specs=(wide,) * outs,
        compiler_params=pltpu.CompilerParams(vmem_limit_bytes=16 << 20),
        cost_estimate=cost,
        name=name,
    )(*ins)


def swapped(x, axis, flip):
    return lax.ppermute(x, axis, [(i, i ^ flip) for i in range(lax.axis_size(axis))])


def shards(gradient, weights, momentum, fresh_momentum, gaussian_noise, resample, step_index):
    rows, cols = gradient.shape
    col_pos = lax.axis_index("col")
    row_pos = lax.axis_index("row")
    core = (col_pos % 2).reshape(1).astype(jnp.int32)
    devices = lax.axis_size("col")
    by_core = [[c for c in range(devices) if c % 2 == k] for k in range(2)]

    phase = jnp.mod(step_index[0], CYCLE).astype(F32) / CYCLE
    rate = BASE_RATE * 0.5 * (1.0 + jnp.cos(jnp.pi * phase))
    coefs = jnp.stack([rate, jnp.sqrt(rate), jnp.sqrt(2.0 * DAMPING_COEFF * rate * HEAT_LEVEL)])
    flags = lax.dynamic_index_in_dim(resample, row_pos, 0, keepdims=False)
    pieces = gradient.reshape(rows, devices, SIDE).transpose(1, 0, 2)
    pieces, momentum, fresh_momentum, gaussian_noise = lax.optimization_barrier(
        (pieces, momentum, fresh_momentum, gaussian_noise)
    )
    (base,) = stream(
        base_kernel,
        "base",
        (rows, cols),
        (flags, coefs, momentum, fresh_momentum, gaussian_noise),
        [smem(), smem()],
        1,
    )

    own = lax.all_to_all(pieces, "col", 0, 0).reshape(BLOCK, SIDE)
    own, base = lax.optimization_barrier((own, base))
    other = swapped(own, "col", 1)
    pair = array(2, BLOCK, SIDE, dtype=BF16)
    pair_space = pltpu.VMEM((2, BLOCK, SIDE), BF16)
    left, grad_sq = whole(
        own_kernel,
        "own",
        (array(HALF, SUB), array(4, LANES)),
        (core, own),
        [pair_space],
        products=0.16,
    )
    left = whole(
        left_kernel, "left", array(HALF, SUB), (core, other, left), [pair_space], products=0.16
    )
    chips = devices // 2
    shares = lax.all_to_all(
        left.reshape(chips, HALF // chips, SUB), "col", 0, 0, axis_index_groups=by_core
    )

    ring = row_pos.reshape(1).astype(jnp.int32)
    two, one = array(2 * RUN, SUB), array(RUN, SUB)
    right, to_first, to_second, own_pair, other_pair = whole(
        right_kernel,
        "right",
        (array(HALF, SUB), two, two, pair, pair),
        (core, ring, own, other),
        [pltpu.VMEM((2, SIDE, BLOCK), BF16)],
        products=0.3,
        scalars=2,
    )
    got = swapped(to_first, "row", 1), swapped(to_second, "row", 3)
    kept, to_first, to_second = whole(
        halve_kernel, "halve", (two, one, one), (ring, right) + got, [pltpu.VMEM((2 * RUN, SUB), F32)]
    )
    got = swapped(to_first, "row", 3), swapped(to_second, "row", 1)
    mine = kept + jnp.concatenate(got, 0)

    share = whole(spread_kernel, "spread", array(*shares.shape), (core, shares))
    left = lax.all_to_all(share, "col", 0, 0, axis_index_groups=by_core).reshape(HALF, SUB)
    near, far = swapped(mine, "row", 1), swapped(mine, "row", 3)
    over = swapped(far[:RUN], "row", 1), swapped(near[RUN:], "row", 3)
    right = whole(place_kernel, "place", array(HALF, SUB), (ring, mine, near, far) + over)

    right_got = lax.ppermute(right, "col", [(i, i + 1) for i in range(0, devices, 2)])
    left_got = lax.ppermute(left, "col", [(i + 1, i) for i in range(0, devices, 2)])
    packed, root = whole(
        root_kernel,
        "root",
        (array(PACKED, SUB), array(2, BLOCK, BLOCK, dtype=BF16)),
        (core, left, left_got, right, right_got),
        [pltpu.VMEM((PACKED, SUB), F32)] + [pltpu.VMEM((2, BLOCK, BLOCK), BF16)] * 5,
        limit=30,
        products=7 * 0.625,
    )
    other_root = swapped(packed, "col", 1)
    early = whole(
        early_kernel,
        "early",
        array(2, BLOCK, BLOCK, dtype=BF16),
        (core, root, own_pair, other_pair),
        products=1.0,
    )
    message = whole(
        late_kernel,
        "late",
        array(devices, rows * SIDE // LANES + 8, LANES),
        (core, early, other_root, grad_sq),
        [pltpu.VMEM((2, BLOCK, BLOCK), BF16), pltpu.VMEM((2, BLOCK, SIDE), BF16)],
        products=0.5,
    )
    message = lax.all_to_all(message, "col", 0, 0)
    sums = jnp.sum(message[:, -8:, :], axis=0)
    total = lax.axis_size("row")
    got = [
        lax.ppermute(sums, "row", [(i, (i + k) % total) for i in range(total)])
        for k in range(1, total)
    ]
    sums = sums + sum(got)
    return stream(
        update_kernel,
        "update",
        (rows, cols),
        (coefs, sums, message, weights, base),
        [
            smem(),
            pl.BlockSpec((8, LANES), lambda i: (0, 0)),
            pl.BlockSpec((2 * STEP_TILES, message.shape[1], LANES), lambda i: (i, 0, 0)),
        ],
        2,
    )


def solution(mesh):
    wide = P(("row", "col"), None)
    in_specs = (wide, wide, wide, wide, wide, P(), P())
    return jax.shard_map(
        shards, mesh=mesh, in_specs=in_specs, out_specs=(wide, wide), check_vma=False
    )
```

```python
import jax
import jax.numpy as jnp
from jax import lax
from jax.experimental import pallas as pl
from jax.experimental.pallas import tpu as pltpu
from jax.sharding import PartitionSpec as P

BLOCK = 1024
CYCLE = 1000
NORM_EPS = 1e-06
BASE_RATE = 0.5
DAMPING_COEFF = 0.1
HEAT_LEVEL = 1.0

SUB = 256
QUARTER = SUB // 2
PARTS = BLOCK // SUB
SIDE = BLOCK // 2
DIAGONAL = ((0, 1), (2, 3))
OTHERS = (((0, 1), (0, 2), (1, 2)), ((2, 3), (3, 0), (3, 1)))
HALF = 3 * QUARTER + 3 * SUB
ROOT_PAIRS = [(a, b) for b in range(PARTS) for a in range(b + 1)]
PLACE = {pair: k for k, pair in enumerate(ROOT_PAIRS)}
PACKED = len(ROOT_PAIRS) * SUB
LEVEL = 125.0 / 64.0
F32, BF16 = jnp.float32, jnp.bfloat16


def vmem():
    return pl.BlockSpec(memory_space=pltpu.VMEM)


def smem():
    return pl.BlockSpec(memory_space=pltpu.SMEM)


def array(*shape, dtype=F32):
    return jax.ShapeDtypeStruct(shape, dtype)


def whole(kernel, name, outs, ins, scratch=(), limit=16, products=0.0, scalars=1):
    cost = pl.CostEstimate(
        flops=int(products * 6 * BLOCK**3), bytes_accessed=8 << 20, transcendentals=0
    )
    return pl.pallas_call(
        kernel,
        out_shape=outs,
        in_specs=[smem()] * scalars + [vmem() for _ in ins[scalars:]],
        out_specs=jax.tree.map(lambda _: vmem(), outs),
        scratch_shapes=list(scratch),
        compiler_params=pltpu.CompilerParams(vmem_limit_bytes=limit << 20),
        cost_estimate=cost,
        name=name,
    )(*ins)


def span(k, size=SUB):
    return slice(k * size, (k + 1) * size)


def split(x):
    high = x.astype(BF16)
    return high, (x - high.astype(F32)).astype(BF16)


def dot(x, y, dims=((1,), (0,))):
    return lax.dot_general(x, y, (dims, ((), ())), preferred_element_type=F32)


def dot_split(x, y, dims=((1,), (0,))):
    return dot(x[0], y[0], dims) + dot(x[0], y[1], dims) + dot(x[1], y[0], dims)


def both(ref, *at):
    return [ref[(k,) + at] for k in range(2)]


def put(dst, a, b, x):
    high, low = split(x)
    dst[0, span(a), span(b)] = high
    dst[1, span(a), span(b)] = low
    if a != b:
        dst[0, span(b), span(a)] = high.T
        dst[1, span(b), span(a)] = low.T


def get(src, *at):
    return src[(0,) + at].astype(F32) + src[(1,) + at].astype(F32)


def block(src, a, b):
    return get(src, span(a), span(b))


def fold(x):
    total = jnp.sum(x.reshape(x.shape[0] // 8, 8, x.shape[1]), axis=0)
    total = sum(total[:, span(k, 128)] for k in range(x.shape[1] // 128))
    return total[:4] + total[4:]


EVERY = slice(None)


def store_diagonal(dst, k, x, part=None):
    pieces = (
        (span(k, QUARTER), EVERY, x[:QUARTER, :]),
        (span(2, QUARTER), span(k, QUARTER), x[QUARTER:, QUARTER:]),
    )
    for rows, cols, piece in pieces:
        dst[rows, cols] = piece if part is None else part[rows, cols] + piece


def store_other(dst, k, x, part=None):
    start = 3 * QUARTER + k * SUB
    rows = slice(start, start + x.shape[0])
    dst[rows, :] = x if part is None else part[rows, :] + x


def load_half(src, at, which):
    for k, a in enumerate(DIAGONAL[which]):
        top = src[at + k * QUARTER : at + (k + 1) * QUARTER, :]
        corner = src[at + 2 * QUARTER : at + 3 * QUARTER, span(k, QUARTER)]
        bottom = jnp.concatenate([top[:, QUARTER:].T, corner], 1)
        yield a, a, jnp.concatenate([top, bottom], 0)
    for k, (a, b) in enumerate(OTHERS[which]):
        start = at + 3 * QUARTER + k * SUB
        yield a, b, src[start : start + SUB, :]


def left_blocks(core, src, dst, part=None):
    def rows(first, end, other_first, other_end):
        return dot_split(
            both(src, slice(first * SUB, end * SUB), EVERY),
            both(src, slice(other_first * SUB, other_end * SUB), EVERY),
            ((1,), (1,)),
        )

    @pl.when(core == 0)
    def _():
        store_diagonal(dst, 0, rows(0, 1, 0, 1), part)
        z = rows(0, 2, 1, 2)
        store_other(dst, 0, z[:SUB], part)
        store_diagonal(dst, 1, z[SUB:], part)
        store_other(dst, 1, rows(0, 2, 2, 3), part)

    @pl.when(core == 1)
    def _():
        store_diagonal(dst, 0, rows(2, 3, 2, 3), part)
        z = rows(2, 4, 3, 4)
        store_other(dst, 0, z[:SUB], part)
        store_diagonal(dst, 1, z[SUB:], part)
        z = rows(3, 4, 0, 2)
        store_other(dst, 1, z[:, span(0)], part)
        store_other(dst, 2, z[:, span(1)], part)


def pair_up(dst, src):
    for part in range(PARTS):
        high, low = split(src[span(part), :])
        dst[0, span(part), :] = high
        dst[1, span(part), :] = low


def turn(dst, src):
    for part in range(PARTS):
        for k in range(2):
            dst[k, :, span(part)] = src[k, span(part), :].T


def own_kernel(core_ref, own_ref, left_ref, pair):
    pair_up(pair, own_ref)
    left_blocks(core_ref[0], pair, left_ref)


def left_kernel(core_ref, other_ref, part_ref, left_ref, sq_ref, pair):
    pair_up(pair, other_ref)
    left_blocks(core_ref[0], pair, left_ref, part_ref)
    sq_ref[...] = fold(other_ref[...] * other_ref[...])


RUN = HALF // 8


def halves(stream, flip):
    def at(pos):
        near, far = (pos ^ flip) % 2, (pos ^ flip) // 2
        return (near ^ far, far) if stream == 0 else (far, near)

    return at


def rows_at(ref, at, size):
    return ref[pl.ds(pl.multiple_of(at, RUN), size), :]


def right_kernel(
    core_ref, ring_ref, own_ref, other_ref, after_ref,
    right_ref, first_ref, second_ref, own_pair, other_pair, turned,
):
    core, ring = core_ref[0], ring_ref[0]
    pair_up(own_pair, own_ref)
    pair_up(other_pair, other_ref)
    turn(turned, own_pair)
    head = slice(0, SUB)
    store_diagonal(
        right_ref, 0, dot_split(both(turned, head, EVERY), both(own_pair, EVERY, head))
    )
    z = dot_split(both(turned, EVERY, EVERY), both(own_pair, EVERY, span(1)))
    store_other(right_ref, 0, z[:SUB])
    store_diagonal(right_ref, 1, z[SUB:])

    @pl.when(core == 0)
    def _():
        z = dot_split(both(turned, EVERY, EVERY), both(other_pair, EVERY, span(0)))
        store_other(right_ref, 1, z)

    @pl.when(core == 1)
    def _():
        z = dot_split(both(turned, span(1), EVERY), both(other_pair, EVERY, EVERY))
        store_other(right_ref, 1, z[:, span(0)])
        store_other(right_ref, 2, z[:, span(1)])

    for stream, out in enumerate((first_ref, second_ref)):
        half, _ = halves(stream, 0)(ring)
        out[...] = rows_at(right_ref, (4 * stream + 2 * (1 - half)) * RUN, 2 * RUN)


def halve_kernel(
    ring_ref, right_ref, first_ref, second_ref, kept_ref, first_out_ref, second_out_ref, both_ref
):
    ring = ring_ref[0]
    for stream, (got, out) in enumerate(
        ((first_ref, first_out_ref), (second_ref, second_out_ref))
    ):
        half, quarter = halves(stream, 0)(ring)
        both_ref[...] = rows_at(right_ref, (4 * stream + 2 * half) * RUN, 2 * RUN) + got[...]
        kept_ref[span(stream, RUN), :] = rows_at(both_ref, quarter * RUN, RUN)
        out[...] = rows_at(both_ref, (1 - quarter) * RUN, RUN)


def place_kernel(ring_ref, mine_ref, near_ref, far_ref, over_first_ref, over_second_ref, out_ref):
    ring = ring_ref[0]
    size = RUN
    pieces = (
        (0, (mine_ref, mine_ref)),
        (1, (near_ref, near_ref)),
        (3, (far_ref, far_ref)),
        (2, (over_first_ref, over_second_ref)),
    )
    for flip, refs in pieces:
        for stream, ref in enumerate(refs):
            half, quarter = halves(stream, flip)(ring)
            at = pl.multiple_of((4 * stream + 2 * half + quarter) * size, size)
            out_ref[pl.ds(at, size), :] = ref[span(stream if flip != 2 else 0, size), :]


def spread_kernel(core_ref, shares_ref, kept_ref, first_ref, second_ref, out_ref, mine_ref):
    total = shares_ref[0]
    for k in range(1, shares_ref.shape[0]):
        total += shares_ref[k]
    out_ref[...] = jnp.broadcast_to(total[None], out_ref.shape)
    mine_ref[span(0, RUN), :] = kept_ref[span(0, RUN), :] + first_ref[...]
    mine_ref[span(1, RUN), :] = kept_ref[span(1, RUN), :] + second_ref[...]


def multiply(x, y, emit):
    for a in range(PARTS):
        z = dot_split(both(x, span(a), EVERY), both(y, EVERY, slice(a * SUB, BLOCK)))
        for b in range(a, PARTS):
            emit(a, b, z[:, span(b - a)])


def root_kernel(
    core_ref, left_ref, left_got_ref, right_ref, right_got_ref, out_ref, root_ref,
    factor, m, n, z, y, t,
):
    core = core_ref[0]

    @pl.when(core == 0)
    def _():
        factor[:HALF, :] = left_ref[...]
        factor[HALF:, :] = left_got_ref[...]

    @pl.when(core == 1)
    def _():
        factor[:HALF, :] = right_got_ref[...]
        factor[HALF:, :] = right_ref[...]

    def blocks():
        for which in range(2):
            yield from load_half(factor, which * HALF, which)

    squares = jnp.zeros((SUB, SUB), F32)
    for a, b, x in blocks():
        squares += x * x * (1.0 if a == b else 2.0)
    scale = 1.0 / (jnp.sqrt(jnp.sum(squares)) + NORM_EPS)
    for a, b, x in blocks():
        put(m, a, b, x * scale)

    multiply(m, m, lambda a, b, p: put(n, a, b, p))

    def cube(a, b, p):
        mm, nn = block(m, a, b), block(n, a, b)
        put(z, a, b, (25.0 * mm - 10.0 * nn + p) * (1.0 / 16.0))
        put(y, a, b, (nn - 10.0 * mm) * (1.0 / 16.0))

    multiply(m, n, cube)
    multiply(z, y, lambda a, b, p: put(t, a, b, (25.0 / 16.0) * block(z, a, b) + p))

    multiply(t, t, lambda a, b, p: put(n, a, b, p))

    def cube_again(a, b, p):
        tt, nn = block(t, a, b), block(n, a, b)
        put(z, a, b, (25.0 * tt - 10.0 * nn + p) * (1.0 / 16.0))
        put(y, a, b, (15.0 * nn - 75.0 * tt - p) * (1.0 / 64.0))

    multiply(t, n, cube_again)

    def last(a, b, p):
        put(n, a, b, -0.3125 * block(t, a, b) - (125.0 / 256.0) * block(z, a, b) - 0.25 * p)

    multiply(z, y, last)

    def result(a, b, p):
        p = 1.25 * block(n, a, b) - (25.0 / 64.0) * block(m, a, b) - 0.25 * p
        out_ref[span(PLACE[(a, b)]), :] = p
        put(root_ref, a, b, p)

    multiply(m, n, result)


def early_kernel(core_ref, root_ref, own_ref, other_ref, out_ref):
    core = core_ref[0]

    def keep(rows, cols, x):
        high, low = split(x)
        out_ref[0, rows, cols] = high
        out_ref[1, rows, cols] = low

    @pl.when(core == 0)
    def _():
        for part in range(PARTS):
            for k, src in enumerate((own_ref, other_ref)):
                x = dot_split(both(root_ref, span(part), EVERY), both(src, EVERY, EVERY))
                keep(span(part), span(k, SIDE), x + LEVEL * get(src, span(part), EVERY))

    @pl.when(core == 1)
    def _():
        for part in range(PARTS):
            at = span(part)
            x = dot_split(both(other_ref, at, EVERY), both(root_ref, span(0, SIDE), span(1, SIDE)))
            x += dot_split(both(own_ref, at, EVERY), both(root_ref, span(1, SIDE), span(1, SIDE)))
            keep(at, span(0, SIDE), x + LEVEL * get(own_ref, at, EVERY))


LANES = 128


def late_kernel(core_ref, early_ref, got_ref, sq_ref, out_ref, left, right):
    core = core_ref[0]
    rows = BLOCK // out_ref.shape[0]
    lanes = SIDE // LANES
    count = SUB // rows

    def finish(product):
        total = jnp.zeros((4, LANES), F32)
        for part in range(PARTS):
            x = product(span(part)) + LEVEL * get(early_ref, span(part), span(0, SIDE))
            total += fold(x * x)
            for lane in range(lanes):
                out_ref[span(part, count), span(lane, rows), :] = x[:, span(lane, LANES)].reshape(
                    count, rows, LANES
                )
        stats = jnp.concatenate([sq_ref[...], total], 0)
        out_ref[:, lanes * rows :, :] = jnp.broadcast_to(
            stats[None], (out_ref.shape[0],) + stats.shape
        )

    @pl.when(core == 0)
    def _():
        for a in range(PARTS):
            for b in range(2):
                x = got_ref[span(PLACE[(min(a, b), max(a, b))]), :]
                high, low = split(x)
                right[0, span(a), span(b)] = high if a <= b else high.T
                right[1, span(a), span(b)] = low if a <= b else low.T
        finish(lambda at: dot_split(both(early_ref, at, EVERY), both(right, EVERY, EVERY)))

    @pl.when(core == 1)
    def _():
        for k, (a, b) in enumerate(ROOT_PAIRS):
            put(left, a, b, got_ref[span(k), :])
        finish(
            lambda at: dot_split(both(left, at, EVERY), both(early_ref, EVERY, span(0, SIDE)))
        )


STEP_TILES = 2


def base_kernel(flag_ref, coef_ref, m_ref, f_ref, n_ref, out_ref):
    for t in range(STEP_TILES):
        at = span(t, BLOCK)
        flag = flag_ref[pl.program_id(0) * STEP_TILES + t]
        prior = jnp.where(flag == 1, coef_ref[1] * f_ref[:, at], m_ref[:, at])
        out_ref[:, at] = (1.0 - DAMPING_COEFF) * prior + coef_ref[2] * n_ref[:, at]


def update_kernel(coef_ref, sums_ref, dir_ref, w_ref, b_ref, ow_ref, om_ref):
    gsq = jnp.sum(sums_ref[:4, :])
    dsq = jnp.sum(sums_ref[4:, :])
    pull = coef_ref[0] * (jnp.sqrt(gsq) / (jnp.sqrt(dsq) + NORM_EPS))
    rows = w_ref.shape[0]
    lanes = SIDE // LANES
    for k in range(dir_ref.shape[0]):
        for lane in range(lanes):
            at = span(k * lanes + lane, LANES)
            moved = b_ref[:, at] - pull * dir_ref[k, span(lane, rows), :]
            om_ref[:, at] = moved
            ow_ref[:, at] = w_ref[:, at] + moved


def stream(kernel, name, shape, ins, specs, outs):
    rows, cols = shape
    width = STEP_TILES * BLOCK
    wide = pl.BlockSpec((rows, width), lambda i: (0, i))
    cost = pl.CostEstimate(
        flops=4 * rows * cols, bytes_accessed=(len(ins) + outs) * 4 * rows * cols, transcendentals=0
    )
    return pl.pallas_call(
        kernel,
        grid=(cols // width,),
        out_shape=tuple(array(*shape) for _ in range(outs)),
        in_specs=specs + [wide] * (len(ins) - len(specs)),
        out_specs=(wide,) * outs,
        compiler_params=pltpu.CompilerParams(vmem_limit_bytes=16 << 20),
        cost_estimate=cost,
        name=name,
    )(*ins)


def swapped(x, axis, flip):
    return lax.ppermute(x, axis, [(i, i ^ flip) for i in range(lax.axis_size(axis))])


def shards(gradient, weights, momentum, fresh_momentum, gaussian_noise, resample, step_index):
    rows, cols = gradient.shape
    col_pos = lax.axis_index("col")
    row_pos = lax.axis_index("row")
    core = (col_pos % 2).reshape(1).astype(jnp.int32)
    devices = lax.axis_size("col")
    by_core = [[c for c in range(devices) if c % 2 == k] for k in range(2)]

    phase = jnp.mod(step_index[0], CYCLE).astype(F32) / CYCLE
    rate = BASE_RATE * 0.5 * (1.0 + jnp.cos(jnp.pi * phase))
    coefs = jnp.stack([rate, jnp.sqrt(rate), jnp.sqrt(2.0 * DAMPING_COEFF * rate * HEAT_LEVEL)])
    flags = lax.dynamic_index_in_dim(resample, row_pos, 0, keepdims=False)
    pieces = gradient.reshape(rows, devices, SIDE).transpose(1, 0, 2)
    pieces, momentum, fresh_momentum, gaussian_noise = lax.optimization_barrier(
        (pieces, momentum, fresh_momentum, gaussian_noise)
    )
    (base,) = stream(
        base_kernel,
        "base",
        (rows, cols),
        (flags, coefs, momentum, fresh_momentum, gaussian_noise),
        [smem(), smem()],
        1,
    )

    own = lax.all_to_all(pieces, "col", 0, 0).reshape(BLOCK, SIDE)
    own, base = lax.optimization_barrier((own, base))
    other = swapped(own, "col", 1)
    pair = array(2, BLOCK, SIDE, dtype=BF16)
    pair_space = pltpu.VMEM((2, BLOCK, SIDE), BF16)
    left = whole(own_kernel, "own", array(HALF, SUB), (core, own), [pair_space], products=0.16)
    left, grad_sq = whole(
        left_kernel,
        "left",
        (array(HALF, SUB), array(4, LANES)),
        (core, other, left),
        [pair_space],
        products=0.16,
    )
    chips = devices // 2
    shares = lax.all_to_all(
        left.reshape(chips, HALF // chips, SUB), "col", 0, 0, axis_index_groups=by_core
    )

    ring = row_pos.reshape(1).astype(jnp.int32)
    two, one = array(2 * RUN, SUB), array(RUN, SUB)
    right, to_first, to_second, own_pair, other_pair = whole(
        right_kernel,
        "right",
        (array(HALF, SUB), two, two, pair, pair),
        (core, ring, own, other, grad_sq),
        [pltpu.VMEM((2, SIDE, BLOCK), BF16)],
        products=0.3,
        scalars=2,
    )
    got = swapped(to_first, "row", 1), swapped(to_second, "row", 3)
    kept, to_first, to_second = whole(
        halve_kernel, "halve", (two, one, one), (ring, right) + got, [pltpu.VMEM((2 * RUN, SUB), F32)]
    )
    got = swapped(to_first, "row", 3), swapped(to_second, "row", 1)
    share, mine = whole(
        spread_kernel, "spread", (array(*shares.shape), two), (core, shares, kept) + got
    )
    left = lax.all_to_all(share, "col", 0, 0, axis_index_groups=by_core).reshape(HALF, SUB)
    near, far = swapped(mine, "row", 1), swapped(mine, "row", 3)
    over = swapped(far[:RUN], "row", 1), swapped(near[RUN:], "row", 3)
    right = whole(place_kernel, "place", array(HALF, SUB), (ring, mine, near, far) + over)

    right_got = lax.ppermute(right, "col", [(i, i + 1) for i in range(0, devices, 2)])
    left_got = lax.ppermute(left, "col", [(i + 1, i) for i in range(0, devices, 2)])
    packed, root = whole(
        root_kernel,
        "root",
        (array(PACKED, SUB), array(2, BLOCK, BLOCK, dtype=BF16)),
        (core, left, left_got, right, right_got),
        [pltpu.VMEM((2 * HALF, SUB), F32)] + [pltpu.VMEM((2, BLOCK, BLOCK), BF16)] * 5,
        limit=30,
        products=7 * 0.625,
    )
    other_root = swapped(packed, "col", 1)
    early = whole(
        early_kernel,
        "early",
        array(2, BLOCK, BLOCK, dtype=BF16),
        (core, root, own_pair, other_pair),
        products=1.0,
    )
    message = whole(
        late_kernel,
        "late",
        array(devices, rows * SIDE // LANES + 8, LANES),
        (core, early, other_root, grad_sq),
        [pltpu.VMEM((2, BLOCK, BLOCK), BF16), pltpu.VMEM((2, BLOCK, SIDE), BF16)],
        products=0.5,
    )
    message = lax.all_to_all(message, "col", 0, 0)
    sums = jnp.sum(message[:, -8:, :], axis=0)
    total = lax.axis_size("row")
    got = [
        lax.ppermute(sums, "row", [(i, (i + k) % total) for i in range(total)])
        for k in range(1, total)
    ]
    sums = sums + sum(got)
    return stream(
        update_kernel,
        "update",
        (rows, cols),
        (coefs, sums, message, weights, base),
        [
            smem(),
            pl.BlockSpec((8, LANES), lambda i: (0, 0)),
            pl.BlockSpec((2 * STEP_TILES, message.shape[1], LANES), lambda i: (i, 0, 0)),
        ],
        2,
    )


def solution(mesh):
    wide = P(("row", "col"), None)
    in_specs = (wide, wide, wide, wide, wide, P(), P())
    return jax.shard_map(
        shards, mesh=mesh, in_specs=in_specs, out_specs=(wide, wide), check_vma=False
    )
```

```python
import jax
import jax.numpy as jnp
from jax import lax
from jax.experimental import pallas as pl
from jax.experimental.pallas import tpu as pltpu
from jax.sharding import PartitionSpec as P

BLOCK = 1024
CYCLE = 1000
NORM_EPS = 1e-06
BASE_RATE = 0.5
DAMPING_COEFF = 0.1
HEAT_LEVEL = 1.0

SUB = 256
QUARTER = SUB // 2
PARTS = BLOCK // SUB
SIDE = BLOCK // 2
DIAGONAL = ((0, 1), (2, 3))
OTHERS = (((0, 1), (0, 2), (1, 2)), ((2, 3), (3, 0), (3, 1)))
HALF = 3 * QUARTER + 3 * SUB
ROOT_PAIRS = [(a, b) for b in range(PARTS) for a in range(b + 1)]
PLACE = {pair: k for k, pair in enumerate(ROOT_PAIRS)}
PACKED = len(ROOT_PAIRS) * SUB
LEVEL = 125.0 / 64.0
F32, BF16 = jnp.float32, jnp.bfloat16


def vmem():
    return pl.BlockSpec(memory_space=pltpu.VMEM)


def smem():
    return pl.BlockSpec(memory_space=pltpu.SMEM)


def array(*shape, dtype=F32):
    return jax.ShapeDtypeStruct(shape, dtype)


def whole(kernel, name, outs, ins, scratch=(), limit=16, products=0.0, scalars=1, far=()):
    cost = pl.CostEstimate(
        flops=int(products * 6 * BLOCK**3), bytes_accessed=8 << 20, transcendentals=0
    )
    return pl.pallas_call(
        kernel,
        out_shape=outs,
        in_specs=[smem()] * scalars + [vmem() for _ in ins[scalars:]],
        out_specs=tuple(
            pl.BlockSpec(memory_space=pl.ANY) if k in far else vmem() for k in range(len(outs))
        ),
        scratch_shapes=list(scratch),
        compiler_params=pltpu.CompilerParams(vmem_limit_bytes=limit << 20),
        cost_estimate=cost,
        name=name,
    )(*ins)


def span(k, size=SUB):
    return slice(k * size, (k + 1) * size)


def split(x):
    high = x.astype(BF16)
    return high, (x - high.astype(F32)).astype(BF16)


def dot(x, y, dims=((1,), (0,))):
    return lax.dot_general(x, y, (dims, ((), ())), preferred_element_type=F32)


def dot_split(x, y, dims=((1,), (0,))):
    return dot(x[0], y[0], dims) + dot(x[0], y[1], dims) + dot(x[1], y[0], dims)


def both(ref, *at):
    return [ref[(k,) + at] for k in range(2)]


def put(dst, a, b, x):
    high, low = split(x)
    dst[0, span(a), span(b)] = high
    dst[1, span(a), span(b)] = low
    if a != b:
        dst[0, span(b), span(a)] = high.T
        dst[1, span(b), span(a)] = low.T


def get(src, *at):
    return src[(0,) + at].astype(F32) + src[(1,) + at].astype(F32)


def block(src, a, b):
    return get(src, span(a), span(b))


def fold(x):
    total = jnp.sum(x.reshape(x.shape[0] // 8, 8, x.shape[1]), axis=0)
    total = sum(total[:, span(k, 128)] for k in range(x.shape[1] // 128))
    return total[:4] + total[4:]


EVERY = slice(None)


def store_diagonal(dst, k, x, part=None):
    pieces = (
        (span(k, QUARTER), EVERY, x[:QUARTER, :]),
        (span(2, QUARTER), span(k, QUARTER), x[QUARTER:, QUARTER:]),
    )
    for rows, cols, piece in pieces:
        dst[rows, cols] = piece if part is None else part[rows, cols] + piece


def store_other(dst, k, x, part=None):
    start = 3 * QUARTER + k * SUB
    rows = slice(start, start + x.shape[0])
    dst[rows, :] = x if part is None else part[rows, :] + x


def load_half(src, at, which):
    for k, a in enumerate(DIAGONAL[which]):
        top = src[at + k * QUARTER : at + (k + 1) * QUARTER, :]
        corner = src[at + 2 * QUARTER : at + 3 * QUARTER, span(k, QUARTER)]
        bottom = jnp.concatenate([top[:, QUARTER:].T, corner], 1)
        yield a, a, jnp.concatenate([top, bottom], 0)
    for k, (a, b) in enumerate(OTHERS[which]):
        start = at + 3 * QUARTER + k * SUB
        yield a, b, src[start : start + SUB, :]


def left_blocks(core, src, dst, part=None):
    def rows(first, end, other_first, other_end):
        return dot_split(
            both(src, slice(first * SUB, end * SUB), EVERY),
            both(src, slice(other_first * SUB, other_end * SUB), EVERY),
            ((1,), (1,)),
        )

    @pl.when(core == 0)
    def _():
        store_diagonal(dst, 0, rows(0, 1, 0, 1), part)
        z = rows(0, 2, 1, 2)
        store_other(dst, 0, z[:SUB], part)
        store_diagonal(dst, 1, z[SUB:], part)
        store_other(dst, 1, rows(0, 2, 2, 3), part)

    @pl.when(core == 1)
    def _():
        store_diagonal(dst, 0, rows(2, 3, 2, 3), part)
        z = rows(2, 4, 3, 4)
        store_other(dst, 0, z[:SUB], part)
        store_diagonal(dst, 1, z[SUB:], part)
        z = rows(3, 4, 0, 2)
        store_other(dst, 1, z[:, span(0)], part)
        store_other(dst, 2, z[:, span(1)], part)


def pair_up(dst, src):
    for part in range(PARTS):
        high, low = split(src[span(part), :])
        dst[0, span(part), :] = high
        dst[1, span(part), :] = low


def turn(dst, src):
    for part in range(PARTS):
        for k in range(2):
            dst[k, :, span(part)] = src[k, span(part), :].T


def own_kernel(core_ref, own_ref, left_ref, pair):
    pair_up(pair, own_ref)
    left_blocks(core_ref[0], pair, left_ref)


def left_kernel(core_ref, other_ref, part_ref, left_ref, sq_ref, pair, total, sem):
    pair_up(pair, other_ref)
    left_blocks(core_ref[0], pair, total, part_ref)
    copy = pltpu.make_async_copy(total, left_ref, sem.at[0])
    copy.start()
    sq_ref[...] = fold(other_ref[...] * other_ref[...])
    copy.wait()


RUN = HALF // 8


def halves(stream, flip):
    def at(pos):
        near, far = (pos ^ flip) % 2, (pos ^ flip) // 2
        return (near ^ far, far) if stream == 0 else (far, near)

    return at


def rows_at(ref, at, size):
    return ref[pl.ds(pl.multiple_of(at, RUN), size), :]


def right_kernel(
    core_ref, ring_ref, own_ref, other_ref, after_ref,
    right_ref, first_ref, second_ref, own_out, other_out, own_pair, other_pair, turned, sems,
):
    core, ring = core_ref[0], ring_ref[0]
    pair_up(own_pair, own_ref)
    pair_up(other_pair, other_ref)
    copies = [
        pltpu.make_async_copy(own_pair, own_out, sems.at[0]),
        pltpu.make_async_copy(other_pair, other_out, sems.at[1]),
    ]
    for copy in copies:
        copy.start()
    turn(turned, own_pair)
    head = slice(0, SUB)
    store_diagonal(
        right_ref, 0, dot_split(both(turned, head, EVERY), both(own_pair, EVERY, head))
    )
    z = dot_split(both(turned, EVERY, EVERY), both(own_pair, EVERY, span(1)))
    store_other(right_ref, 0, z[:SUB])
    store_diagonal(right_ref, 1, z[SUB:])

    @pl.when(core == 0)
    def _():
        z = dot_split(both(turned, EVERY, EVERY), both(other_pair, EVERY, span(0)))
        store_other(right_ref, 1, z)

    @pl.when(core == 1)
    def _():
        z = dot_split(both(turned, span(1), EVERY), both(other_pair, EVERY, EVERY))
        store_other(right_ref, 1, z[:, span(0)])
        store_other(right_ref, 2, z[:, span(1)])

    for stream, out in enumerate((first_ref, second_ref)):
        half, _ = halves(stream, 0)(ring)
        out[...] = rows_at(right_ref, (4 * stream + 2 * (1 - half)) * RUN, 2 * RUN)
    for copy in copies:
        copy.wait()


def halve_kernel(
    ring_ref, right_ref, first_ref, second_ref, kept_ref, first_out_ref, second_out_ref, both_ref
):
    ring = ring_ref[0]
    for stream, (got, out) in enumerate(
        ((first_ref, first_out_ref), (second_ref, second_out_ref))
    ):
        half, quarter = halves(stream, 0)(ring)
        both_ref[...] = rows_at(right_ref, (4 * stream + 2 * half) * RUN, 2 * RUN) + got[...]
        kept_ref[span(stream, RUN), :] = rows_at(both_ref, quarter * RUN, RUN)
        out[...] = rows_at(both_ref, (1 - quarter) * RUN, RUN)


def place_kernel(ring_ref, mine_ref, near_ref, far_ref, over_first_ref, over_second_ref, out_ref):
    ring = ring_ref[0]
    size = RUN
    pieces = (
        (0, (mine_ref, mine_ref)),
        (1, (near_ref, near_ref)),
        (3, (far_ref, far_ref)),
        (2, (over_first_ref, over_second_ref)),
    )
    for flip, refs in pieces:
        for stream, ref in enumerate(refs):
            half, quarter = halves(stream, flip)(ring)
            at = pl.multiple_of((4 * stream + 2 * half + quarter) * size, size)
            out_ref[pl.ds(at, size), :] = ref[span(stream if flip != 2 else 0, size), :]


def spread_kernel(core_ref, shares_ref, after_ref, out_ref, total, sems):
    share = shares_ref[0]
    for k in range(1, shares_ref.shape[0]):
        share += shares_ref[k]
    total[...] = share
    copies = [
        pltpu.make_async_copy(total, out_ref.at[k], sems.at[k]) for k in range(out_ref.shape[0])
    ]
    for copy in copies:
        copy.start()
    for copy in copies:
        copy.wait()


def multiply(x, y, emit):
    for a in range(PARTS):
        z = dot_split(both(x, span(a), EVERY), both(y, EVERY, slice(a * SUB, BLOCK)))
        for b in range(a, PARTS):
            emit(a, b, z[:, span(b - a)])


def root_kernel(
    core_ref, left_ref, left_got_ref, right_ref, right_got_ref, out_ref, root_ref,
    factor, m, n, z, y, t,
):
    core = core_ref[0]

    @pl.when(core == 0)
    def _():
        factor[:HALF, :] = left_ref[...]
        factor[HALF:, :] = left_got_ref[...]

    @pl.when(core == 1)
    def _():
        factor[:HALF, :] = right_got_ref[...]
        factor[HALF:, :] = right_ref[...]

    def blocks():
        for which in range(2):
            yield from load_half(factor, which * HALF, which)

    squares = jnp.zeros((SUB, SUB), F32)
    for a, b, x in blocks():
        squares += x * x * (1.0 if a == b else 2.0)
    scale = 1.0 / (jnp.sqrt(jnp.sum(squares)) + NORM_EPS)
    for a, b, x in blocks():
        put(m, a, b, x * scale)

    multiply(m, m, lambda a, b, p: put(n, a, b, p))

    def cube(a, b, p):
        mm, nn = block(m, a, b), block(n, a, b)
        put(z, a, b, (25.0 * mm - 10.0 * nn + p) * (1.0 / 16.0))
        put(y, a, b, (nn - 10.0 * mm) * (1.0 / 16.0))

    multiply(m, n, cube)
    multiply(z, y, lambda a, b, p: put(t, a, b, (25.0 / 16.0) * block(z, a, b) + p))

    multiply(t, t, lambda a, b, p: put(n, a, b, p))

    def cube_again(a, b, p):
        tt, nn = block(t, a, b), block(n, a, b)
        put(z, a, b, (25.0 * tt - 10.0 * nn + p) * (1.0 / 16.0))
        put(y, a, b, (15.0 * nn - 75.0 * tt - p) * (1.0 / 64.0))

    multiply(t, n, cube_again)

    def last(a, b, p):
        put(n, a, b, -0.3125 * block(t, a, b) - (125.0 / 256.0) * block(z, a, b) - 0.25 * p)

    multiply(z, y, last)

    def result(a, b, p):
        p = 1.25 * block(n, a, b) - (25.0 / 64.0) * block(m, a, b) - 0.25 * p
        out_ref[span(PLACE[(a, b)]), :] = p
        put(root_ref, a, b, p)

    multiply(m, n, result)


def early_kernel(core_ref, root_ref, own_ref, other_ref, out_ref):
    core = core_ref[0]

    def keep(rows, cols, x):
        high, low = split(x)
        out_ref[0, rows, cols] = high
        out_ref[1, rows, cols] = low

    @pl.when(core == 0)
    def _():
        for part in range(PARTS):
            for k, src in enumerate((own_ref, other_ref)):
                x = dot_split(both(root_ref, span(part), EVERY), both(src, EVERY, EVERY))
                keep(span(part), span(k, SIDE), x + LEVEL * get(src, span(part), EVERY))

    @pl.when(core == 1)
    def _():
        for part in range(PARTS):
            at = span(part)
            x = dot_split(both(other_ref, at, EVERY), both(root_ref, span(0, SIDE), span(1, SIDE)))
            x += dot_split(both(own_ref, at, EVERY), both(root_ref, span(1, SIDE), span(1, SIDE)))
            keep(at, span(0, SIDE), x + LEVEL * get(own_ref, at, EVERY))


LANES = 128


def late_kernel(core_ref, early_ref, got_ref, sq_ref, out_ref, left, right):
    core = core_ref[0]
    rows = BLOCK // out_ref.shape[0]
    lanes = SIDE // LANES
    count = SUB // rows

    def finish(product):
        total = jnp.zeros((4, LANES), F32)
        for part in range(PARTS):
            x = product(span(part)) + LEVEL * get(early_ref, span(part), span(0, SIDE))
            total += fold(x * x)
            for lane in range(lanes):
                out_ref[span(part, count), span(lane, rows), :] = x[:, span(lane, LANES)].reshape(
                    count, rows, LANES
                )
        stats = jnp.concatenate([sq_ref[...], total], 0)
        out_ref[:, lanes * rows :, :] = jnp.broadcast_to(
            stats[None], (out_ref.shape[0],) + stats.shape
        )

    @pl.when(core == 0)
    def _():
        for a in range(PARTS):
            for b in range(2):
                x = got_ref[span(PLACE[(min(a, b), max(a, b))]), :]
                high, low = split(x)
                right[0, span(a), span(b)] = high if a <= b else high.T
                right[1, span(a), span(b)] = low if a <= b else low.T
        finish(lambda at: dot_split(both(early_ref, at, EVERY), both(right, EVERY, EVERY)))

    @pl.when(core == 1)
    def _():
        for k, (a, b) in enumerate(ROOT_PAIRS):
            put(left, a, b, got_ref[span(k), :])
        finish(
            lambda at: dot_split(both(left, at, EVERY), both(early_ref, EVERY, span(0, SIDE)))
        )


STEP_TILES = 2


def base_kernel(flag_ref, coef_ref, m_ref, f_ref, n_ref, out_ref):
    for t in range(STEP_TILES):
        at = span(t, BLOCK)
        flag = flag_ref[pl.program_id(0) * STEP_TILES + t]
        prior = jnp.where(flag == 1, coef_ref[1] * f_ref[:, at], m_ref[:, at])
        out_ref[:, at] = (1.0 - DAMPING_COEFF) * prior + coef_ref[2] * n_ref[:, at]


def update_kernel(coef_ref, sums_ref, dir_ref, w_ref, b_ref, ow_ref, om_ref):
    gsq = jnp.sum(sums_ref[:4, :])
    dsq = jnp.sum(sums_ref[4:, :])
    pull = coef_ref[0] * (jnp.sqrt(gsq) / (jnp.sqrt(dsq) + NORM_EPS))
    rows = w_ref.shape[0]
    lanes = SIDE // LANES
    for k in range(dir_ref.shape[0]):
        for lane in range(lanes):
            at = span(k * lanes + lane, LANES)
            moved = b_ref[:, at] - pull * dir_ref[k, span(lane, rows), :]
            om_ref[:, at] = moved
            ow_ref[:, at] = w_ref[:, at] + moved


def stream(kernel, name, shape, ins, specs, outs):
    rows, cols = shape
    width = STEP_TILES * BLOCK
    wide = pl.BlockSpec((rows, width), lambda i: (0, i))
    cost = pl.CostEstimate(
        flops=4 * rows * cols, bytes_accessed=(len(ins) + outs) * 4 * rows * cols, transcendentals=0
    )
    return pl.pallas_call(
        kernel,
        grid=(cols // width,),
        out_shape=tuple(array(*shape) for _ in range(outs)),
        in_specs=specs + [wide] * (len(ins) - len(specs)),
        out_specs=(wide,) * outs,
        compiler_params=pltpu.CompilerParams(vmem_limit_bytes=16 << 20),
        cost_estimate=cost,
        name=name,
    )(*ins)


def swapped(x, axis, flip):
    return lax.ppermute(x, axis, [(i, i ^ flip) for i in range(lax.axis_size(axis))])


def shards(gradient, weights, momentum, fresh_momentum, gaussian_noise, resample, step_index):
    rows, cols = gradient.shape
    col_pos = lax.axis_index("col")
    row_pos = lax.axis_index("row")
    core = (col_pos % 2).reshape(1).astype(jnp.int32)
    devices = lax.axis_size("col")
    by_core = [[c for c in range(devices) if c % 2 == k] for k in range(2)]

    phase = jnp.mod(step_index[0], CYCLE).astype(F32) / CYCLE
    rate = BASE_RATE * 0.5 * (1.0 + jnp.cos(jnp.pi * phase))
    coefs = jnp.stack([rate, jnp.sqrt(rate), jnp.sqrt(2.0 * DAMPING_COEFF * rate * HEAT_LEVEL)])
    flags = lax.dynamic_index_in_dim(resample, row_pos, 0, keepdims=False)
    pieces = gradient.reshape(rows, devices, SIDE).transpose(1, 0, 2)
    own = lax.all_to_all(pieces, "col", 0, 0).reshape(BLOCK, SIDE)
    other = swapped(own, "col", 1)
    pair = array(2, BLOCK, SIDE, dtype=BF16)
    pair_space = pltpu.VMEM((2, BLOCK, SIDE), BF16)
    (left,) = whole(own_kernel, "own", (array(HALF, SUB),), (core, own), [pair_space], products=0.16)
    left, grad_sq = whole(
        left_kernel,
        "left",
        (array(HALF, SUB), array(4, LANES)),
        (core, other, left),
        [pair_space, pltpu.VMEM((HALF, SUB), F32), pltpu.SemaphoreType.DMA((1,))],
        products=0.16,
        far=(0,),
    )
    chips = devices // 2
    shares = lax.all_to_all(
        left.reshape(chips, HALF // chips, SUB), "col", 0, 0, axis_index_groups=by_core
    )

    ring = row_pos.reshape(1).astype(jnp.int32)
    two, one = array(2 * RUN, SUB), array(RUN, SUB)
    right, to_first, to_second, own_pair, other_pair = whole(
        right_kernel,
        "right",
        (array(HALF, SUB), two, two, pair, pair),
        (core, ring, own, other, grad_sq),
        [
            pair_space,
            pair_space,
            pltpu.VMEM((2, SIDE, BLOCK), BF16),
            pltpu.SemaphoreType.DMA((2,)),
        ],
        products=0.3,
        scalars=2,
        far=(3, 4),
    )
    got = swapped(to_first, "row", 1), swapped(to_second, "row", 3)
    kept, to_first, to_second = whole(
        halve_kernel, "halve", (two, one, one), (ring, right) + got, [pltpu.VMEM((2 * RUN, SUB), F32)]
    )
    got = swapped(to_first, "row", 3), swapped(to_second, "row", 1)
    mine = kept + jnp.concatenate(got, 0)
    (share,) = whole(
        spread_kernel,
        "spread",
        (array(*shares.shape),),
        (core, shares, mine[:8]),
        [pltpu.VMEM(shares.shape[1:], F32), pltpu.SemaphoreType.DMA((chips,))],
        far=(0,),
    )
    left = lax.all_to_all(share, "col", 0, 0, axis_index_groups=by_core).reshape(HALF, SUB)
    mine, momentum, fresh_momentum, gaussian_noise = lax.optimization_barrier(
        (mine, momentum, fresh_momentum, gaussian_noise)
    )
    own = lax.all_to_all(pieces, "col", 0, 0).reshape(BLOCK, SIDE)
    other = swapped(own, "col", 1)
    pair = array(2, BLOCK, SIDE, dtype=BF16)
    pair_space = pltpu.VMEM((2, BLOCK, SIDE), BF16)
    (left,) = whole(own_kernel, "own", (array(HALF, SUB),), (core, own), [pair_space], products=0.16)
    left, grad_sq = whole(
        left_kernel,
        "left",
        (array(HALF, SUB), array(4, LANES)),
        (core, other, left),
        [pair_space, pltpu.VMEM((HALF, SUB), F32), pltpu.SemaphoreType.DMA((1,))],
        products=0.16,
        far=(0,),
    )
    chips = devices // 2
    shares = lax.all_to_all(
        left.reshape(chips, HALF // chips, SUB), "col", 0, 0, axis_index_groups=by_core
    )

    ring = row_pos.reshape(1).astype(jnp.int32)
    two, one = array(2 * RUN, SUB), array(RUN, SUB)
    right, to_first, to_second, own_pair, other_pair = whole(
        right_kernel,
        "right",
        (array(HALF, SUB), two, two, pair, pair),
        (core, ring, own, other, grad_sq),
        [
            pair_space,
            pair_space,
            pltpu.VMEM((2, SIDE, BLOCK), BF16),
            pltpu.SemaphoreType.DMA((2,)),
        ],
        products=0.3,
        scalars=2,
        far=(3, 4),
    )
    got = swapped(to_first, "row", 1), swapped(to_second, "row", 3)
    kept, to_first, to_second = whole(
        halve_kernel, "halve", (two, one, one), (ring, right) + got, [pltpu.VMEM((2 * RUN, SUB), F32)]
    )
    got = swapped(to_first, "row", 3), swapped(to_second, "row", 1)
    mine = kept + jnp.concatenate(got, 0)
    (share,) = whole(
        spread_kernel,
        "spread",
        (array(*shares.shape),),
        (core, shares, mine[:8]),
        [pltpu.VMEM(shares.shape[1:], F32), pltpu.SemaphoreType.DMA((chips,))],
        far=(0,),
    )
    left = lax.all_to_all(share, "col", 0, 0, axis_index_groups=by_core).reshape(HALF, SUB)
    mine, momentum, fresh_momentum, gaussian_noise = lax.optimization_barrier(
        (mine, momentum, fresh_momentum, gaussian_noise)
    )
    (base,) = stream(
        base_kernel,
        "base",
        (rows, cols),
        (flags, coefs, momentum, fresh_momentum, gaussian_noise),
        [smem(), smem()],
        1,
    )
    near, far = swapped(mine, "row", 1), swapped(mine, "row", 3)
    near, far, base = lax.optimization_barrier((near, far, base))
    over = swapped(far[:RUN], "row", 1), swapped(near[RUN:], "row", 3)
    (right,) = whole(place_kernel, "place", (array(HALF, SUB),), (ring, mine, near, far) + over)

    right_got = lax.ppermute(right, "col", [(i, i + 1) for i in range(0, devices, 2)])
    left_got = lax.ppermute(left, "col", [(i + 1, i) for i in range(0, devices, 2)])
    packed, root = whole(
        root_kernel,
        "root",
        (array(PACKED, SUB), array(2, BLOCK, BLOCK, dtype=BF16)),
        (core, left, left_got, right, right_got),
        [pltpu.VMEM((2 * HALF, SUB), F32)] + [pltpu.VMEM((2, BLOCK, BLOCK), BF16)] * 5,
        limit=30,
        products=7 * 0.625,
    )
    other_root = swapped(packed, "col", 1)
    (early,) = whole(
        early_kernel,
        "early",
        (array(2, BLOCK, BLOCK, dtype=BF16),),
        (core, root, own_pair, other_pair),
        products=1.0,
    )
    (message,) = whole(
        late_kernel,
        "late",
        (array(devices, rows * SIDE // LANES + 8, LANES),),
        (core, early, other_root, grad_sq),
        [pltpu.VMEM((2, BLOCK, BLOCK), BF16), pltpu.VMEM((2, BLOCK, SIDE), BF16)],
        products=0.5,
    )
    message = lax.all_to_all(message, "col", 0, 0)
    sums = jnp.sum(message[:, -8:, :], axis=0)
    total = lax.axis_size("row")
    got = [
        lax.ppermute(sums, "row", [(i, (i + k) % total) for i in range(total)])
        for k in range(1, total)
    ]
    sums = sums + sum(got)
    return stream(
        update_kernel,
        "update",
        (rows, cols),
        (coefs, sums, message, weights, base),
        [
            smem(),
            pl.BlockSpec((8, LANES), lambda i: (0, 0)),
            pl.BlockSpec((2 * STEP_TILES, message.shape[1], LANES), lambda i: (i, 0, 0)),
        ],
        2,
    )


def solution(mesh):
    wide = P(("row", "col"), None)
    in_specs = (wide, wide, wide, wide, wide, P(), P())
    return jax.shard_map(
        shards, mesh=mesh, in_specs=in_specs, out_specs=(wide, wide), check_vma=False
    )
```

```python
import jax
import jax.numpy as jnp
from jax import lax
from jax.experimental import pallas as pl
from jax.experimental.pallas import tpu as pltpu
from jax.sharding import PartitionSpec as P

BLOCK = 1024
CYCLE = 1000
NORM_EPS = 1e-06
BASE_RATE = 0.5
DAMPING_COEFF = 0.1
HEAT_LEVEL = 1.0

SUB = 256
QUARTER = SUB // 2
PARTS = BLOCK // SUB
SIDE = BLOCK // 2
DIAGONAL = ((0, 1), (2, 3))
OTHERS = (((0, 1), (0, 2), (1, 2)), ((2, 3), (3, 0), (3, 1)))
HALF = 3 * QUARTER + 3 * SUB
ROOT_PAIRS = [(a, b) for b in range(PARTS) for a in range(b + 1)]
PLACE = {pair: k for k, pair in enumerate(ROOT_PAIRS)}
PACKED = len(ROOT_PAIRS) * SUB
LEVEL = 125.0 / 64.0
F32, BF16 = jnp.float32, jnp.bfloat16


def vmem():
    return pl.BlockSpec(memory_space=pltpu.VMEM)


def smem():
    return pl.BlockSpec(memory_space=pltpu.SMEM)


def array(*shape, dtype=F32):
    return jax.ShapeDtypeStruct(shape, dtype)


def whole(kernel, name, outs, ins, scratch=(), limit=16, products=0.0, scalars=1, far=()):
    cost = pl.CostEstimate(
        flops=int(products * 6 * BLOCK**3), bytes_accessed=8 << 20, transcendentals=0
    )
    return pl.pallas_call(
        kernel,
        out_shape=outs,
        in_specs=[smem()] * scalars + [vmem() for _ in ins[scalars:]],
        out_specs=tuple(
            pl.BlockSpec(memory_space=pltpu.HBM) if k in far else vmem() for k in range(len(outs))
        ),
        scratch_shapes=list(scratch),
        compiler_params=pltpu.CompilerParams(vmem_limit_bytes=limit << 20),
        cost_estimate=cost,
        name=name,
    )(*ins)


def span(k, size=SUB):
    return slice(k * size, (k + 1) * size)


def split(x):
    high = x.astype(BF16)
    return high, (x - high.astype(F32)).astype(BF16)


def dot(x, y, dims=((1,), (0,))):
    return lax.dot_general(x, y, (dims, ((), ())), preferred_element_type=F32)


def dot_split(x, y, dims=((1,), (0,))):
    return dot(x[0], y[0], dims) + dot(x[0], y[1], dims) + dot(x[1], y[0], dims)


def both(ref, *at):
    return [ref[(k,) + at] for k in range(2)]


def put(dst, a, b, x):
    high, low = split(x)
    dst[0, span(a), span(b)] = high
    dst[1, span(a), span(b)] = low
    if a != b:
        dst[0, span(b), span(a)] = high.T
        dst[1, span(b), span(a)] = low.T


def get(src, *at):
    return src[(0,) + at].astype(F32) + src[(1,) + at].astype(F32)


def block(src, a, b):
    return get(src, span(a), span(b))


def fold(x):
    total = jnp.sum(x.reshape(x.shape[0] // 8, 8, x.shape[1]), axis=0)
    total = sum(total[:, span(k, 128)] for k in range(x.shape[1] // 128))
    return total[:4] + total[4:]


EVERY = slice(None)


def store_diagonal(dst, k, x, part=None):
    pieces = (
        (span(k, QUARTER), EVERY, x[:QUARTER, :]),
        (span(2, QUARTER), span(k, QUARTER), x[QUARTER:, QUARTER:]),
    )
    for rows, cols, piece in pieces:
        dst[rows, cols] = piece if part is None else part[rows, cols] + piece


def store_other(dst, k, x, part=None):
    start = 3 * QUARTER + k * SUB
    rows = slice(start, start + x.shape[0])
    dst[rows, :] = x if part is None else part[rows, :] + x


def load_half(src, at, which):
    for k, a in enumerate(DIAGONAL[which]):
        top = src[at + k * QUARTER : at + (k + 1) * QUARTER, :]
        corner = src[at + 2 * QUARTER : at + 3 * QUARTER, span(k, QUARTER)]
        bottom = jnp.concatenate([top[:, QUARTER:].T, corner], 1)
        yield a, a, jnp.concatenate([top, bottom], 0)
    for k, (a, b) in enumerate(OTHERS[which]):
        start = at + 3 * QUARTER + k * SUB
        yield a, b, src[start : start + SUB, :]


def left_blocks(core, src, dst, part=None):
    def rows(first, end, other_first, other_end):
        return dot_split(
            both(src, slice(first * SUB, end * SUB), EVERY),
            both(src, slice(other_first * SUB, other_end * SUB), EVERY),
            ((1,), (1,)),
        )

    @pl.when(core == 0)
    def _():
        store_diagonal(dst, 0, rows(0, 1, 0, 1), part)
        z = rows(0, 2, 1, 2)
        store_other(dst, 0, z[:SUB], part)
        store_diagonal(dst, 1, z[SUB:], part)
        store_other(dst, 1, rows(0, 2, 2, 3), part)

    @pl.when(core == 1)
    def _():
        store_diagonal(dst, 0, rows(2, 3, 2, 3), part)
        z = rows(2, 4, 3, 4)
        store_other(dst, 0, z[:SUB], part)
        store_diagonal(dst, 1, z[SUB:], part)
        z = rows(3, 4, 0, 2)
        store_other(dst, 1, z[:, span(0)], part)
        store_other(dst, 2, z[:, span(1)], part)


def pair_up(dst, src):
    for part in range(PARTS):
        high, low = split(src[span(part), :])
        dst[0, span(part), :] = high
        dst[1, span(part), :] = low


def turn(dst, src):
    for part in range(PARTS):
        for k in range(2):
            dst[k, :, span(part)] = src[k, span(part), :].T


def own_kernel(core_ref, own_ref, left_ref, pair):
    pair_up(pair, own_ref)
    left_blocks(core_ref[0], pair, left_ref)


def left_kernel(core_ref, other_ref, part_ref, left_ref, sq_ref, pair, total, sem):
    pair_up(pair, other_ref)
    left_blocks(core_ref[0], pair, total, part_ref)
    copy = pltpu.make_async_copy(total, left_ref, sem.at[0])
    copy.start()
    sq_ref[...] = fold(other_ref[...] * other_ref[...])
    copy.wait()


RUN = HALF // 8


def halves(stream, flip):
    def at(pos):
        near, far = (pos ^ flip) % 2, (pos ^ flip) // 2
        return (near ^ far, far) if stream == 0 else (far, near)

    return at


def rows_at(ref, at, size):
    return ref[pl.ds(pl.multiple_of(at, RUN), size), :]


def right_kernel(
    core_ref, ring_ref, own_ref, other_ref, after_ref,
    right_ref, first_ref, second_ref, own_out, other_out, own_pair, other_pair, turned, sems,
):
    core, ring = core_ref[0], ring_ref[0]
    pair_up(own_pair, own_ref)
    pair_up(other_pair, other_ref)
    copies = [
        pltpu.make_async_copy(own_pair, own_out, sems.at[0]),
        pltpu.make_async_copy(other_pair, other_out, sems.at[1]),
    ]
    for copy in copies:
        copy.start()
    turn(turned, own_pair)
    head = slice(0, SUB)
    store_diagonal(
        right_ref, 0, dot_split(both(turned, head, EVERY), both(own_pair, EVERY, head))
    )
    z = dot_split(both(turned, EVERY, EVERY), both(own_pair, EVERY, span(1)))
    store_other(right_ref, 0, z[:SUB])
    store_diagonal(right_ref, 1, z[SUB:])

    @pl.when(core == 0)
    def _():
        z = dot_split(both(turned, EVERY, EVERY), both(other_pair, EVERY, span(0)))
        store_other(right_ref, 1, z)

    @pl.when(core == 1)
    def _():
        z = dot_split(both(turned, span(1), EVERY), both(other_pair, EVERY, EVERY))
        store_other(right_ref, 1, z[:, span(0)])
        store_other(right_ref, 2, z[:, span(1)])

    for stream, out in enumerate((first_ref, second_ref)):
        half, _ = halves(stream, 0)(ring)
        out[...] = rows_at(right_ref, (4 * stream + 2 * (1 - half)) * RUN, 2 * RUN)
    for copy in copies:
        copy.wait()


def halve_kernel(
    ring_ref, right_ref, first_ref, second_ref, kept_ref, first_out_ref, second_out_ref, both_ref
):
    ring = ring_ref[0]
    for stream, (got, out) in enumerate(
        ((first_ref, first_out_ref), (second_ref, second_out_ref))
    ):
        half, quarter = halves(stream, 0)(ring)
        both_ref[...] = rows_at(right_ref, (4 * stream + 2 * half) * RUN, 2 * RUN) + got[...]
        kept_ref[span(stream, RUN), :] = rows_at(both_ref, quarter * RUN, RUN)
        out[...] = rows_at(both_ref, (1 - quarter) * RUN, RUN)


def place_kernel(ring_ref, mine_ref, near_ref, far_ref, over_first_ref, over_second_ref, out_ref):
    ring = ring_ref[0]
    size = RUN
    pieces = (
        (0, (mine_ref, mine_ref)),
        (1, (near_ref, near_ref)),
        (3, (far_ref, far_ref)),
        (2, (over_first_ref, over_second_ref)),
    )
    for flip, refs in pieces:
        for stream, ref in enumerate(refs):
            half, quarter = halves(stream, flip)(ring)
            at = pl.multiple_of((4 * stream + 2 * half + quarter) * size, size)
            out_ref[pl.ds(at, size), :] = ref[span(stream if flip != 2 else 0, size), :]


def spread_kernel(core_ref, shares_ref, after_ref, out_ref, total, sems):
    share = shares_ref[0]
    for k in range(1, shares_ref.shape[0]):
        share += shares_ref[k]
    total[...] = share
    copies = [
        pltpu.make_async_copy(total, out_ref.at[k], sems.at[k]) for k in range(out_ref.shape[0])
    ]
    for copy in copies:
        copy.start()
    for copy in copies:
        copy.wait()


def multiply(x, y, emit):
    for a in range(PARTS):
        z = dot_split(both(x, span(a), EVERY), both(y, EVERY, slice(a * SUB, BLOCK)))
        for b in range(a, PARTS):
            emit(a, b, z[:, span(b - a)])


def root_kernel(
    core_ref, left_ref, left_got_ref, right_ref, right_got_ref, out_ref, root_ref,
    factor, m, n, z, y, t,
):
    core = core_ref[0]

    @pl.when(core == 0)
    def _():
        factor[:HALF, :] = left_ref[...]
        factor[HALF:, :] = left_got_ref[...]

    @pl.when(core == 1)
    def _():
        factor[:HALF, :] = right_got_ref[...]
        factor[HALF:, :] = right_ref[...]

    def blocks():
        for which in range(2):
            yield from load_half(factor, which * HALF, which)

    squares = jnp.zeros((SUB, SUB), F32)
    for a, b, x in blocks():
        squares += x * x * (1.0 if a == b else 2.0)
    scale = 1.0 / (jnp.sqrt(jnp.sum(squares)) + NORM_EPS)
    for a, b, x in blocks():
        put(m, a, b, x * scale)

    multiply(m, m, lambda a, b, p: put(n, a, b, p))

    def cube(a, b, p):
        mm, nn = block(m, a, b), block(n, a, b)
        put(z, a, b, (25.0 * mm - 10.0 * nn + p) * (1.0 / 16.0))
        put(y, a, b, (nn - 10.0 * mm) * (1.0 / 16.0))

    multiply(m, n, cube)
    multiply(z, y, lambda a, b, p: put(t, a, b, (25.0 / 16.0) * block(z, a, b) + p))

    multiply(t, t, lambda a, b, p: put(n, a, b, p))

    def cube_again(a, b, p):
        tt, nn = block(t, a, b), block(n, a, b)
        put(z, a, b, (25.0 * tt - 10.0 * nn + p) * (1.0 / 16.0))
        put(y, a, b, (15.0 * nn - 75.0 * tt - p) * (1.0 / 64.0))

    multiply(t, n, cube_again)

    def last(a, b, p):
        put(n, a, b, -0.3125 * block(t, a, b) - (125.0 / 256.0) * block(z, a, b) - 0.25 * p)

    multiply(z, y, last)

    def result(a, b, p):
        p = 1.25 * block(n, a, b) - (25.0 / 64.0) * block(m, a, b) - 0.25 * p
        out_ref[span(PLACE[(a, b)]), :] = p
        put(root_ref, a, b, p)

    multiply(m, n, result)


def early_kernel(core_ref, root_ref, own_ref, other_ref, out_ref):
    core = core_ref[0]

    def keep(rows, cols, x):
        high, low = split(x)
        out_ref[0, rows, cols] = high
        out_ref[1, rows, cols] = low

    @pl.when(core == 0)
    def _():
        for part in range(PARTS):
            for k, src in enumerate((own_ref, other_ref)):
                x = dot_split(both(root_ref, span(part), EVERY), both(src, EVERY, EVERY))
                keep(span(part), span(k, SIDE), x + LEVEL * get(src, span(part), EVERY))

    @pl.when(core == 1)
    def _():
        for part in range(PARTS):
            at = span(part)
            x = dot_split(both(other_ref, at, EVERY), both(root_ref, span(0, SIDE), span(1, SIDE)))
            x += dot_split(both(own_ref, at, EVERY), both(root_ref, span(1, SIDE), span(1, SIDE)))
            keep(at, span(0, SIDE), x + LEVEL * get(own_ref, at, EVERY))


LANES = 128


FIRST_ROWS = 24


def late_kernel(
    core_ref, early_ref, got_ref, sq_ref, first_out, second_out, left, right, first, second, sems
):
    core = core_ref[0]
    rows = BLOCK // first.shape[0]
    lanes = SIDE // LANES
    count = SUB // rows
    rest = rows - FIRST_ROWS
    body = slice(0, lanes * FIRST_ROWS)
    tail = slice(lanes * FIRST_ROWS, lanes * FIRST_ROWS + 8)

    def finish(product):
        total = jnp.zeros((4, LANES), F32)
        copies = []
        for part in range(PARTS):
            at = span(part, count)
            x = product(span(part)) + LEVEL * get(early_ref, span(part), span(0, SIDE))
            total += fold(x * x)
            for lane in range(lanes):
                piece = x[:, span(lane, LANES)].reshape(count, rows, LANES)
                first[at, span(lane, FIRST_ROWS), :] = piece[:, :FIRST_ROWS]
                second[at, span(lane, rest), :] = piece[:, FIRST_ROWS:]
            copies += [
                pltpu.make_async_copy(
                    first.at[at, body], first_out.at[at, body], sems.at[2 * part]
                ),
                pltpu.make_async_copy(second.at[at], second_out.at[at], sems.at[2 * part + 1]),
            ]
            for copy in copies[-2:]:
                copy.start()
        stats = jnp.concatenate([sq_ref[...], total], 0)
        first[:, tail, :] = jnp.broadcast_to(stats[None], (first.shape[0],) + stats.shape)
        copies.append(
            pltpu.make_async_copy(first.at[:, tail], first_out.at[:, tail], sems.at[2 * PARTS])
        )
        copies[-1].start()
        for copy in copies:
            copy.wait()

    @pl.when(core == 0)
    def _():
        for a in range(PARTS):
            for b in range(2):
                x = got_ref[span(PLACE[(min(a, b), max(a, b))]), :]
                high, low = split(x)
                right[0, span(a), span(b)] = high if a <= b else high.T
                right[1, span(a), span(b)] = low if a <= b else low.T
        finish(lambda at: dot_split(both(early_ref, at, EVERY), both(right, EVERY, EVERY)))

    @pl.when(core == 1)
    def _():
        for k, (a, b) in enumerate(ROOT_PAIRS):
            put(left, a, b, got_ref[span(k), :])
        finish(
            lambda at: dot_split(both(left, at, EVERY), both(early_ref, EVERY, span(0, SIDE)))
        )


STEP_TILES = 2


def base_kernel(flag_ref, coef_ref, m_ref, f_ref, n_ref, out_ref):
    for t in range(STEP_TILES):
        at = span(t, BLOCK)
        flag = flag_ref[pl.program_id(0) * STEP_TILES + t]
        prior = jnp.where(flag == 1, coef_ref[1] * f_ref[:, at], m_ref[:, at])
        out_ref[:, at] = (1.0 - DAMPING_COEFF) * prior + coef_ref[2] * n_ref[:, at]


def update_kernel(coef_ref, sums_ref, dir_ref, w_ref, b_ref, *refs):
    ow_ref, om_ref = refs[-2:]
    gsq = jnp.sum(sums_ref[:4, :])
    dsq = jnp.sum(sums_ref[4:, :])
    pull = coef_ref[0] * (jnp.sqrt(gsq) / (jnp.sqrt(dsq) + NORM_EPS))
    rows = w_ref.shape[0]
    lanes = SIDE // LANES
    for k in range(dir_ref.shape[0]):
        for lane in range(lanes):
            at = span(k * lanes + lane, LANES)
            moved = b_ref[:, at] - pull * dir_ref[k, span(lane, rows), :]
            om_ref[:, at] = moved
            ow_ref[:, at] = w_ref[:, at] + moved


def update(name, shape, coefs, sums, message, weights, base, row, count, tiles, done=()):
    wide = pl.BlockSpec((count, tiles * BLOCK), lambda i: (row // count, i))
    return pl.pallas_call(
        update_kernel,
        grid=(shape[1] // (tiles * BLOCK),),
        out_shape=(array(*shape), array(*shape)),
        in_specs=[
            smem(),
            pl.BlockSpec((8, LANES), lambda i: (0, 0)),
            pl.BlockSpec((2 * tiles,) + message.shape[1:], lambda i: (i, 0, 0)),
            wide,
            wide,
        ]
        + [pl.BlockSpec(memory_space=pltpu.HBM)] * len(done),
        out_specs=(wide, wide),
        input_output_aliases={5: 0, 6: 1} if done else {},
        compiler_params=pltpu.CompilerParams(vmem_limit_bytes=16 << 20),
        cost_estimate=pl.CostEstimate(
            flops=4 * count * shape[1], bytes_accessed=20 * count * shape[1], transcendentals=0
        ),
        name=name,
    )(coefs, sums, message, weights, base, *done)


def stream(kernel, name, shape, ins, specs, outs):
    rows, cols = shape
    width = STEP_TILES * BLOCK
    wide = pl.BlockSpec((rows, width), lambda i: (0, i))
    cost = pl.CostEstimate(
        flops=4 * rows * cols, bytes_accessed=(len(ins) + outs) * 4 * rows * cols, transcendentals=0
    )
    return pl.pallas_call(
        kernel,
        grid=(cols // width,),
        out_shape=tuple(array(*shape) for _ in range(outs)),
        in_specs=specs + [wide] * (len(ins) - len(specs)),
        out_specs=(wide,) * outs,
        compiler_params=pltpu.CompilerParams(vmem_limit_bytes=16 << 20),
        cost_estimate=cost,
        name=name,
    )(*ins)


def swapped(x, axis, flip):
    return lax.ppermute(x, axis, [(i, i ^ flip) for i in range(lax.axis_size(axis))])


def shards(gradient, weights, momentum, fresh_momentum, gaussian_noise, resample, step_index):
    rows, cols = gradient.shape
    col_pos = lax.axis_index("col")
    row_pos = lax.axis_index("row")
    core = (col_pos % 2).reshape(1).astype(jnp.int32)
    devices = lax.axis_size("col")
    by_core = [[c for c in range(devices) if c % 2 == k] for k in range(2)]

    phase = jnp.mod(step_index[0], CYCLE).astype(F32) / CYCLE
    rate = BASE_RATE * 0.5 * (1.0 + jnp.cos(jnp.pi * phase))
    coefs = jnp.stack([rate, jnp.sqrt(rate), jnp.sqrt(2.0 * DAMPING_COEFF * rate * HEAT_LEVEL)])
    flags = lax.dynamic_index_in_dim(resample, row_pos, 0, keepdims=False)
    pieces = gradient.reshape(rows, devices, SIDE).transpose(1, 0, 2)
    own = lax.all_to_all(pieces, "col", 0, 0).reshape(BLOCK, SIDE)
    other = swapped(own, "col", 1)
    pair = array(2, BLOCK, SIDE, dtype=BF16)
    pair_space = pltpu.VMEM((2, BLOCK, SIDE), BF16)
    (left,) = whole(own_kernel, "own", (array(HALF, SUB),), (core, own), [pair_space], products=0.16)
    left, grad_sq = whole(
        left_kernel,
        "left",
        (array(HALF, SUB), array(4, LANES)),
        (core, other, left),
        [pair_space, pltpu.VMEM((HALF, SUB), F32), pltpu.SemaphoreType.DMA((1,))],
        products=0.16,
        far=(0,),
    )
    chips = devices // 2
    shares = lax.all_to_all(
        left.reshape(chips, HALF // chips, SUB), "col", 0, 0, axis_index_groups=by_core
    )

    ring = row_pos.reshape(1).astype(jnp.int32)
    two, one = array(2 * RUN, SUB), array(RUN, SUB)
    right, to_first, to_second, own_pair, other_pair = whole(
        right_kernel,
        "right",
        (array(HALF, SUB), two, two, pair, pair),
        (core, ring, own, other, grad_sq),
        [
            pair_space,
            pair_space,
            pltpu.VMEM((2, SIDE, BLOCK), BF16),
            pltpu.SemaphoreType.DMA((2,)),
        ],
        products=0.3,
        scalars=2,
        far=(3, 4),
    )
    got = swapped(to_first, "row", 1), swapped(to_second, "row", 3)
    kept, to_first, to_second = whole(
        halve_kernel, "halve", (two, one, one), (ring, right) + got, [pltpu.VMEM((2 * RUN, SUB), F32)]
    )
    got = swapped(to_first, "row", 3), swapped(to_second, "row", 1)
    mine = kept + jnp.concatenate(got, 0)
    (share,) = whole(
        spread_kernel,
        "spread",
        (array(*shares.shape),),
        (core, shares, kept[:8]),
        [pltpu.VMEM(shares.shape[1:], F32), pltpu.SemaphoreType.DMA((chips,))],
        far=(0,),
    )
    left = lax.all_to_all(share, "col", 0, 0, axis_index_groups=by_core).reshape(HALF, SUB)
    mine, momentum, fresh_momentum, gaussian_noise = lax.optimization_barrier(
        (mine, momentum, fresh_momentum, gaussian_noise)
    )
    (base,) = stream(
        base_kernel,
        "base",
        (rows, cols),
        (flags, coefs, momentum, fresh_momentum, gaussian_noise),
        [smem(), smem()],
        1,
    )
    near, far = swapped(mine, "row", 1), swapped(mine, "row", 3)
    near, far, base = lax.optimization_barrier((near, far, base))
    over = swapped(far[:RUN], "row", 1), swapped(near[RUN:], "row", 3)
    (right,) = whole(place_kernel, "place", (array(HALF, SUB),), (ring, mine, near, far) + over)

    right_got = lax.ppermute(right, "col", [(i, i + 1) for i in range(0, devices, 2)])
    left_got = lax.ppermute(left, "col", [(i + 1, i) for i in range(0, devices, 2)])
    packed, root = whole(
        root_kernel,
        "root",
        (array(PACKED, SUB), array(2, BLOCK, BLOCK, dtype=BF16)),
        (core, left, left_got, right, right_got),
        [pltpu.VMEM((2 * HALF, SUB), F32)] + [pltpu.VMEM((2, BLOCK, BLOCK), BF16)] * 5,
        limit=30,
        products=7 * 0.625,
    )
    other_root = swapped(packed, "col", 1)
    (early,) = whole(
        early_kernel,
        "early",
        (array(2, BLOCK, BLOCK, dtype=BF16),),
        (core, root, own_pair, other_pair),
        products=1.0,
    )
    lanes = SIDE // LANES
    first = array(devices, lanes * FIRST_ROWS + 8, LANES)
    second = array(devices, lanes * (rows - FIRST_ROWS), LANES)
    message, rest = whole(
        late_kernel,
        "late",
        (first, second),
        (core, early, other_root, grad_sq),
        [
            pltpu.VMEM((2, BLOCK, BLOCK), BF16),
            pltpu.VMEM((2, BLOCK, SIDE), BF16),
            pltpu.VMEM(first.shape, F32),
            pltpu.VMEM(second.shape, F32),
            pltpu.SemaphoreType.DMA((2 * PARTS + 1,)),
        ],
        products=0.5,
        far=(0, 1),
    )
    message = lax.all_to_all(message, "col", 0, 0)
    rest = lax.all_to_all(rest, "col", 0, 0)
    sums = jnp.sum(message[:, -8:, :], axis=0)
    total = lax.axis_size("row")
    got = [
        lax.ppermute(sums, "row", [(i, (i + k) % total) for i in range(total)])
        for k in range(1, total)
    ]
    sums = sums + sum(got)
    shape = (rows, cols)
    done = update("most", shape, coefs, sums, message, weights, base, 0, FIRST_ROWS, 2)
    return update(
        "rest", shape, coefs, sums, rest, weights, base, FIRST_ROWS, rows - FIRST_ROWS, 8, done
    )


def solution(mesh):
    wide = P(("row", "col"), None)
    in_specs = (wide, wide, wide, wide, wide, P(), P())
    return jax.shard_map(
        shards, mesh=mesh, in_specs=in_specs, out_specs=(wide, wide), check_vma=False
    )
```

```python
import functools

import jax
import jax.numpy as jnp
from jax import lax
from jax.experimental import pallas as pl
from jax.experimental.pallas import tpu as pltpu
from jax.sharding import PartitionSpec as P

BLOCK = 1024
CYCLE = 1000
NORM_EPS = 1e-06
BASE_RATE = 0.5
DAMPING_COEFF = 0.1
HEAT_LEVEL = 1.0

SUB = 256
QUARTER = SUB // 2
PARTS = BLOCK // SUB
SIDE = BLOCK // 2
DIAGONAL = ((0, 1), (2, 3))
OTHERS = (((0, 1), (0, 2), (1, 2)), ((2, 3), (3, 0), (3, 1)))
HALF = 3 * QUARTER + 3 * SUB
ROOT_PAIRS = [(a, b) for b in range(PARTS) for a in range(b + 1)]
PLACE = {pair: k for k, pair in enumerate(ROOT_PAIRS)}
PACKED = len(ROOT_PAIRS) * SUB
LEVEL = 125.0 / 64.0
F32, BF16 = jnp.float32, jnp.bfloat16


def vmem():
    return pl.BlockSpec(memory_space=pltpu.VMEM)


def smem():
    return pl.BlockSpec(memory_space=pltpu.SMEM)


def array(*shape, dtype=F32):
    return jax.ShapeDtypeStruct(shape, dtype)


def whole(kernel, name, outs, ins, scratch=(), limit=16, products=0.0, scalars=1, far=()):
    cost = pl.CostEstimate(
        flops=int(products * 6 * BLOCK**3), bytes_accessed=8 << 20, transcendentals=0
    )
    return pl.pallas_call(
        kernel,
        out_shape=outs,
        in_specs=[smem()] * scalars + [vmem() for _ in ins[scalars:]],
        out_specs=tuple(
            pl.BlockSpec(memory_space=pltpu.HBM) if k in far else vmem() for k in range(len(outs))
        ),
        scratch_shapes=list(scratch),
        compiler_params=pltpu.CompilerParams(vmem_limit_bytes=limit << 20),
        cost_estimate=cost,
        name=name,
    )(*ins)


def span(k, size=SUB):
    return slice(k * size, (k + 1) * size)


def split(x):
    high = x.astype(BF16)
    return high, (x - high.astype(F32)).astype(BF16)


def dot(x, y, dims=((1,), (0,))):
    return lax.dot_general(x, y, (dims, ((), ())), preferred_element_type=F32)


def dot_split(x, y, dims=((1,), (0,))):
    return dot(x[0], y[0], dims) + dot(x[0], y[1], dims) + dot(x[1], y[0], dims)


def both(ref, *at):
    return [ref[(k,) + at] for k in range(2)]


def put(dst, a, b, x):
    high, low = split(x)
    dst[0, span(a), span(b)] = high
    dst[1, span(a), span(b)] = low
    if a != b:
        dst[0, span(b), span(a)] = high.T
        dst[1, span(b), span(a)] = low.T


def get(src, *at):
    return src[(0,) + at].astype(F32) + src[(1,) + at].astype(F32)


def block(src, a, b):
    return get(src, span(a), span(b))


def fold(x):
    total = jnp.sum(x.reshape(x.shape[0] // 8, 8, x.shape[1]), axis=0)
    total = sum(total[:, span(k, 128)] for k in range(x.shape[1] // 128))
    return total[:4] + total[4:]


EVERY = slice(None)


def store_diagonal(dst, k, x, part=None):
    pieces = (
        (span(k, QUARTER), EVERY, x[:QUARTER, :]),
        (span(2, QUARTER), span(k, QUARTER), x[QUARTER:, QUARTER:]),
    )
    for rows, cols, piece in pieces:
        dst[rows, cols] = piece if part is None else part[rows, cols] + piece


def store_other(dst, k, x, part=None):
    start = 3 * QUARTER + k * SUB
    rows = slice(start, start + x.shape[0])
    dst[rows, :] = x if part is None else part[rows, :] + x


def load_half(src, at, which):
    for k, a in enumerate(DIAGONAL[which]):
        top = src[at + k * QUARTER : at + (k + 1) * QUARTER, :]
        corner = src[at + 2 * QUARTER : at + 3 * QUARTER, span(k, QUARTER)]
        bottom = jnp.concatenate([top[:, QUARTER:].T, corner], 1)
        yield a, a, jnp.concatenate([top, bottom], 0)
    for k, (a, b) in enumerate(OTHERS[which]):
        start = at + 3 * QUARTER + k * SUB
        yield a, b, src[start : start + SUB, :]


def left_blocks(core, src, dst, part=None):
    def rows(first, end, other_first, other_end):
        return dot_split(
            both(src, slice(first * SUB, end * SUB), EVERY),
            both(src, slice(other_first * SUB, other_end * SUB), EVERY),
            ((1,), (1,)),
        )

    @pl.when(core == 0)
    def _():
        store_diagonal(dst, 0, rows(0, 1, 0, 1), part)
        z = rows(0, 2, 1, 2)
        store_other(dst, 0, z[:SUB], part)
        store_diagonal(dst, 1, z[SUB:], part)
        store_other(dst, 1, rows(0, 2, 2, 3), part)

    @pl.when(core == 1)
    def _():
        store_diagonal(dst, 0, rows(2, 3, 2, 3), part)
        z = rows(2, 4, 3, 4)
        store_other(dst, 0, z[:SUB], part)
        store_diagonal(dst, 1, z[SUB:], part)
        z = rows(3, 4, 0, 2)
        store_other(dst, 1, z[:, span(0)], part)
        store_other(dst, 2, z[:, span(1)], part)


def pair_up(dst, src):
    for part in range(PARTS):
        high, low = split(src[span(part), :])
        dst[0, span(part), :] = high
        dst[1, span(part), :] = low


def turn(dst, src):
    for part in range(PARTS):
        for k in range(2):
            dst[k, :, span(part)] = src[k, span(part), :].T


def own_kernel(core_ref, own_ref, left_ref, pair):
    pair_up(pair, own_ref)
    left_blocks(core_ref[0], pair, left_ref)


def left_kernel(core_ref, other_ref, part_ref, left_ref, sq_ref, pair, total, sem):
    pair_up(pair, other_ref)
    left_blocks(core_ref[0], pair, total, part_ref)
    copy = pltpu.make_async_copy(total, left_ref, sem.at[0])
    copy.start()
    sq_ref[...] = fold(other_ref[...] * other_ref[...])
    copy.wait()


RUN = HALF // 4
HALF_FLIPS, QUARTER_FLIPS = (1, 3), (3, 1)


def ring_place(core, pos):
    near, far = pos % 2, pos // 2
    return jnp.where(core == 0, near ^ far, far), jnp.where(core == 0, far, near)


def rows_at(k, size):
    return pl.ds(pl.multiple_of(k * size, size), size)


def right_kernel(
    core_ref, ring_ref, own_ref, other_ref, after_ref, right_ref, sent_ref, own_pair, other_pair, turned
):
    core = core_ref[0]
    pair_up(own_pair, own_ref)
    pair_up(other_pair, other_ref)
    turn(turned, own_pair)
    head = slice(0, SUB)
    store_diagonal(
        right_ref, 0, dot_split(both(turned, head, EVERY), both(own_pair, EVERY, head))
    )
    z = dot_split(both(turned, EVERY, EVERY), both(own_pair, EVERY, span(1)))
    store_other(right_ref, 0, z[:SUB])
    store_diagonal(right_ref, 1, z[SUB:])

    @pl.when(core == 0)
    def _():
        z = dot_split(both(turned, EVERY, EVERY), both(other_pair, EVERY, span(0)))
        store_other(right_ref, 1, z)

    @pl.when(core == 1)
    def _():
        z = dot_split(both(turned, span(1), EVERY), both(other_pair, EVERY, EVERY))
        store_other(right_ref, 1, z[:, span(0)])
        store_other(right_ref, 2, z[:, span(1)])

    half, _ = ring_place(core, ring_ref[0])
    sent_ref[...] = right_ref[rows_at(1 - half, 2 * RUN), :]


def halve_kernel(core_ref, ring_ref, right_ref, got_ref, kept_ref, sent_ref, total):
    half, quarter = ring_place(core_ref[0], ring_ref[0])
    total[...] = right_ref[rows_at(half, 2 * RUN), :] + got_ref[...]
    kept_ref[...] = total[rows_at(quarter, RUN), :]
    sent_ref[...] = total[rows_at(1 - quarter, RUN), :]


def join_kernel(core_ref, ring_ref, mine_ref, got_ref, out_ref, *, which):
    at = ring_place(core_ref[0], ring_ref[0])[which]
    size = mine_ref.shape[0]
    out_ref[rows_at(at, size), :] = mine_ref[...]
    out_ref[rows_at(1 - at, size), :] = got_ref[...]


def pair_kernel(core_ref, own_ref, other_ref, after_ref, own_pair, other_pair):
    pair_up(own_pair, own_ref)
    pair_up(other_pair, other_ref)


def spread_kernel(core_ref, shares_ref, after_ref, out_ref, total, sems):
    share = shares_ref[0]
    for k in range(1, shares_ref.shape[0]):
        share += shares_ref[k]
    total[...] = share
    copies = [
        pltpu.make_async_copy(total, out_ref.at[k], sems.at[k]) for k in range(out_ref.shape[0])
    ]
    for copy in copies:
        copy.start()
    for copy in copies:
        copy.wait()


def multiply(x, y, emit):
    for a in range(PARTS):
        z = dot_split(both(x, span(a), EVERY), both(y, EVERY, slice(a * SUB, BLOCK)))
        for b in range(a, PARTS):
            emit(a, b, z[:, span(b - a)])


def root_kernel(
    core_ref, left_ref, left_got_ref, right_ref, right_got_ref, out_ref, root_ref,
    factor, m, n, z, y, t,
):
    core = core_ref[0]

    @pl.when(core == 0)
    def _():
        factor[:HALF, :] = left_ref[...]
        factor[HALF:, :] = left_got_ref[...]

    @pl.when(core == 1)
    def _():
        factor[:HALF, :] = right_got_ref[...]
        factor[HALF:, :] = right_ref[...]

    def blocks():
        for which in range(2):
            yield from load_half(factor, which * HALF, which)

    squares = jnp.zeros((SUB, SUB), F32)
    for a, b, x in blocks():
        squares += x * x * (1.0 if a == b else 2.0)
    scale = 1.0 / (jnp.sqrt(jnp.sum(squares)) + NORM_EPS)
    for a, b, x in blocks():
        put(m, a, b, x * scale)

    multiply(m, m, lambda a, b, p: put(n, a, b, p))

    def cube(a, b, p):
        mm, nn = block(m, a, b), block(n, a, b)
        put(z, a, b, (25.0 * mm - 10.0 * nn + p) * (1.0 / 16.0))
        put(y, a, b, (nn - 10.0 * mm) * (1.0 / 16.0))

    multiply(m, n, cube)
    multiply(z, y, lambda a, b, p: put(t, a, b, (25.0 / 16.0) * block(z, a, b) + p))

    multiply(t, t, lambda a, b, p: put(n, a, b, p))

    def cube_again(a, b, p):
        tt, nn = block(t, a, b), block(n, a, b)
        put(z, a, b, (25.0 * tt - 10.0 * nn + p) * (1.0 / 16.0))
        put(y, a, b, (15.0 * nn - 75.0 * tt - p) * (1.0 / 64.0))

    multiply(t, n, cube_again)

    def last(a, b, p):
        put(n, a, b, -0.3125 * block(t, a, b) - (125.0 / 256.0) * block(z, a, b) - 0.25 * p)

    multiply(z, y, last)

    def result(a, b, p):
        p = 1.25 * block(n, a, b) - (25.0 / 64.0) * block(m, a, b) - 0.25 * p
        out_ref[span(PLACE[(a, b)]), :] = p
        put(root_ref, a, b, p)

    multiply(m, n, result)


def early_kernel(core_ref, root_ref, own_ref, other_ref, out_ref):
    core = core_ref[0]

    def keep(rows, cols, x):
        high, low = split(x)
        out_ref[0, rows, cols] = high
        out_ref[1, rows, cols] = low

    @pl.when(core == 0)
    def _():
        for part in range(PARTS):
            for k, src in enumerate((own_ref, other_ref)):
                x = dot_split(both(root_ref, span(part), EVERY), both(src, EVERY, EVERY))
                keep(span(part), span(k, SIDE), x + LEVEL * get(src, span(part), EVERY))

    @pl.when(core == 1)
    def _():
        for part in range(PARTS):
            at = span(part)
            x = dot_split(both(other_ref, at, EVERY), both(root_ref, span(0, SIDE), span(1, SIDE)))
            x += dot_split(both(own_ref, at, EVERY), both(root_ref, span(1, SIDE), span(1, SIDE)))
            keep(at, span(0, SIDE), x + LEVEL * get(own_ref, at, EVERY))


LANES = 128


def late_kernel(core_ref, early_ref, got_ref, sq_ref, out_ref, left, right):
    core = core_ref[0]
    rows = BLOCK // out_ref.shape[0]
    lanes = SIDE // LANES
    count = SUB // rows

    def finish(product):
        total = jnp.zeros((4, LANES), F32)
        for part in range(PARTS):
            x = product(span(part)) + LEVEL * get(early_ref, span(part), span(0, SIDE))
            total += fold(x * x)
            for lane in range(lanes):
                out_ref[span(part, count), span(lane, rows), :] = x[:, span(lane, LANES)].reshape(
                    count, rows, LANES
                )
        stats = jnp.concatenate([sq_ref[...], total], 0)
        out_ref[:, lanes * rows :, :] = jnp.broadcast_to(
            stats[None], (out_ref.shape[0],) + stats.shape
        )

    @pl.when(core == 0)
    def _():
        for a in range(PARTS):
            for b in range(2):
                x = got_ref[span(PLACE[(min(a, b), max(a, b))]), :]
                high, low = split(x)
                right[0, span(a), span(b)] = high if a <= b else high.T
                right[1, span(a), span(b)] = low if a <= b else low.T
        finish(lambda at: dot_split(both(early_ref, at, EVERY), both(right, EVERY, EVERY)))

    @pl.when(core == 1)
    def _():
        for k, (a, b) in enumerate(ROOT_PAIRS):
            put(left, a, b, got_ref[span(k), :])
        finish(
            lambda at: dot_split(both(left, at, EVERY), both(early_ref, EVERY, span(0, SIDE)))
        )


STEP_TILES = 2


def base_kernel(flag_ref, coef_ref, m_ref, f_ref, n_ref, out_ref):
    for t in range(STEP_TILES):
        at = span(t, BLOCK)
        flag = flag_ref[pl.program_id(0) * STEP_TILES + t]
        prior = jnp.where(flag == 1, coef_ref[1] * f_ref[:, at], m_ref[:, at])
        out_ref[:, at] = (1.0 - DAMPING_COEFF) * prior + coef_ref[2] * n_ref[:, at]


def update_kernel(coef_ref, sums_ref, dir_ref, w_ref, b_ref, ow_out, om_out, ow, om, sems):
    gsq = jnp.sum(sums_ref[:4, :])
    dsq = jnp.sum(sums_ref[4:, :])
    pull = coef_ref[0] * (jnp.sqrt(gsq) / (jnp.sqrt(dsq) + NORM_EPS))
    rows = w_ref.shape[0]
    lanes = SIDE // LANES
    chunk = 2 * STEP_TILES
    copies = []
    for step in range(dir_ref.shape[0] // chunk):
        for k in range(step * chunk, (step + 1) * chunk):
            for lane in range(lanes):
                at = span(k * lanes + lane, LANES)
                moved = b_ref[:, at] - pull * dir_ref[k, span(lane, rows), :]
                om[:, at] = moved
                ow[:, at] = w_ref[:, at] + moved
        at = span(step, chunk * SIDE)
        pair = [
            pltpu.make_async_copy(ow.at[:, at], ow_out.at[:, at], sems.at[0, step]),
            pltpu.make_async_copy(om.at[:, at], om_out.at[:, at], sems.at[1, step]),
        ]
        for copy in pair:
            copy.start()
        copies += pair
    for copy in copies:
        copy.wait()


def stream(kernel, name, shape, ins, specs, outs):
    rows, cols = shape
    width = STEP_TILES * BLOCK
    wide = pl.BlockSpec((rows, width), lambda i: (0, i))
    cost = pl.CostEstimate(
        flops=4 * rows * cols, bytes_accessed=(len(ins) + outs) * 4 * rows * cols, transcendentals=0
    )
    return pl.pallas_call(
        kernel,
        grid=(cols // width,),
        out_shape=tuple(array(*shape) for _ in range(outs)),
        in_specs=specs + [wide] * (len(ins) - len(specs)),
        out_specs=(wide,) * outs,
        compiler_params=pltpu.CompilerParams(vmem_limit_bytes=16 << 20),
        cost_estimate=cost,
        name=name,
    )(*ins)


def ring_swapped(x, flips):
    cols = lax.axis_size("col")
    pairs = [
        (r * cols + c, (r ^ flips[c % 2]) * cols + c)
        for r in range(lax.axis_size("row"))
        for c in range(cols)
    ]
    return lax.ppermute(x, ("row", "col"), pairs)


def swapped(x, axis, flip):
    return lax.ppermute(x, axis, [(i, i ^ flip) for i in range(lax.axis_size(axis))])


def shards(gradient, weights, momentum, fresh_momentum, gaussian_noise, resample, step_index):
    rows, cols = gradient.shape
    col_pos = lax.axis_index("col")
    row_pos = lax.axis_index("row")
    core = (col_pos % 2).reshape(1).astype(jnp.int32)
    devices = lax.axis_size("col")
    by_core = [[c for c in range(devices) if c % 2 == k] for k in range(2)]

    phase = jnp.mod(step_index[0], CYCLE).astype(F32) / CYCLE
    rate = BASE_RATE * 0.5 * (1.0 + jnp.cos(jnp.pi * phase))
    coefs = jnp.stack([rate, jnp.sqrt(rate), jnp.sqrt(2.0 * DAMPING_COEFF * rate * HEAT_LEVEL)])
    flags = lax.dynamic_index_in_dim(resample, row_pos, 0, keepdims=False)
    pieces = gradient.reshape(rows, devices, SIDE).transpose(1, 0, 2)
    own = lax.all_to_all(pieces, "col", 0, 0).reshape(BLOCK, SIDE)
    other = swapped(own, "col", 1)
    pair = array(2, BLOCK, SIDE, dtype=BF16)
    pair_space = pltpu.VMEM((2, BLOCK, SIDE), BF16)
    (left,) = whole(own_kernel, "own", (array(HALF, SUB),), (core, own), [pair_space], products=0.16)
    left, grad_sq = whole(
        left_kernel,
        "left",
        (array(HALF, SUB), array(4, LANES)),
        (core, other, left),
        [pair_space, pltpu.VMEM((HALF, SUB), F32), pltpu.SemaphoreType.DMA((1,))],
        products=0.16,
        far=(0,),
    )
    chips = devices // 2
    shares = lax.all_to_all(
        left.reshape(chips, HALF // chips, SUB), "col", 0, 0, axis_index_groups=by_core
    )

    ring = row_pos.reshape(1).astype(jnp.int32)
    two, one = array(2 * RUN, SUB), array(RUN, SUB)
    right, sent = whole(
        right_kernel,
        "right",
        (array(HALF, SUB), two),
        (core, ring, own, other, grad_sq),
        [pair_space, pair_space, pltpu.VMEM((2, SIDE, BLOCK), BF16)],
        products=0.3,
        scalars=2,
    )
    got = ring_swapped(sent, HALF_FLIPS)
    kept, sent = whole(
        halve_kernel,
        "halve",
        (one, one),
        (core, ring, right, got),
        [pltpu.VMEM((2 * RUN, SUB), F32)],
        scalars=2,
    )
    mine = kept + ring_swapped(sent, QUARTER_FLIPS)
    (share,) = whole(
        spread_kernel,
        "spread",
        (array(*shares.shape),),
        (core, shares, kept[:8]),
        [pltpu.VMEM(shares.shape[1:], F32), pltpu.SemaphoreType.DMA((chips,))],
        far=(0,),
    )
    left = lax.all_to_all(share, "col", 0, 0, axis_index_groups=by_core).reshape(HALF, SUB)
    own_pair, other_pair = whole(
        pair_kernel, "pairs", (pair, pair), (core, own, other, mine[:8]), products=0.1
    )
    got = ring_swapped(mine, QUARTER_FLIPS)
    got, own_pair, other_pair = lax.optimization_barrier((got, own_pair, other_pair))
    (right,) = whole(
        functools.partial(join_kernel, which=1), "join", (two,), (core, ring, mine, got), scalars=2
    )
    right, momentum, fresh_momentum, gaussian_noise = lax.optimization_barrier(
        (right, momentum, fresh_momentum, gaussian_noise)
    )
    (base,) = stream(
        base_kernel,
        "base",
        (rows, cols),
        (flags, coefs, momentum, fresh_momentum, gaussian_noise),
        [smem(), smem()],
        1,
    )
    got = ring_swapped(right, HALF_FLIPS)
    got, base = lax.optimization_barrier((got, base))
    (right,) = whole(
        functools.partial(join_kernel, which=0),
        "place",
        (array(HALF, SUB),),
        (core, ring, right, got),
        scalars=2,
    )
    right_got = lax.ppermute(right, "col", [(i, i + 1) for i in range(0, devices, 2)])
    left_got = lax.ppermute(left, "col", [(i + 1, i) for i in range(0, devices, 2)])
    packed, root = whole(
        root_kernel,
        "root",
        (array(PACKED, SUB), array(2, BLOCK, BLOCK, dtype=BF16)),
        (core, left, left_got, right, right_got),
        [pltpu.VMEM((2 * HALF, SUB), F32)] + [pltpu.VMEM((2, BLOCK, BLOCK), BF16)] * 5,
        limit=30,
        products=7 * 0.625,
    )
    other_root = swapped(packed, "col", 1)
    (early,) = whole(
        early_kernel,
        "early",
        (array(2, BLOCK, BLOCK, dtype=BF16),),
        (core, root, own_pair, other_pair),
        products=1.0,
    )
    (message,) = whole(
        late_kernel,
        "late",
        (array(devices, rows * SIDE // LANES + 8, LANES),),
        (core, early, other_root, grad_sq),
        [pltpu.VMEM((2, BLOCK, BLOCK), BF16), pltpu.VMEM((2, BLOCK, SIDE), BF16)],
        products=0.5,
    )
    message = lax.all_to_all(message, "col", 0, 0)
    sums = jnp.sum(message[:, -8:, :], axis=0)
    total = lax.axis_size("row")
    got = [
        lax.ppermute(sums, "row", [(i, (i + k) % total) for i in range(total)])
        for k in range(1, total)
    ]
    sums = sums + sum(got)
    chunks = cols // (STEP_TILES * BLOCK)
    return whole(
        update_kernel,
        "update",
        (array(rows, cols), array(rows, cols)),
        (coefs, sums, message, weights, base),
        [
            pltpu.VMEM((rows, cols), F32),
            pltpu.VMEM((rows, cols), F32),
            pltpu.SemaphoreType.DMA((2, chunks)),
        ],
        far=(0, 1),
    )


def solution(mesh):
    wide = P(("row", "col"), None)
    in_specs = (wide, wide, wide, wide, wide, P(), P())
    return jax.shard_map(
        shards, mesh=mesh, in_specs=in_specs, out_specs=(wide, wide), check_vma=False
    )
```

```python
import functools

import jax
import jax.numpy as jnp
from jax import lax
from jax.experimental import pallas as pl
from jax.experimental.pallas import tpu as pltpu
from jax.sharding import PartitionSpec as P

BLOCK = 1024
CYCLE = 1000
NORM_EPS = 1e-06
BASE_RATE = 0.5
DAMPING_COEFF = 0.1
HEAT_LEVEL = 1.0

SUB = 256
QUARTER = SUB // 2
PARTS = BLOCK // SUB
SIDE = BLOCK // 2
DIAGONAL = ((0, 1), (2, 3))
OTHERS = (((0, 1), (0, 2), (1, 2)), ((2, 3), (3, 0), (3, 1)))
HALF = 3 * QUARTER + 3 * SUB
ROOT_PAIRS = [(a, b) for b in range(PARTS) for a in range(b + 1)]
PLACE = {pair: k for k, pair in enumerate(ROOT_PAIRS)}
PACKED = len(ROOT_PAIRS) * SUB
LEVEL = 125.0 / 64.0
F32, BF16 = jnp.float32, jnp.bfloat16


def vmem():
    return pl.BlockSpec(memory_space=pltpu.VMEM)


def smem():
    return pl.BlockSpec(memory_space=pltpu.SMEM)


def array(*shape, dtype=F32):
    return jax.ShapeDtypeStruct(shape, dtype)


def whole(kernel, name, outs, ins, scratch=(), limit=16, products=0.0, scalars=1, far=()):
    cost = pl.CostEstimate(
        flops=int(products * 6 * BLOCK**3), bytes_accessed=8 << 20, transcendentals=0
    )
    return pl.pallas_call(
        kernel,
        out_shape=outs,
        in_specs=[smem()] * scalars + [vmem() for _ in ins[scalars:]],
        out_specs=tuple(
            pl.BlockSpec(memory_space=pltpu.HBM) if k in far else vmem() for k in range(len(outs))
        ),
        scratch_shapes=list(scratch),
        compiler_params=pltpu.CompilerParams(vmem_limit_bytes=limit << 20),
        cost_estimate=cost,
        name=name,
    )(*ins)


def span(k, size=SUB):
    return slice(k * size, (k + 1) * size)


def split(x):
    high = x.astype(BF16)
    return high, (x - high.astype(F32)).astype(BF16)


def dot(x, y, dims=((1,), (0,))):
    return lax.dot_general(x, y, (dims, ((), ())), preferred_element_type=F32)


def dot_split(x, y, dims=((1,), (0,))):
    x = jnp.concatenate([x[0], x[0], x[1]], dims[0][0])
    y = jnp.concatenate([y[0], y[1], y[0]], dims[1][0])
    return dot(x, y, dims)


def both(ref, *at):
    return [ref[(k,) + at] for k in range(2)]


def put(dst, a, b, x):
    high, low = split(x)
    dst[0, span(a), span(b)] = high
    dst[1, span(a), span(b)] = low
    if a != b:
        dst[0, span(b), span(a)] = high.T
        dst[1, span(b), span(a)] = low.T


def get(src, *at):
    return src[(0,) + at].astype(F32) + src[(1,) + at].astype(F32)


def block(src, a, b):
    return get(src, span(a), span(b))


def fold(x):
    total = jnp.sum(x.reshape(x.shape[0] // 8, 8, x.shape[1]), axis=0)
    total = sum(total[:, span(k, 128)] for k in range(x.shape[1] // 128))
    return total[:4] + total[4:]


EVERY = slice(None)


def store_diagonal(dst, k, x, part=None):
    pieces = (
        (span(k, QUARTER), EVERY, x[:QUARTER, :]),
        (span(2, QUARTER), span(k, QUARTER), x[QUARTER:, QUARTER:]),
    )
    for rows, cols, piece in pieces:
        dst[rows, cols] = piece if part is None else part[rows, cols] + piece


def store_other(dst, k, x, part=None):
    start = 3 * QUARTER + k * SUB
    rows = slice(start, start + x.shape[0])
    dst[rows, :] = x if part is None else part[rows, :] + x


def load_half(src, at, which):
    for k, a in enumerate(DIAGONAL[which]):
        top = src[at + k * QUARTER : at + (k + 1) * QUARTER, :]
        corner = src[at + 2 * QUARTER : at + 3 * QUARTER, span(k, QUARTER)]
        bottom = jnp.concatenate([top[:, QUARTER:].T, corner], 1)
        yield a, a, jnp.concatenate([top, bottom], 0)
    for k, (a, b) in enumerate(OTHERS[which]):
        start = at + 3 * QUARTER + k * SUB
        yield a, b, src[start : start + SUB, :]


def left_blocks(core, src, dst, part=None):
    def rows(first, end, other_first, other_end):
        return dot_split(
            both(src, slice(first * SUB, end * SUB), EVERY),
            both(src, slice(other_first * SUB, other_end * SUB), EVERY),
            ((1,), (1,)),
        )

    @pl.when(core == 0)
    def _():
        store_diagonal(dst, 0, rows(0, 1, 0, 1), part)
        z = rows(0, 2, 1, 2)
        store_other(dst, 0, z[:SUB], part)
        store_diagonal(dst, 1, z[SUB:], part)
        store_other(dst, 1, rows(0, 2, 2, 3), part)

    @pl.when(core == 1)
    def _():
        store_diagonal(dst, 0, rows(2, 3, 2, 3), part)
        z = rows(2, 4, 3, 4)
        store_other(dst, 0, z[:SUB], part)
        store_diagonal(dst, 1, z[SUB:], part)
        z = rows(3, 4, 0, 2)
        store_other(dst, 1, z[:, span(0)], part)
        store_other(dst, 2, z[:, span(1)], part)


def pair_up(dst, src):
    for part in range(PARTS):
        high, low = split(src[span(part), :])
        dst[0, span(part), :] = high
        dst[1, span(part), :] = low


def turn(dst, src):
    for part in range(PARTS):
        for k in range(2):
            dst[k, :, span(part)] = src[k, span(part), :].T


def own_kernel(core_ref, own_ref, left_ref, pair):
    pair_up(pair, own_ref)
    left_blocks(core_ref[0], pair, left_ref)


def left_kernel(core_ref, other_ref, part_ref, left_ref, sq_ref, pair, total, sem):
    pair_up(pair, other_ref)
    left_blocks(core_ref[0], pair, total, part_ref)
    copy = pltpu.make_async_copy(total, left_ref, sem.at[0])
    copy.start()
    sq_ref[...] = fold(other_ref[...] * other_ref[...])
    copy.wait()


RUN = HALF // 4
HALF_FLIPS, QUARTER_FLIPS = (1, 3), (3, 1)


def ring_place(core, pos):
    near, far = pos % 2, pos // 2
    return jnp.where(core == 0, near ^ far, far), jnp.where(core == 0, far, near)


def rows_at(k, size):
    return pl.ds(pl.multiple_of(k * size, size), size)


def right_kernel(
    core_ref, ring_ref, own_ref, other_ref, after_ref, right_ref, sent_ref, own_pair, other_pair, turned
):
    core = core_ref[0]
    pair_up(own_pair, own_ref)
    pair_up(other_pair, other_ref)
    turn(turned, own_pair)
    head = slice(0, SUB)
    store_diagonal(
        right_ref, 0, dot_split(both(turned, head, EVERY), both(own_pair, EVERY, head))
    )
    z = dot_split(both(turned, EVERY, EVERY), both(own_pair, EVERY, span(1)))
    store_other(right_ref, 0, z[:SUB])
    store_diagonal(right_ref, 1, z[SUB:])

    @pl.when(core == 0)
    def _():
        z = dot_split(both(turned, EVERY, EVERY), both(other_pair, EVERY, span(0)))
        store_other(right_ref, 1, z)

    @pl.when(core == 1)
    def _():
        z = dot_split(both(turned, span(1), EVERY), both(other_pair, EVERY, EVERY))
        store_other(right_ref, 1, z[:, span(0)])
        store_other(right_ref, 2, z[:, span(1)])

    half, _ = ring_place(core, ring_ref[0])
    sent_ref[...] = right_ref[rows_at(1 - half, 2 * RUN), :]


def halve_kernel(core_ref, ring_ref, right_ref, got_ref, kept_ref, sent_ref, total):
    half, quarter = ring_place(core_ref[0], ring_ref[0])
    total[...] = right_ref[rows_at(half, 2 * RUN), :] + got_ref[...]
    kept_ref[...] = total[rows_at(quarter, RUN), :]
    sent_ref[...] = total[rows_at(1 - quarter, RUN), :]


def join_kernel(core_ref, ring_ref, mine_ref, got_ref, out_ref, *, which):
    at = ring_place(core_ref[0], ring_ref[0])[which]
    size = mine_ref.shape[0]
    out_ref[rows_at(at, size), :] = mine_ref[...]
    out_ref[rows_at(1 - at, size), :] = got_ref[...]


def pair_kernel(core_ref, own_ref, other_ref, after_ref, own_pair, other_pair):
    pair_up(own_pair, own_ref)
    pair_up(other_pair, other_ref)


def spread_kernel(core_ref, shares_ref, after_ref, out_ref, total, sems):
    share = shares_ref[0]
    for k in range(1, shares_ref.shape[0]):
        share += shares_ref[k]
    total[...] = share
    copies = [
        pltpu.make_async_copy(total, out_ref.at[k], sems.at[k]) for k in range(out_ref.shape[0])
    ]
    for copy in copies:
        copy.start()
    for copy in copies:
        copy.wait()


def multiply(x, y, emit):
    for a in range(PARTS):
        z = dot_split(both(x, span(a), EVERY), both(y, EVERY, slice(a * SUB, BLOCK)))
        for b in range(a, PARTS):
            emit(a, b, z[:, span(b - a)])


def root_kernel(
    core_ref, left_ref, left_got_ref, right_ref, right_got_ref, out_ref, root_ref,
    factor, m, n, z, y, t,
):
    core = core_ref[0]

    @pl.when(core == 0)
    def _():
        factor[:HALF, :] = left_ref[...]
        factor[HALF:, :] = left_got_ref[...]

    @pl.when(core == 1)
    def _():
        factor[:HALF, :] = right_got_ref[...]
        factor[HALF:, :] = right_ref[...]

    def blocks():
        for which in range(2):
            yield from load_half(factor, which * HALF, which)

    squares = jnp.zeros((SUB, SUB), F32)
    for a, b, x in blocks():
        squares += x * x * (1.0 if a == b else 2.0)
    scale = 1.0 / (jnp.sqrt(jnp.sum(squares)) + NORM_EPS)
    for a, b, x in blocks():
        put(m, a, b, x * scale)

    multiply(m, m, lambda a, b, p: put(n, a, b, p))

    def cube(a, b, p):
        mm, nn = block(m, a, b), block(n, a, b)
        put(z, a, b, (25.0 * mm - 10.0 * nn + p) * (1.0 / 16.0))
        put(y, a, b, (nn - 10.0 * mm) * (1.0 / 16.0))

    multiply(m, n, cube)
    multiply(z, y, lambda a, b, p: put(t, a, b, (25.0 / 16.0) * block(z, a, b) + p))

    multiply(t, t, lambda a, b, p: put(n, a, b, p))

    def cube_again(a, b, p):
        tt, nn = block(t, a, b), block(n, a, b)
        put(z, a, b, (25.0 * tt - 10.0 * nn + p) * (1.0 / 16.0))
        put(y, a, b, (15.0 * nn - 75.0 * tt - p) * (1.0 / 64.0))

    multiply(t, n, cube_again)

    def last(a, b, p):
        put(n, a, b, -0.3125 * block(t, a, b) - (125.0 / 256.0) * block(z, a, b) - 0.25 * p)

    multiply(z, y, last)

    def result(a, b, p):
        p = 1.25 * block(n, a, b) - (25.0 / 64.0) * block(m, a, b) - 0.25 * p
        out_ref[span(PLACE[(a, b)]), :] = p
        put(root_ref, a, b, p)

    multiply(m, n, result)


def early_kernel(core_ref, root_ref, own_ref, other_ref, out_ref):
    core = core_ref[0]

    def keep(rows, cols, x):
        high, low = split(x)
        out_ref[0, rows, cols] = high
        out_ref[1, rows, cols] = low

    @pl.when(core == 0)
    def _():
        for part in range(PARTS):
            for k, src in enumerate((own_ref, other_ref)):
                x = dot_split(both(root_ref, span(part), EVERY), both(src, EVERY, EVERY))
                keep(span(part), span(k, SIDE), x + LEVEL * get(src, span(part), EVERY))

    @pl.when(core == 1)
    def _():
        for part in range(PARTS):
            at = span(part)
            x = dot_split(both(other_ref, at, EVERY), both(root_ref, span(0, SIDE), span(1, SIDE)))
            x += dot_split(both(own_ref, at, EVERY), both(root_ref, span(1, SIDE), span(1, SIDE)))
            keep(at, span(0, SIDE), x + LEVEL * get(own_ref, at, EVERY))


LANES = 128


def late_kernel(core_ref, early_ref, got_ref, sq_ref, out_ref, left, right):
    core = core_ref[0]
    rows = BLOCK // out_ref.shape[0]
    lanes = SIDE // LANES
    count = SUB // rows

    def finish(product):
        total = jnp.zeros((4, LANES), F32)
        for part in range(PARTS):
            x = product(span(part)) + LEVEL * get(early_ref, span(part), span(0, SIDE))
            total += fold(x * x)
            for lane in range(lanes):
                out_ref[span(part, count), span(lane, rows), :] = x[:, span(lane, LANES)].reshape(
                    count, rows, LANES
                )
        stats = jnp.concatenate([sq_ref[...], total], 0)
        out_ref[:, lanes * rows :, :] = jnp.broadcast_to(
            stats[None], (out_ref.shape[0],) + stats.shape
        )

    @pl.when(core == 0)
    def _():
        for a in range(PARTS):
            for b in range(2):
                x = got_ref[span(PLACE[(min(a, b), max(a, b))]), :]
                high, low = split(x)
                right[0, span(a), span(b)] = high if a <= b else high.T
                right[1, span(a), span(b)] = low if a <= b else low.T
        finish(lambda at: dot_split(both(early_ref, at, EVERY), both(right, EVERY, EVERY)))

    @pl.when(core == 1)
    def _():
        for k, (a, b) in enumerate(ROOT_PAIRS):
            put(left, a, b, got_ref[span(k), :])
        finish(
            lambda at: dot_split(both(left, at, EVERY), both(early_ref, EVERY, span(0, SIDE)))
        )


STEP_TILES = 2


def base_kernel(flag_ref, coef_ref, m_ref, f_ref, n_ref, out_ref):
    for t in range(STEP_TILES):
        at = span(t, BLOCK)
        flag = flag_ref[pl.program_id(0) * STEP_TILES + t]
        prior = jnp.where(flag == 1, coef_ref[1] * f_ref[:, at], m_ref[:, at])
        out_ref[:, at] = (1.0 - DAMPING_COEFF) * prior + coef_ref[2] * n_ref[:, at]


def update_kernel(coef_ref, sums_ref, dir_ref, w_ref, b_ref, ow_out, om_out, ow, om, sems):
    gsq = jnp.sum(sums_ref[:4, :])
    dsq = jnp.sum(sums_ref[4:, :])
    pull = coef_ref[0] * (jnp.sqrt(gsq) / (jnp.sqrt(dsq) + NORM_EPS))
    rows = w_ref.shape[0]
    lanes = SIDE // LANES
    chunk = 2 * STEP_TILES
    copies = []
    for step in range(dir_ref.shape[0] // chunk):
        for k in range(step * chunk, (step + 1) * chunk):
            for lane in range(lanes):
                at = span(k * lanes + lane, LANES)
                moved = b_ref[:, at] - pull * dir_ref[k, span(lane, rows), :]
                om[:, at] = moved
                ow[:, at] = w_ref[:, at] + moved
        at = span(step, chunk * SIDE)
        pair = [
            pltpu.make_async_copy(ow.at[:, at], ow_out.at[:, at], sems.at[0, step]),
            pltpu.make_async_copy(om.at[:, at], om_out.at[:, at], sems.at[1, step]),
        ]
        for copy in pair:
            copy.start()
        copies += pair
    for copy in copies:
        copy.wait()


def stream(kernel, name, shape, ins, specs, outs):
    rows, cols = shape
    width = STEP_TILES * BLOCK
    wide = pl.BlockSpec((rows, width), lambda i: (0, i))
    cost = pl.CostEstimate(
        flops=4 * rows * cols, bytes_accessed=(len(ins) + outs) * 4 * rows * cols, transcendentals=0
    )
    return pl.pallas_call(
        kernel,
        grid=(cols // width,),
        out_shape=tuple(array(*shape) for _ in range(outs)),
        in_specs=specs + [wide] * (len(ins) - len(specs)),
        out_specs=(wide,) * outs,
        compiler_params=pltpu.CompilerParams(vmem_limit_bytes=16 << 20),
        cost_estimate=cost,
        name=name,
    )(*ins)


def ring_swapped(x, flips):
    cols = lax.axis_size("col")
    pairs = [
        (r * cols + c, (r ^ flips[c % 2]) * cols + c)
        for r in range(lax.axis_size("row"))
        for c in range(cols)
    ]
    return lax.ppermute(x, ("row", "col"), pairs)


def swapped(x, axis, flip):
    return lax.ppermute(x, axis, [(i, i ^ flip) for i in range(lax.axis_size(axis))])


def shards(gradient, weights, momentum, fresh_momentum, gaussian_noise, resample, step_index):
    rows, cols = gradient.shape
    col_pos = lax.axis_index("col")
    row_pos = lax.axis_index("row")
    core = (col_pos % 2).reshape(1).astype(jnp.int32)
    devices = lax.axis_size("col")
    by_core = [[c for c in range(devices) if c % 2 == k] for k in range(2)]

    phase = jnp.mod(step_index[0], CYCLE).astype(F32) / CYCLE
    rate = BASE_RATE * 0.5 * (1.0 + jnp.cos(jnp.pi * phase))
    coefs = jnp.stack([rate, jnp.sqrt(rate), jnp.sqrt(2.0 * DAMPING_COEFF * rate * HEAT_LEVEL)])
    flags = lax.dynamic_index_in_dim(resample, row_pos, 0, keepdims=False)
    pieces = gradient.reshape(rows, devices, SIDE).transpose(1, 0, 2)
    own = lax.all_to_all(pieces, "col", 0, 0).reshape(BLOCK, SIDE)
    other = swapped(own, "col", 1)
    pair = array(2, BLOCK, SIDE, dtype=BF16)
    pair_space = pltpu.VMEM((2, BLOCK, SIDE), BF16)
    (left,) = whole(own_kernel, "own", (array(HALF, SUB),), (core, own), [pair_space], products=0.16)
    left, grad_sq = whole(
        left_kernel,
        "left",
        (array(HALF, SUB), array(4, LANES)),
        (core, other, left),
        [pair_space, pltpu.VMEM((HALF, SUB), F32), pltpu.SemaphoreType.DMA((1,))],
        products=0.16,
        far=(0,),
    )
    chips = devices // 2
    shares = lax.all_to_all(
        left.reshape(chips, HALF // chips, SUB), "col", 0, 0, axis_index_groups=by_core
    )

    ring = row_pos.reshape(1).astype(jnp.int32)
    two, one = array(2 * RUN, SUB), array(RUN, SUB)
    right, sent = whole(
        right_kernel,
        "right",
        (array(HALF, SUB), two),
        (core, ring, own, other, grad_sq),
        [pair_space, pair_space, pltpu.VMEM((2, SIDE, BLOCK), BF16)],
        products=0.3,
        scalars=2,
    )
    got = ring_swapped(sent, HALF_FLIPS)
    own_pair, other_pair = whole(
        pair_kernel, "pairs", (pair, pair), (core, own, other, sent[:8]), products=0.1
    )
    got, own_pair, other_pair = lax.optimization_barrier((got, own_pair, other_pair))
    kept, sent = whole(
        halve_kernel,
        "halve",
        (one, one),
        (core, ring, right, got),
        [pltpu.VMEM((2 * RUN, SUB), F32)],
        scalars=2,
    )
    mine = kept + ring_swapped(sent, QUARTER_FLIPS)
    (share,) = whole(
        spread_kernel,
        "spread",
        (array(*shares.shape),),
        (core, shares, kept[:8]),
        [pltpu.VMEM(shares.shape[1:], F32), pltpu.SemaphoreType.DMA((chips,))],
        far=(0,),
    )
    left = lax.all_to_all(share, "col", 0, 0, axis_index_groups=by_core).reshape(HALF, SUB)
    got = ring_swapped(mine, QUARTER_FLIPS)
    (right,) = whole(
        functools.partial(join_kernel, which=1), "join", (two,), (core, ring, mine, got), scalars=2
    )
    right, momentum, fresh_momentum, gaussian_noise = lax.optimization_barrier(
        (right, momentum, fresh_momentum, gaussian_noise)
    )
    (base,) = stream(
        base_kernel,
        "base",
        (rows, cols),
        (flags, coefs, momentum, fresh_momentum, gaussian_noise),
        [smem(), smem()],
        1,
    )
    got = ring_swapped(right, HALF_FLIPS)
    got, base = lax.optimization_barrier((got, base))
    (right,) = whole(
        functools.partial(join_kernel, which=0),
        "place",
        (array(HALF, SUB),),
        (core, ring, right, got),
        scalars=2,
    )
    right_got = lax.ppermute(right, "col", [(i, i + 1) for i in range(0, devices, 2)])
    left_got = lax.ppermute(left, "col", [(i + 1, i) for i in range(0, devices, 2)])
    packed, root = whole(
        root_kernel,
        "root",
        (array(PACKED, SUB), array(2, BLOCK, BLOCK, dtype=BF16)),
        (core, left, left_got, right, right_got),
        [pltpu.VMEM((2 * HALF, SUB), F32)] + [pltpu.VMEM((2, BLOCK, BLOCK), BF16)] * 5,
        limit=30,
        products=7 * 0.625,
    )
    other_root = swapped(packed, "col", 1)
    (early,) = whole(
        early_kernel,
        "early",
        (array(2, BLOCK, BLOCK, dtype=BF16),),
        (core, root, own_pair, other_pair),
        products=1.0,
    )
    (message,) = whole(
        late_kernel,
        "late",
        (array(devices, rows * SIDE // LANES + 8, LANES),),
        (core, early, other_root, grad_sq),
        [pltpu.VMEM((2, BLOCK, BLOCK), BF16), pltpu.VMEM((2, BLOCK, SIDE), BF16)],
        products=0.5,
    )
    message = lax.all_to_all(message, "col", 0, 0)
    sums = jnp.sum(message[:, -8:, :], axis=0)
    total = lax.axis_size("row")
    got = [
        lax.ppermute(sums, "row", [(i, (i + k) % total) for i in range(total)])
        for k in range(1, total)
    ]
    sums = sums + sum(got)
    chunks = cols // (STEP_TILES * BLOCK)
    return whole(
        update_kernel,
        "update",
        (array(rows, cols), array(rows, cols)),
        (coefs, sums, message, weights, base),
        [
            pltpu.VMEM((rows, cols), F32),
            pltpu.VMEM((rows, cols), F32),
            pltpu.SemaphoreType.DMA((2, chunks)),
        ],
        far=(0, 1),
    )


def solution(mesh):
    wide = P(("row", "col"), None)
    in_specs = (wide, wide, wide, wide, wide, P(), P())
    return jax.shard_map(
        shards, mesh=mesh, in_specs=in_specs, out_specs=(wide, wide), check_vma=False
    )
```

```python
import functools

import jax
import jax.numpy as jnp
from jax import lax
from jax.experimental import pallas as pl
from jax.experimental.pallas import tpu as pltpu
from jax.sharding import PartitionSpec as P

BLOCK = 1024
CYCLE = 1000
NORM_EPS = 1e-06
BASE_RATE = 0.5
DAMPING_COEFF = 0.1
HEAT_LEVEL = 1.0

SUB = 256
QUARTER = SUB // 2
PARTS = BLOCK // SUB
SIDE = BLOCK // 2
DIAGONAL = ((0, 1), (2, 3))
OTHERS = (((0, 1), (0, 2), (1, 2)), ((2, 3), (3, 0), (3, 1)))
HALF = 3 * QUARTER + 3 * SUB
ROOT_PAIRS = [(a, b) for b in range(PARTS) for a in range(b + 1)]
PLACE = {pair: k for k, pair in enumerate(ROOT_PAIRS)}
PACKED = len(ROOT_PAIRS) * SUB
LEVEL = 125.0 / 64.0
F32, BF16 = jnp.float32, jnp.bfloat16


def vmem():
    return pl.BlockSpec(memory_space=pltpu.VMEM)


def smem():
    return pl.BlockSpec(memory_space=pltpu.SMEM)


def array(*shape, dtype=F32):
    return jax.ShapeDtypeStruct(shape, dtype)


def whole(kernel, name, outs, ins, scratch=(), limit=16, products=0.0, scalars=1, far=()):
    cost = pl.CostEstimate(
        flops=int(products * 6 * BLOCK**3), bytes_accessed=8 << 20, transcendentals=0
    )
    return pl.pallas_call(
        kernel,
        out_shape=outs,
        in_specs=[smem()] * scalars + [vmem() for _ in ins[scalars:]],
        out_specs=tuple(
            pl.BlockSpec(memory_space=pltpu.HBM) if k in far else vmem() for k in range(len(outs))
        ),
        scratch_shapes=list(scratch),
        compiler_params=pltpu.CompilerParams(vmem_limit_bytes=limit << 20),
        cost_estimate=cost,
        name=name,
    )(*ins)


def span(k, size=SUB):
    return slice(k * size, (k + 1) * size)


def split(x):
    high = x.astype(BF16)
    return high, (x - high.astype(F32)).astype(BF16)


def dot(x, y, dims=((1,), (0,))):
    return lax.dot_general(x, y, (dims, ((), ())), preferred_element_type=F32)


def dot_split(x, y, dims=((1,), (0,))):
    x = jnp.concatenate([x[0], x[0], x[1]], dims[0][0])
    y = jnp.concatenate([y[0], y[1], y[0]], dims[1][0])
    return dot(x, y, dims)


def both(ref, *at):
    return [ref[(k,) + at] for k in range(2)]


def put(dst, a, b, x):
    high, low = split(x)
    dst[0, span(a), span(b)] = high
    dst[1, span(a), span(b)] = low
    if a != b:
        dst[0, span(b), span(a)] = high.T
        dst[1, span(b), span(a)] = low.T


def get(src, *at):
    return src[(0,) + at].astype(F32) + src[(1,) + at].astype(F32)


def block(src, a, b):
    return get(src, span(a), span(b))


def fold(x):
    total = jnp.sum(x.reshape(x.shape[0] // 8, 8, x.shape[1]), axis=0)
    total = sum(total[:, span(k, 128)] for k in range(x.shape[1] // 128))
    return total[:4] + total[4:]


EVERY = slice(None)


def store_diagonal(dst, k, x, part=None):
    pieces = (
        (span(k, QUARTER), EVERY, x[:QUARTER, :]),
        (span(2, QUARTER), span(k, QUARTER), x[QUARTER:, QUARTER:]),
    )
    for rows, cols, piece in pieces:
        dst[rows, cols] = piece if part is None else part[rows, cols] + piece


def store_other(dst, k, x, part=None):
    start = 3 * QUARTER + k * SUB
    rows = slice(start, start + x.shape[0])
    dst[rows, :] = x if part is None else part[rows, :] + x


def load_half(src, at, which):
    for k, a in enumerate(DIAGONAL[which]):
        top = src[at + k * QUARTER : at + (k + 1) * QUARTER, :]
        corner = src[at + 2 * QUARTER : at + 3 * QUARTER, span(k, QUARTER)]
        bottom = jnp.concatenate([top[:, QUARTER:].T, corner], 1)
        yield a, a, jnp.concatenate([top, bottom], 0)
    for k, (a, b) in enumerate(OTHERS[which]):
        start = at + 3 * QUARTER + k * SUB
        yield a, b, src[start : start + SUB, :]


def left_blocks(core, src, dst, part=None):
    def rows(first, end, other_first, other_end):
        return dot_split(
            both(src, slice(first * SUB, end * SUB), EVERY),
            both(src, slice(other_first * SUB, other_end * SUB), EVERY),
            ((1,), (1,)),
        )

    @pl.when(core == 0)
    def _():
        store_diagonal(dst, 0, rows(0, 1, 0, 1), part)
        z = rows(0, 2, 1, 2)
        store_other(dst, 0, z[:SUB], part)
        store_diagonal(dst, 1, z[SUB:], part)
        store_other(dst, 1, rows(0, 2, 2, 3), part)

    @pl.when(core == 1)
    def _():
        store_diagonal(dst, 0, rows(2, 3, 2, 3), part)
        z = rows(2, 4, 3, 4)
        store_other(dst, 0, z[:SUB], part)
        store_diagonal(dst, 1, z[SUB:], part)
        z = rows(3, 4, 0, 2)
        store_other(dst, 1, z[:, span(0)], part)
        store_other(dst, 2, z[:, span(1)], part)


def pair_up(dst, src):
    for part in range(PARTS):
        high, low = split(src[span(part), :])
        dst[0, span(part), :] = high
        dst[1, span(part), :] = low


def turn(dst, src):
    for part in range(PARTS):
        for k in range(2):
            dst[k, :, span(part)] = src[k, span(part), :].T


def own_kernel(core_ref, own_ref, left_ref, pair):
    pair_up(pair, own_ref)
    left_blocks(core_ref[0], pair, left_ref)


def left_kernel(core_ref, other_ref, part_ref, left_ref, sq_ref, pair, total, sems):
    pair_up(pair, other_ref)
    left_blocks(core_ref[0], pair, total, part_ref)
    chips, rows, _ = left_ref.shape
    copies = [
        pltpu.make_async_copy(total.at[span(k, rows)], left_ref.at[k], sems.at[k])
        for k in range(chips)
    ]
    for copy in copies:
        copy.start()
    sq_ref[...] = fold(other_ref[...] * other_ref[...])
    for copy in copies:
        copy.wait()


RUN = HALF // 4
HALF_FLIPS, QUARTER_FLIPS = (1, 3), (3, 1)


def ring_place(core, pos):
    near, far = pos % 2, pos // 2
    return jnp.where(core == 0, near ^ far, far), jnp.where(core == 0, far, near)


def rows_at(k, size):
    return pl.ds(pl.multiple_of(k * size, size), size)


def right_kernel(
    core_ref, ring_ref, own_ref, other_ref, after_ref, right_ref, sent_ref, own_pair, other_pair, turned
):
    core = core_ref[0]
    pair_up(own_pair, own_ref)
    pair_up(other_pair, other_ref)
    turn(turned, own_pair)
    head = slice(0, SUB)
    store_diagonal(
        right_ref, 0, dot_split(both(turned, head, EVERY), both(own_pair, EVERY, head))
    )
    z = dot_split(both(turned, EVERY, EVERY), both(own_pair, EVERY, span(1)))
    store_other(right_ref, 0, z[:SUB])
    store_diagonal(right_ref, 1, z[SUB:])

    @pl.when(core == 0)
    def _():
        z = dot_split(both(turned, EVERY, EVERY), both(other_pair, EVERY, span(0)))
        store_other(right_ref, 1, z)

    @pl.when(core == 1)
    def _():
        z = dot_split(both(turned, span(1), EVERY), both(other_pair, EVERY, EVERY))
        store_other(right_ref, 1, z[:, span(0)])
        store_other(right_ref, 2, z[:, span(1)])

    half, _ = ring_place(core, ring_ref[0])
    sent_ref[...] = right_ref[rows_at(1 - half, 2 * RUN), :]


def halve_kernel(core_ref, ring_ref, right_ref, got_ref, kept_ref, sent_ref, total):
    half, quarter = ring_place(core_ref[0], ring_ref[0])
    total[...] = right_ref[rows_at(half, 2 * RUN), :] + got_ref[...]
    kept_ref[...] = total[rows_at(quarter, RUN), :]
    sent_ref[...] = total[rows_at(1 - quarter, RUN), :]


def join_kernel(core_ref, ring_ref, mine_ref, got_ref, out_ref, *, which):
    at = ring_place(core_ref[0], ring_ref[0])[which]
    size = mine_ref.shape[0]
    out_ref[rows_at(at, size), :] = mine_ref[...]
    out_ref[rows_at(1 - at, size), :] = got_ref[...]


def pair_kernel(core_ref, own_ref, other_ref, after_ref, own_pair, other_pair):
    pair_up(own_pair, own_ref)
    pair_up(other_pair, other_ref)


def spread_kernel(core_ref, shares_ref, after_ref, out_ref, total, sems):
    share = shares_ref[0]
    for k in range(1, shares_ref.shape[0]):
        share += shares_ref[k]
    total[...] = share
    copies = [
        pltpu.make_async_copy(total, out_ref.at[k], sems.at[k]) for k in range(out_ref.shape[0])
    ]
    for copy in copies:
        copy.start()
    for copy in copies:
        copy.wait()


def multiply(x, y, emit):
    for a in range(PARTS):
        z = dot_split(both(x, span(a), EVERY), both(y, EVERY, slice(a * SUB, BLOCK)))
        for b in range(a, PARTS):
            emit(a, b, z[:, span(b - a)])


def root_kernel(
    core_ref, left_ref, left_got_ref, right_ref, right_got_ref, out_ref, root_ref,
    factor, m, n, z, y, t,
):
    core = core_ref[0]

    @pl.when(core == 0)
    def _():
        factor[:HALF, :] = left_ref[...]
        factor[HALF:, :] = left_got_ref[...]

    @pl.when(core == 1)
    def _():
        factor[:HALF, :] = right_got_ref[...]
        factor[HALF:, :] = right_ref[...]

    def blocks():
        for which in range(2):
            yield from load_half(factor, which * HALF, which)

    squares = jnp.zeros((SUB, SUB), F32)
    for a, b, x in blocks():
        squares += x * x * (1.0 if a == b else 2.0)
    scale = 1.0 / (jnp.sqrt(jnp.sum(squares)) + NORM_EPS)
    for a, b, x in blocks():
        put(m, a, b, x * scale)

    multiply(m, m, lambda a, b, p: put(n, a, b, p))

    def cube(a, b, p):
        mm, nn = block(m, a, b), block(n, a, b)
        put(z, a, b, (25.0 * mm - 10.0 * nn + p) * (1.0 / 16.0))
        put(y, a, b, (nn - 10.0 * mm) * (1.0 / 16.0))

    multiply(m, n, cube)
    multiply(z, y, lambda a, b, p: put(t, a, b, (25.0 / 16.0) * block(z, a, b) + p))

    multiply(t, t, lambda a, b, p: put(n, a, b, p))

    def cube_again(a, b, p):
        tt, nn = block(t, a, b), block(n, a, b)
        put(z, a, b, (25.0 * tt - 10.0 * nn + p) * (1.0 / 16.0))
        put(y, a, b, (15.0 * nn - 75.0 * tt - p) * (1.0 / 64.0))

    multiply(t, n, cube_again)

    def last(a, b, p):
        put(n, a, b, -0.3125 * block(t, a, b) - (125.0 / 256.0) * block(z, a, b) - 0.25 * p)

    multiply(z, y, last)

    def result(a, b, p):
        p = 1.25 * block(n, a, b) - (25.0 / 64.0) * block(m, a, b) - 0.25 * p
        out_ref[span(PLACE[(a, b)]), :] = p
        put(root_ref, a, b, p)

    multiply(m, n, result)


def early_kernel(core_ref, root_ref, own_ref, other_ref, out_ref):
    core = core_ref[0]

    def keep(rows, cols, x):
        high, low = split(x)
        out_ref[0, rows, cols] = high
        out_ref[1, rows, cols] = low

    @pl.when(core == 0)
    def _():
        for part in range(PARTS):
            for k, src in enumerate((own_ref, other_ref)):
                x = dot_split(both(root_ref, span(part), EVERY), both(src, EVERY, EVERY))
                keep(span(part), span(k, SIDE), x + LEVEL * get(src, span(part), EVERY))

    @pl.when(core == 1)
    def _():
        for part in range(PARTS):
            at = span(part)
            x = dot_split(both(other_ref, at, EVERY), both(root_ref, span(0, SIDE), span(1, SIDE)))
            x += dot_split(both(own_ref, at, EVERY), both(root_ref, span(1, SIDE), span(1, SIDE)))
            keep(at, span(0, SIDE), x + LEVEL * get(own_ref, at, EVERY))


LANES = 128


def late_kernel(core_ref, early_ref, got_ref, sq_ref, out_ref, left, right):
    core = core_ref[0]
    rows = BLOCK // out_ref.shape[0]
    lanes = SIDE // LANES
    count = SUB // rows

    def finish(product):
        total = jnp.zeros((4, LANES), F32)
        for part in range(PARTS):
            x = product(span(part)) + LEVEL * get(early_ref, span(part), span(0, SIDE))
            total += fold(x * x)
            for lane in range(lanes):
                out_ref[span(part, count), span(lane, rows), :] = x[:, span(lane, LANES)].reshape(
                    count, rows, LANES
                )
        stats = jnp.concatenate([sq_ref[...], total], 0)
        out_ref[:, lanes * rows :, :] = jnp.broadcast_to(
            stats[None], (out_ref.shape[0],) + stats.shape
        )

    @pl.when(core == 0)
    def _():
        for a in range(PARTS):
            for b in range(2):
                x = got_ref[span(PLACE[(min(a, b), max(a, b))]), :]
                high, low = split(x)
                right[0, span(a), span(b)] = high if a <= b else high.T
                right[1, span(a), span(b)] = low if a <= b else low.T
        finish(lambda at: dot_split(both(early_ref, at, EVERY), both(right, EVERY, EVERY)))

    @pl.when(core == 1)
    def _():
        for k, (a, b) in enumerate(ROOT_PAIRS):
            put(left, a, b, got_ref[span(k), :])
        finish(
            lambda at: dot_split(both(left, at, EVERY), both(early_ref, EVERY, span(0, SIDE)))
        )


STEP_TILES = 2


def base_kernel(flag_ref, coef_ref, m_ref, f_ref, n_ref, out_ref):
    for t in range(STEP_TILES):
        at = span(t, BLOCK)
        flag = flag_ref[pl.program_id(0) * STEP_TILES + t]
        prior = jnp.where(flag == 1, coef_ref[1] * f_ref[:, at], m_ref[:, at])
        out_ref[:, at] = (1.0 - DAMPING_COEFF) * prior + coef_ref[2] * n_ref[:, at]


def update_kernel(coef_ref, sums_ref, dir_ref, w_ref, b_ref, ow_out, om_out, ow, om, sems):
    gsq = jnp.sum(sums_ref[:4, :])
    dsq = jnp.sum(sums_ref[4:, :])
    pull = coef_ref[0] * (jnp.sqrt(gsq) / (jnp.sqrt(dsq) + NORM_EPS))
    rows = w_ref.shape[0]
    lanes = SIDE // LANES
    chunk = 2 * STEP_TILES
    copies = []
    for step in range(dir_ref.shape[0] // chunk):
        for k in range(step * chunk, (step + 1) * chunk):
            for lane in range(lanes):
                at = span(k * lanes + lane, LANES)
                moved = b_ref[:, at] - pull * dir_ref[k, span(lane, rows), :]
                om[:, at] = moved
                ow[:, at] = w_ref[:, at] + moved
        at = span(step, chunk * SIDE)
        pair = [
            pltpu.make_async_copy(ow.at[:, at], ow_out.at[:, at], sems.at[0, step]),
            pltpu.make_async_copy(om.at[:, at], om_out.at[:, at], sems.at[1, step]),
        ]
        for copy in pair:
            copy.start()
        copies += pair
    for copy in copies:
        copy.wait()


def stream(kernel, name, shape, ins, specs, outs):
    rows, cols = shape
    width = STEP_TILES * BLOCK
    wide = pl.BlockSpec((rows, width), lambda i: (0, i))
    cost = pl.CostEstimate(
        flops=4 * rows * cols, bytes_accessed=(len(ins) + outs) * 4 * rows * cols, transcendentals=0
    )
    return pl.pallas_call(
        kernel,
        grid=(cols // width,),
        out_shape=tuple(array(*shape) for _ in range(outs)),
        in_specs=specs + [wide] * (len(ins) - len(specs)),
        out_specs=(wide,) * outs,
        compiler_params=pltpu.CompilerParams(vmem_limit_bytes=16 << 20),
        cost_estimate=cost,
        name=name,
    )(*ins)


def ring_swapped(x, flips):
    cols = lax.axis_size("col")
    pairs = [
        (r * cols + c, (r ^ flips[c % 2]) * cols + c)
        for r in range(lax.axis_size("row"))
        for c in range(cols)
    ]
    return lax.ppermute(x, ("row", "col"), pairs)


def swapped(x, axis, flip):
    return lax.ppermute(x, axis, [(i, i ^ flip) for i in range(lax.axis_size(axis))])


def shards(gradient, weights, momentum, fresh_momentum, gaussian_noise, resample, step_index):
    rows, cols = gradient.shape
    col_pos = lax.axis_index("col")
    row_pos = lax.axis_index("row")
    core = (col_pos % 2).reshape(1).astype(jnp.int32)
    devices = lax.axis_size("col")
    chips = devices // 2
    by_core = [[c for c in range(devices) if c % 2 == k] for k in range(2)]

    phase = jnp.mod(step_index[0], CYCLE).astype(F32) / CYCLE
    rate = BASE_RATE * 0.5 * (1.0 + jnp.cos(jnp.pi * phase))
    coefs = jnp.stack([rate, jnp.sqrt(rate), jnp.sqrt(2.0 * DAMPING_COEFF * rate * HEAT_LEVEL)])
    flags = lax.dynamic_index_in_dim(resample, row_pos, 0, keepdims=False)
    pieces = gradient.reshape(rows, devices, SIDE).transpose(1, 0, 2)
    own = lax.all_to_all(pieces, "col", 0, 0).reshape(BLOCK, SIDE)
    other = swapped(own, "col", 1)
    pair = array(2, BLOCK, SIDE, dtype=BF16)
    pair_space = pltpu.VMEM((2, BLOCK, SIDE), BF16)
    (left,) = whole(own_kernel, "own", (array(HALF, SUB),), (core, own), [pair_space], products=0.16)
    left, grad_sq = whole(
        left_kernel,
        "left",
        (array(chips, HALF // chips, SUB), array(4, LANES)),
        (core, other, left),
        [pair_space, pltpu.VMEM((HALF, SUB), F32), pltpu.SemaphoreType.DMA((chips,))],
        products=0.16,
        far=(0,),
    )
    shares = lax.all_to_all(left, "col", 0, 0, axis_index_groups=by_core)

    ring = row_pos.reshape(1).astype(jnp.int32)
    two, one = array(2 * RUN, SUB), array(RUN, SUB)
    right, sent = whole(
        right_kernel,
        "right",
        (array(HALF, SUB), two),
        (core, ring, own, other, grad_sq),
        [pair_space, pair_space, pltpu.VMEM((2, SIDE, BLOCK), BF16)],
        products=0.3,
        scalars=2,
    )
    got = ring_swapped(sent, HALF_FLIPS)
    own_pair, other_pair = whole(
        pair_kernel, "pairs", (pair, pair), (core, own, other, sent[:8]), products=0.1
    )
    got, own_pair, other_pair = lax.optimization_barrier((got, own_pair, other_pair))
    kept, sent = whole(
        halve_kernel,
        "halve",
        (one, one),
        (core, ring, right, got),
        [pltpu.VMEM((2 * RUN, SUB), F32)],
        scalars=2,
    )
    mine = kept + ring_swapped(sent, QUARTER_FLIPS)
    (share,) = whole(
        spread_kernel,
        "spread",
        (array(*shares.shape),),
        (core, shares, kept[:8]),
        [pltpu.VMEM(shares.shape[1:], F32), pltpu.SemaphoreType.DMA((chips,))],
        far=(0,),
    )
    left = lax.all_to_all(share, "col", 0, 0, axis_index_groups=by_core).reshape(HALF, SUB)
    got = ring_swapped(mine, QUARTER_FLIPS)
    (right,) = whole(
        functools.partial(join_kernel, which=1), "join", (two,), (core, ring, mine, got), scalars=2
    )
    right, momentum, fresh_momentum, gaussian_noise = lax.optimization_barrier(
        (right, momentum, fresh_momentum, gaussian_noise)
    )
    (base,) = stream(
        base_kernel,
        "base",
        (rows, cols),
        (flags, coefs, momentum, fresh_momentum, gaussian_noise),
        [smem(), smem()],
        1,
    )
    got = ring_swapped(right, HALF_FLIPS)
    got, base = lax.optimization_barrier((got, base))
    (right,) = whole(
        functools.partial(join_kernel, which=0),
        "place",
        (array(HALF, SUB),),
        (core, ring, right, got),
        scalars=2,
    )
    right_got, left_got = swapped(right, "col", 1), swapped(left, "col", 1)
    packed, root = whole(
        root_kernel,
        "root",
        (array(PACKED, SUB), array(2, BLOCK, BLOCK, dtype=BF16)),
        (core, left, left_got, right, right_got),
        [pltpu.VMEM((2 * HALF, SUB), F32)] + [pltpu.VMEM((2, BLOCK, BLOCK), BF16)] * 5,
        limit=30,
        products=7 * 0.625,
    )
    other_root = swapped(packed, "col", 1)
    (early,) = whole(
        early_kernel,
        "early",
        (array(2, BLOCK, BLOCK, dtype=BF16),),
        (core, root, own_pair, other_pair),
        products=1.0,
    )
    (message,) = whole(
        late_kernel,
        "late",
        (array(devices, rows * SIDE // LANES + 8, LANES),),
        (core, early, other_root, grad_sq),
        [pltpu.VMEM((2, BLOCK, BLOCK), BF16), pltpu.VMEM((2, BLOCK, SIDE), BF16)],
        products=0.5,
    )
    message = lax.all_to_all(message, "col", 0, 0)
    sums = jnp.sum(message[:, -8:, :], axis=0)
    for flip in (1, 3):
        sums = sums + swapped(sums, "row", flip)
    chunks = cols // (STEP_TILES * BLOCK)
    return whole(
        update_kernel,
        "update",
        (array(rows, cols), array(rows, cols)),
        (coefs, sums, message, weights, base),
        [
            pltpu.VMEM((rows, cols), F32),
            pltpu.VMEM((rows, cols), F32),
            pltpu.SemaphoreType.DMA((2, chunks)),
        ],
        far=(0, 1),
    )


def solution(mesh):
    wide = P(("row", "col"), None)
    in_specs = (wide, wide, wide, wide, wide, P(), P())
    return jax.shard_map(
        shards, mesh=mesh, in_specs=in_specs, out_specs=(wide, wide), check_vma=False
    )
```

```python
import jax
import jax.numpy as jnp
from jax import lax
from jax.experimental import pallas as pl
from jax.experimental.pallas import tpu as pltpu
from jax.sharding import PartitionSpec as P

BLOCK = 1024
CYCLE = 1000
NORM_EPS = 1e-06
BASE_RATE = 0.5
DAMPING_COEFF = 0.1
HEAT_LEVEL = 1.0

SUB = 256
QUARTER = SUB // 2
PARTS = BLOCK // SUB
SIDE = BLOCK // 2
DIAGONAL = ((0, 1), (2, 3))
OTHERS = (((0, 1), (0, 2), (1, 2)), ((2, 3), (3, 0), (3, 1)))
HALF = 3 * QUARTER + 3 * SUB
ROOT_PAIRS = [(a, b) for b in range(PARTS) for a in range(b + 1)]
PLACE = {pair: k for k, pair in enumerate(ROOT_PAIRS)}
PACKED = len(ROOT_PAIRS) * SUB
LEVEL = 125.0 / 64.0
F32, BF16 = jnp.float32, jnp.bfloat16


def vmem():
    return pl.BlockSpec(memory_space=pltpu.VMEM)


def smem():
    return pl.BlockSpec(memory_space=pltpu.SMEM)


def array(*shape, dtype=F32):
    return jax.ShapeDtypeStruct(shape, dtype)


def whole(kernel, name, outs, ins, scratch=(), limit=16, products=0.0, scalars=1, far=()):
    cost = pl.CostEstimate(
        flops=int(products * 6 * BLOCK**3), bytes_accessed=8 << 20, transcendentals=0
    )
    return pl.pallas_call(
        kernel,
        out_shape=outs,
        in_specs=[smem()] * scalars + [vmem() for _ in ins[scalars:]],
        out_specs=tuple(
            pl.BlockSpec(memory_space=pltpu.HBM) if k in far else vmem() for k in range(len(outs))
        ),
        scratch_shapes=list(scratch),
        compiler_params=pltpu.CompilerParams(vmem_limit_bytes=limit << 20),
        cost_estimate=cost,
        name=name,
    )(*ins)


def span(k, size=SUB):
    return slice(k * size, (k + 1) * size)


def split(x):
    high = x.astype(BF16)
    return high, (x - high.astype(F32)).astype(BF16)


def dot(x, y, dims=((1,), (0,))):
    return lax.dot_general(x, y, (dims, ((), ())), preferred_element_type=F32)


def dot_split(x, y, dims=((1,), (0,))):
    x = jnp.concatenate([x[0], x[0], x[1]], dims[0][0])
    y = jnp.concatenate([y[0], y[1], y[0]], dims[1][0])
    return dot(x, y, dims)


def both(ref, *at):
    return [ref[(k,) + at] for k in range(2)]


def put(dst, a, b, x):
    high, low = split(x)
    dst[0, span(a), span(b)] = high
    dst[1, span(a), span(b)] = low
    if a != b:
        dst[0, span(b), span(a)] = high.T
        dst[1, span(b), span(a)] = low.T


def get(src, *at):
    return src[(0,) + at].astype(F32) + src[(1,) + at].astype(F32)


def block(src, a, b):
    return get(src, span(a), span(b))


def fold(x):
    total = jnp.sum(x.reshape(x.shape[0] // 8, 8, x.shape[1]), axis=0)
    total = sum(total[:, span(k, 128)] for k in range(x.shape[1] // 128))
    return total[:4] + total[4:]


EVERY = slice(None)


def store_diagonal(dst, k, x, part=None):
    pieces = (
        (span(k, QUARTER), EVERY, x[:QUARTER, :]),
        (span(2, QUARTER), span(k, QUARTER), x[QUARTER:, QUARTER:]),
    )
    for rows, cols, piece in pieces:
        dst[rows, cols] = piece if part is None else part[rows, cols] + piece


def store_other(dst, k, x, part=None):
    start = 3 * QUARTER + k * SUB
    rows = slice(start, start + x.shape[0])
    dst[rows, :] = x if part is None else part[rows, :] + x


def load_half(src, at, which):
    for k, a in enumerate(DIAGONAL[which]):
        top = src[at + k * QUARTER : at + (k + 1) * QUARTER, :]
        corner = src[at + 2 * QUARTER : at + 3 * QUARTER, span(k, QUARTER)]
        bottom = jnp.concatenate([top[:, QUARTER:].T, corner], 1)
        yield a, a, jnp.concatenate([top, bottom], 0)
    for k, (a, b) in enumerate(OTHERS[which]):
        start = at + 3 * QUARTER + k * SUB
        yield a, b, src[start : start + SUB, :]


def left_blocks(core, src, dst, part=None):
    def rows(first, end, other_first, other_end):
        return dot_split(
            both(src, slice(first * SUB, end * SUB), EVERY),
            both(src, slice(other_first * SUB, other_end * SUB), EVERY),
            ((1,), (1,)),
        )

    @pl.when(core == 0)
    def _():
        store_diagonal(dst, 0, rows(0, 1, 0, 1), part)
        z = rows(0, 2, 1, 2)
        store_other(dst, 0, z[:SUB], part)
        store_diagonal(dst, 1, z[SUB:], part)
        store_other(dst, 1, rows(0, 2, 2, 3), part)

    @pl.when(core == 1)
    def _():
        store_diagonal(dst, 0, rows(2, 3, 2, 3), part)
        z = rows(2, 4, 3, 4)
        store_other(dst, 0, z[:SUB], part)
        store_diagonal(dst, 1, z[SUB:], part)
        z = rows(3, 4, 0, 2)
        store_other(dst, 1, z[:, span(0)], part)
        store_other(dst, 2, z[:, span(1)], part)


def pair_up(dst, src):
    for part in range(PARTS):
        high, low = split(src[span(part), :])
        dst[0, span(part), :] = high
        dst[1, span(part), :] = low


def turn(dst, src):
    for part in range(PARTS):
        for k in range(2):
            dst[k, :, span(part)] = src[k, span(part), :].T


def own_kernel(core_ref, own_ref, left_ref, pair):
    pair_up(pair, own_ref)
    left_blocks(core_ref[0], pair, left_ref)


def left_kernel(core_ref, other_ref, part_ref, left_ref, mark_ref, pair):
    pair_up(pair, other_ref)
    left_blocks(core_ref[0], pair, left_ref, part_ref)
    mark_ref[...] = part_ref[:8, :]


RUN = HALF // 4
HALF_FLIPS, QUARTER_FLIPS = (1, 3), (3, 1)


def ring_place(core, pos):
    near, far = pos % 2, pos // 2
    return jnp.where(core == 0, near ^ far, far), jnp.where(core == 0, far, near)


def rows_at(k, size):
    return pl.ds(pl.multiple_of(k * size, size), size)


def right_kernel(
    core_ref, ring_ref, own_ref, other_ref, after_ref, right_ref, sent_ref, own_pair, other_pair, turned
):
    core = core_ref[0]
    pair_up(own_pair, own_ref)
    pair_up(other_pair, other_ref)
    turn(turned, own_pair)
    head = slice(0, SUB)
    store_diagonal(
        right_ref, 0, dot_split(both(turned, head, EVERY), both(own_pair, EVERY, head))
    )
    z = dot_split(both(turned, EVERY, EVERY), both(own_pair, EVERY, span(1)))
    store_other(right_ref, 0, z[:SUB])
    store_diagonal(right_ref, 1, z[SUB:])

    @pl.when(core == 0)
    def _():
        z = dot_split(both(turned, EVERY, EVERY), both(other_pair, EVERY, span(0)))
        store_other(right_ref, 1, z)

    @pl.when(core == 1)
    def _():
        z = dot_split(both(turned, span(1), EVERY), both(other_pair, EVERY, EVERY))
        store_other(right_ref, 1, z[:, span(0)])
        store_other(right_ref, 2, z[:, span(1)])

    half, _ = ring_place(core, ring_ref[0])
    sent_ref[...] = right_ref[rows_at(1 - half, 2 * RUN), :]


def halve_kernel(core_ref, ring_ref, right_ref, got_ref, kept_ref, sent_ref, total):
    half, quarter = ring_place(core_ref[0], ring_ref[0])
    total[...] = right_ref[rows_at(half, 2 * RUN), :] + got_ref[...]
    kept_ref[...] = total[rows_at(quarter, RUN), :]
    sent_ref[...] = total[rows_at(1 - quarter, RUN), :]


def join_kernel(core_ref, ring_ref, mine_ref, got_ref, out_ref):
    _, quarter = ring_place(core_ref[0], ring_ref[0])
    out_ref[rows_at(quarter, RUN), :] = mine_ref[...]
    out_ref[rows_at(1 - quarter, RUN), :] = got_ref[...]


def pair_kernel(core_ref, own_ref, other_ref, after_ref, own_pair, other_pair, sq_ref):
    pair_up(own_pair, own_ref)
    pair_up(other_pair, other_ref)
    sq_ref[...] = fold(own_ref[...] * own_ref[...])


def spread_kernel(core_ref, shares_ref, after_ref, out_ref, total, sems):
    share = shares_ref[0]
    for k in range(1, shares_ref.shape[0]):
        share += shares_ref[k]
    total[...] = share
    copies = [
        pltpu.make_async_copy(total, out_ref.at[k], sems.at[k]) for k in range(out_ref.shape[0])
    ]
    for copy in copies:
        copy.start()
    for copy in copies:
        copy.wait()


def multiply(x, y, emit):
    for a in range(PARTS):
        z = dot_split(both(x, span(a), EVERY), both(y, EVERY, slice(a * SUB, BLOCK)))
        for b in range(a, PARTS):
            emit(a, b, z[:, span(b - a)])


def root_kernel(
    core_ref, ring_ref, left_ref, left_got_ref, half_ref, rest_ref, half_got_ref, rest_got_ref,
    out_ref, root_ref, factor, m, n, z, y, t,
):
    core = core_ref[0]

    @pl.when(core == 0)
    def _():
        factor[:HALF, :] = left_ref[...]
        factor[HALF:, :] = left_got_ref[...]

    @pl.when(core == 1)
    def _():
        for which, mine, rest in ((0, half_got_ref, rest_got_ref), (1, half_ref, rest_ref)):
            half, _ = ring_place(which, ring_ref[0])
            factor[rows_at(2 * which + half, 2 * RUN), :] = mine[...]
            factor[rows_at(2 * which + 1 - half, 2 * RUN), :] = rest[...]

    def blocks():
        for which in range(2):
            yield from load_half(factor, which * HALF, which)

    squares = jnp.zeros((SUB, SUB), F32)
    for a, b, x in blocks():
        squares += x * x * (1.0 if a == b else 2.0)
    scale = 1.0 / (jnp.sqrt(jnp.sum(squares)) + NORM_EPS)
    for a, b, x in blocks():
        put(m, a, b, x * scale)

    multiply(m, m, lambda a, b, p: put(n, a, b, p))

    def cube(a, b, p):
        mm, nn = block(m, a, b), block(n, a, b)
        put(z, a, b, (25.0 * mm - 10.0 * nn + p) * (1.0 / 16.0))
        put(y, a, b, (nn - 10.0 * mm) * (1.0 / 16.0))

    multiply(m, n, cube)
    multiply(z, y, lambda a, b, p: put(t, a, b, (25.0 / 16.0) * block(z, a, b) + p))

    multiply(t, t, lambda a, b, p: put(n, a, b, p))

    def cube_again(a, b, p):
        tt, nn = block(t, a, b), block(n, a, b)
        put(z, a, b, (25.0 * tt - 10.0 * nn + p) * (1.0 / 16.0))
        put(y, a, b, (15.0 * nn - 75.0 * tt - p) * (1.0 / 64.0))

    multiply(t, n, cube_again)

    def last(a, b, p):
        put(n, a, b, -0.3125 * block(t, a, b) - (125.0 / 256.0) * block(z, a, b) - 0.25 * p)

    multiply(z, y, last)

    def result(a, b, p):
        p = 1.25 * block(n, a, b) - (25.0 / 64.0) * block(m, a, b) - 0.25 * p
        out_ref[span(PLACE[(a, b)]), :] = p
        put(root_ref, a, b, p)

    multiply(m, n, result)


def early_kernel(core_ref, root_ref, own_ref, other_ref, out_ref):
    core = core_ref[0]

    def keep(rows, cols, x):
        high, low = split(x)
        out_ref[0, rows, cols] = high
        out_ref[1, rows, cols] = low

    @pl.when(core == 0)
    def _():
        for part in range(PARTS):
            for k, src in enumerate((own_ref, other_ref)):
                x = dot_split(both(root_ref, span(part), EVERY), both(src, EVERY, EVERY))
                keep(span(part), span(k, SIDE), x + LEVEL * get(src, span(part), EVERY))

    @pl.when(core == 1)
    def _():
        for part in range(PARTS):
            at = span(part)
            x = dot_split(both(other_ref, at, EVERY), both(root_ref, span(0, SIDE), span(1, SIDE)))
            x += dot_split(both(own_ref, at, EVERY), both(root_ref, span(1, SIDE), span(1, SIDE)))
            keep(at, span(0, SIDE), x + LEVEL * get(own_ref, at, EVERY))


LANES = 128


def late_kernel(core_ref, early_ref, got_ref, sq_ref, out_ref, left, right):
    core = core_ref[0]
    rows = BLOCK // out_ref.shape[0]
    lanes = SIDE // LANES
    count = SUB // rows

    def finish(product):
        total = jnp.zeros((4, LANES), F32)
        for part in range(PARTS):
            x = product(span(part)) + LEVEL * get(early_ref, span(part), span(0, SIDE))
            total += fold(x * x)
            for lane in range(lanes):
                out_ref[span(part, count), span(lane, rows), :] = x[:, span(lane, LANES)].reshape(
                    count, rows, LANES
                )
        stats = jnp.concatenate([sq_ref[...], total], 0)
        out_ref[:, lanes * rows :, :] = jnp.broadcast_to(
            stats[None], (out_ref.shape[0],) + stats.shape
        )

    @pl.when(core == 0)
    def _():
        for a in range(PARTS):
            for b in range(2):
                x = got_ref[span(PLACE[(min(a, b), max(a, b))]), :]
                high, low = split(x)
                right[0, span(a), span(b)] = high if a <= b else high.T
                right[1, span(a), span(b)] = low if a <= b else low.T
        finish(lambda at: dot_split(both(early_ref, at, EVERY), both(right, EVERY, EVERY)))

    @pl.when(core == 1)
    def _():
        for k, (a, b) in enumerate(ROOT_PAIRS):
            put(left, a, b, got_ref[span(k), :])
        finish(
            lambda at: dot_split(both(left, at, EVERY), both(early_ref, EVERY, span(0, SIDE)))
        )


STEP_TILES = 2


def base_kernel(flag_ref, coef_ref, m_ref, f_ref, n_ref, out_ref):
    for t in range(STEP_TILES):
        at = span(t, BLOCK)
        flag = flag_ref[pl.program_id(0) * STEP_TILES + t]
        prior = jnp.where(flag == 1, coef_ref[1] * f_ref[:, at], m_ref[:, at])
        out_ref[:, at] = (1.0 - DAMPING_COEFF) * prior + coef_ref[2] * n_ref[:, at]


def update_kernel(coef_ref, sums_ref, dir_ref, w_ref, b_ref, ow_out, om_out, ow, om, sems):
    gsq = jnp.sum(sums_ref[:4, :])
    dsq = jnp.sum(sums_ref[4:, :])
    pull = coef_ref[0] * (jnp.sqrt(gsq) / (jnp.sqrt(dsq) + NORM_EPS))
    rows = w_ref.shape[0]
    lanes = SIDE // LANES
    chunk = 2 * STEP_TILES
    copies = []
    for step in range(dir_ref.shape[0] // chunk):
        for k in range(step * chunk, (step + 1) * chunk):
            for lane in range(lanes):
                at = span(k * lanes + lane, LANES)
                moved = b_ref[:, at] - pull * dir_ref[k, span(lane, rows), :]
                om[:, at] = moved
                ow[:, at] = w_ref[:, at] + moved
        at = span(step, chunk * SIDE)
        pair = [
            pltpu.make_async_copy(ow.at[:, at], ow_out.at[:, at], sems.at[0, step]),
            pltpu.make_async_copy(om.at[:, at], om_out.at[:, at], sems.at[1, step]),
        ]
        for copy in pair:
            copy.start()
        copies += pair
    for copy in copies:
        copy.wait()


def stream(kernel, name, shape, ins, specs, outs):
    rows, cols = shape
    width = STEP_TILES * BLOCK
    wide = pl.BlockSpec((rows, width), lambda i: (0, i))
    cost = pl.CostEstimate(
        flops=4 * rows * cols, bytes_accessed=(len(ins) + outs) * 4 * rows * cols, transcendentals=0
    )
    return pl.pallas_call(
        kernel,
        grid=(cols // width,),
        out_shape=tuple(array(*shape) for _ in range(outs)),
        in_specs=specs + [wide] * (len(ins) - len(specs)),
        out_specs=(wide,) * outs,
        compiler_params=pltpu.CompilerParams(vmem_limit_bytes=16 << 20),
        cost_estimate=cost,
        name=name,
    )(*ins)


def ring_swapped(x, flips):
    cols = lax.axis_size("col")
    pairs = [
        (r * cols + c, (r ^ flips[c % 2]) * cols + c)
        for r in range(lax.axis_size("row"))
        for c in range(cols)
    ]
    return lax.ppermute(x, ("row", "col"), pairs)


def swapped(x, axis, flip):
    return lax.ppermute(x, axis, [(i, i ^ flip) for i in range(lax.axis_size(axis))])


def shards(gradient, weights, momentum, fresh_momentum, gaussian_noise, resample, step_index):
    rows, cols = gradient.shape
    col_pos = lax.axis_index("col")
    row_pos = lax.axis_index("row")
    core = (col_pos % 2).reshape(1).astype(jnp.int32)
    devices = lax.axis_size("col")
    chips = devices // 2
    by_core = [[c for c in range(devices) if c % 2 == k] for k in range(2)]

    phase = jnp.mod(step_index[0], CYCLE).astype(F32) / CYCLE
    rate = BASE_RATE * 0.5 * (1.0 + jnp.cos(jnp.pi * phase))
    coefs = jnp.stack([rate, jnp.sqrt(rate), jnp.sqrt(2.0 * DAMPING_COEFF * rate * HEAT_LEVEL)])
    flags = lax.dynamic_index_in_dim(resample, row_pos, 0, keepdims=False)
    pieces = gradient.reshape(rows, devices, SIDE).transpose(1, 0, 2)
    own = lax.all_to_all(pieces, "col", 0, 0).reshape(BLOCK, SIDE)
    other = swapped(own, "col", 1)
    pair = array(2, BLOCK, SIDE, dtype=BF16)
    pair_space = pltpu.VMEM((2, BLOCK, SIDE), BF16)
    (left,) = whole(own_kernel, "own", (array(HALF, SUB),), (core, own), [pair_space], products=0.16)
    left, mark = whole(
        left_kernel,
        "left",
        (array(HALF, SUB), array(8, SUB)),
        (core, other, left),
        [pair_space],
        products=0.16,
    )
    left = left.reshape(chips, HALF // chips, SUB)
    shares = lax.all_to_all(left, "col", 0, 0, axis_index_groups=by_core)

    ring = row_pos.reshape(1).astype(jnp.int32)
    two, one = array(2 * RUN, SUB), array(RUN, SUB)
    right, sent = whole(
        right_kernel,
        "right",
        (array(HALF, SUB), two),
        (core, ring, own, other, mark),
        [pair_space, pair_space, pltpu.VMEM((2, SIDE, BLOCK), BF16)],
        products=0.3,
        scalars=2,
    )
    got = ring_swapped(sent, HALF_FLIPS)
    own_pair, other_pair, grad_sq = whole(
        pair_kernel,
        "pairs",
        (pair, pair, array(4, LANES)),
        (core, own, other, sent[:8]),
        products=0.1,
    )
    got, own_pair, other_pair = lax.optimization_barrier((got, own_pair, other_pair))
    kept, sent = whole(
        halve_kernel,
        "halve",
        (one, one),
        (core, ring, right, got),
        [pltpu.VMEM((2 * RUN, SUB), F32)],
        scalars=2,
    )
    mine = kept + ring_swapped(sent, QUARTER_FLIPS)
    (share,) = whole(
        spread_kernel,
        "spread",
        (array(*shares.shape),),
        (core, shares, kept[:8]),
        [pltpu.VMEM(shares.shape[1:], F32), pltpu.SemaphoreType.DMA((chips,))],
        far=(0,),
    )
    left = lax.all_to_all(share, "col", 0, 0, axis_index_groups=by_core).reshape(HALF, SUB)
    got = ring_swapped(mine, QUARTER_FLIPS)
    (right,) = whole(join_kernel, "join", (two,), (core, ring, mine, got), scalars=2)
    right, momentum, fresh_momentum, gaussian_noise = lax.optimization_barrier(
        (right, momentum, fresh_momentum, gaussian_noise)
    )
    (base,) = stream(
        base_kernel,
        "base",
        (rows, cols),
        (flags, coefs, momentum, fresh_momentum, gaussian_noise),
        [smem(), smem()],
        1,
    )
    got = ring_swapped(right, HALF_FLIPS)
    got, base = lax.optimization_barrier((got, base))
    rights = (right, got, swapped(right, "col", 1), swapped(got, "col", 1))
    left_got = swapped(left, "col", 1)
    packed, root = whole(
        root_kernel,
        "root",
        (array(PACKED, SUB), array(2, BLOCK, BLOCK, dtype=BF16)),
        (core, ring, left, left_got) + rights,
        [pltpu.VMEM((2 * HALF, SUB), F32)] + [pltpu.VMEM((2, BLOCK, BLOCK), BF16)] * 5,
        scalars=2,
        limit=30,
        products=7 * 0.625,
    )
    other_root = swapped(packed, "col", 1)
    (early,) = whole(
        early_kernel,
        "early",
        (array(2, BLOCK, BLOCK, dtype=BF16),),
        (core, root, own_pair, other_pair),
        products=1.0,
    )
    (message,) = whole(
        late_kernel,
        "late",
        (array(devices, rows * SIDE // LANES + 8, LANES),),
        (core, early, other_root, grad_sq),
        [pltpu.VMEM((2, BLOCK, BLOCK), BF16), pltpu.VMEM((2, BLOCK, SIDE), BF16)],
        products=0.5,
    )
    message = lax.all_to_all(message, "col", 0, 0)
    sums = jnp.sum(message[:, -8:, :], axis=0)
    sums = sums + sum([swapped(sums, "row", flip) for flip in (1, 3, 2)])
    chunks = cols // (STEP_TILES * BLOCK)
    return whole(
        update_kernel,
        "update",
        (array(rows, cols), array(rows, cols)),
        (coefs, sums, message, weights, base),
        [
            pltpu.VMEM((rows, cols), F32),
            pltpu.VMEM((rows, cols), F32),
            pltpu.SemaphoreType.DMA((2, chunks)),
        ],
        far=(0, 1),
    )


def solution(mesh):
    wide = P(("row", "col"), None)
    in_specs = (wide, wide, wide, wide, wide, P(), P())
    return jax.shard_map(
        shards, mesh=mesh, in_specs=in_specs, out_specs=(wide, wide), check_vma=False
    )
```
